32 devices in a mesh: seq: 8 (over z, y), head: 4 (over x, core).
Axes of the slice: x: 2, y: 2, z: 4, core: 2. Of those that a mesh axis runs over, the one named last changes fastest.
Arguments:
- query_vectors: bfloat16 [16384, 1024], P('seq', 'head'), may hold values from -6 to 6
- key_vectors: bfloat16 [16384, 128], P('seq'), may hold values from -6 to 6
- value_vectors: bfloat16 [16384, 128], P('seq'), may hold values from -6 to 6
- output_grad: bfloat16 [16384, 1024], P('seq', 'head'), may hold values from -48 to 48
- random_blocks: int32 [128, 3], P('seq'), may hold values from 0 to 127, as said below
- global_blocks: int32 [2], replicated, may hold values from 0 to 127
Outputs:
- query_grad: bfloat16 [16384, 1024], P('seq', 'head')
- key_grad: bfloat16 [16384, 128], P('seq')
- value_grad: bfloat16 [16384, 128], P('seq')
The draws below stay inside these ranges and needn't reach their ends.
Inputs may be any that keep to these rules, and one draw needn't show every extreme that they name: `random_blocks`: take the query blocks in aligned runs of 16 and the key blocks in aligned runs of 16: all entries of one run of query blocks that fall into one run of key blocks name the same key block.
All inputs are finite; a program needn't handle non-finite values.
Results may differ from the reference program's by a relative error of at most 0.012.
Values may be sent and summed in bfloat16 or wider, within the bound.
No kernel may reach another device: no remote copies, remote signals or barrier semaphores. Data moves between devices by JAX's collectives and lax.ppermute only.
A program may use at most 128 MiB of HBM per device.

```python
import jax
import jax.numpy as jnp
from jax import lax

DH = 128
HEADS = 8
BLOCK = 128
R = 3
G = 2
BPD = 16
NBLK = 128
TOKENS = 16384


def draw_query_vectors(key, part):
    result = jnp.clip(jax.random.normal(jax.random.fold_in(key, 1), (TOKENS, HEADS * DH), jnp.float32), -4.0, 4.0)
    return result.astype(jnp.bfloat16)


def draw_key_vectors(key, part):
    result = jnp.clip(jax.random.normal(jax.random.fold_in(key, 2), (TOKENS, DH), jnp.float32), -4.0, 4.0)
    return result.astype(jnp.bfloat16)


def draw_random_blocks(key, part):
    device_count = NBLK // BPD
    owner_block = jax.random.randint(jax.random.fold_in(key, 3), (device_count, device_count), 0, BPD)
    owner_ids = jax.random.randint(jax.random.fold_in(key, 4), (NBLK, R), 0, device_count)
    requester = jnp.arange(NBLK, dtype=jnp.int32) // BPD
    picked = owner_block[requester[:, None], owner_ids]
    return (owner_ids * BPD + picked).astype(jnp.int32)


def steps_of(rng, extent, cuts, least, high):
    factor_of = 1.0
    for dim, blocks in cuts:
        heights = jax.random.uniform(jax.random.fold_in(jax.random.fold_in(rng, 6), dim), (blocks,), jnp.float32, least / len(cuts), high / len(cuts))
        factor_of = factor_of * jnp.repeat(jnp.exp(heights), extent[dim] // blocks).reshape((-1,) + (1,) * (len(extent) - 1 - dim))
    return factor_of


def centred(rng, dims, scale, bound, split=(), kind=jnp.bfloat16):
    factor_of = steps_of(rng, dims, split, -0.22, 0.18) if split else 1.0
    drawn = jax.random.normal(rng, dims, jnp.float32) * scale * factor_of
    return jnp.minimum(jnp.maximum(drawn, -bound), bound).astype(kind)


def setup_inputs(seed: int = 0) -> dict:
    streams_of = jax.random.split(jax.random.key(seed), 7)
    return {
        "query_vectors": draw_query_vectors(jax.random.fold_in(streams_of[6], 71), 0),
        "key_vectors": draw_key_vectors(jax.random.fold_in(streams_of[6], 71), 0),
        "value_vectors": centred(streams_of[2], (TOKENS, DH), 1.0, 6.0, ((0, 8),)),
        "output_grad": centred(streams_of[3], (TOKENS, HEADS * DH), 8.0, 48.0, ((0, 8), (1, 4))),
        "random_blocks": draw_random_blocks(jax.random.fold_in(streams_of[6], 71), 0),
        "global_blocks": jax.random.randint(streams_of[5], (G,), 0, NBLK).astype(jnp.int32),
    }


def softmax_rows(scores):
    largest = jnp.max(scores, axis=-1, keepdims=True)
    powers = jnp.exp(scores - largest)
    return powers / jnp.sum(powers, axis=-1, keepdims=True)


def reference(query_vectors, key_vectors, value_vectors, output_grad, random_blocks, global_blocks):
    block_count = query_vectors.shape[0] // BLOCK
    factor = float(DH) ** -0.5
    listed = 3 + R + G
    query_blocks = query_vectors.reshape(block_count, BLOCK, HEADS, DH)
    grad_blocks = output_grad.reshape(block_count, BLOCK, HEADS, DH)
    key_blocks = key_vectors.reshape(block_count, BLOCK, DH)
    value_blocks = value_vectors.reshape(block_count, BLOCK, DH)
    order_ids = jnp.arange(block_count, dtype=jnp.int32)
    window = order_ids[:, None] + jnp.array([-1, 0, 1], dtype=jnp.int32)[None, :]
    inside = (window >= 0) & (window < block_count)
    window = jnp.clip(window, 0, block_count - 1).astype(jnp.int32)
    global_rows = jnp.broadcast_to(global_blocks.astype(jnp.int32)[None, :], (block_count, G))
    key_lists = jnp.concatenate([window, random_blocks.astype(jnp.int32), global_rows], axis=1)
    allowed = jnp.concatenate([inside, jnp.ones((block_count, R + G), dtype=jnp.bool_)], axis=1)

    def advance(totals, position):
        key_acc, value_acc = totals
        chosen = key_lists[position]
        key_row_matrix = key_blocks[chosen].reshape(listed * BLOCK, DH).astype(jnp.float32)
        value_row_matrix = value_blocks[chosen].reshape(listed * BLOCK, DH).astype(jnp.float32)
        query_row_matrix = query_blocks[position].astype(jnp.float32)
        gradient_rows = grad_blocks[position].astype(jnp.float32)
        visible = jnp.repeat(allowed[position], BLOCK)
        scores = jnp.einsum("qhd,kd->hqk", query_row_matrix, key_row_matrix) * factor
        scores = jnp.where(visible[None, None, :], scores, -jnp.inf)
        attention = softmax_rows(scores)
        attention_reduced = attention.astype(jnp.bfloat16)
        outputs = jnp.einsum("hqk,kd->qhd", attention_reduced.astype(jnp.float32), value_row_matrix)
        row_delta = jnp.sum(gradient_rows * outputs, axis=-1)
        prob_grad = jnp.einsum("qhd,kd->hqk", gradient_rows, value_row_matrix)
        score_gradient = (attention * (prob_grad - jnp.transpose(row_delta)[:, :, None])).astype(jnp.bfloat16)
        query_part = (jnp.einsum("hqk,kd->qhd", score_gradient.astype(jnp.float32), key_row_matrix) * factor).astype(jnp.bfloat16)
        key_part = jnp.einsum("hqk,qhd->kd", score_gradient.astype(jnp.float32), query_row_matrix) * factor
        value_part = jnp.einsum("hqk,qhd->kd", attention_reduced.astype(jnp.float32), gradient_rows)
        key_acc = key_acc.at[chosen].add(key_part.reshape(listed, BLOCK, DH))
        value_acc = value_acc.at[chosen].add(value_part.reshape(listed, BLOCK, DH))
        return (key_acc, value_acc), query_part

    zeros_acc = jnp.zeros((block_count, BLOCK, DH), dtype=jnp.float32)
    (key_acc, value_acc), query_parts = lax.scan(advance, (zeros_acc, zeros_acc), order_ids)
    query_grad = query_parts.reshape(block_count * BLOCK, HEADS * DH)
    key_grad = key_acc.reshape(block_count * BLOCK, DH).astype(jnp.bfloat16)
    value_grad = value_acc.reshape(block_count * BLOCK, DH).astype(jnp.bfloat16)
    return (query_grad, key_grad, value_grad)
```

```python
import functools
import math

import jax
import jax.numpy as jnp
from jax import lax
from jax.experimental import pallas as pl
from jax.experimental.pallas import tpu as pltpu
from jax.sharding import PartitionSpec as P

DH = 128
BLOCK = 128
R = 3
G = 2
WINDOW = 3
LISTED = WINDOW + R + G
PER_STEP = 2
VMEM_LIMIT = 56 * 1024 * 1024
MASKED = -1e30
FACTOR = float(DH) ** -0.5
LOG2E = math.log2(math.e)

NT = (((1,), (1,)), ((), ()))
NN = (((1,), (0,)), ((), ()))


def mm(a, b, dims):
    return lax.dot_general(a, b, dims, preferred_element_type=jnp.float32)


def stack_heads(rows):
    heads = rows.shape[1] // DH
    return jnp.concatenate([rows[:, h * DH : (h + 1) * DH] for h in range(heads)], axis=0)


def serve_kernel(requested, k_ref, v_ref, out_ref):
    half = BLOCK // 2
    core = lax.rem(lax.axis_index("head"), 2)
    last = k_ref.shape[0] // BLOCK - 1

    def one(j, carry):
        start = pl.multiple_of(jnp.clip(requested[j], 0, last) * BLOCK + core * half, half)
        out_ref[j, 0] = k_ref[pl.ds(start, half), :]
        out_ref[j, 1] = v_ref[pl.ds(start, half), :]
        return carry

    lax.fori_loop(0, out_ref.shape[0], one, 0)


def attend_kernel(
    owners,
    q_ref,
    g_ref,
    k_ref,
    v_ref,
    before_ref,
    after_ref,
    mine_ref,
    other_ref,
    glob_mine_ref,
    glob_other_ref,
    ds_ref,
    pw_ref,
    keep_ref,
    send_ref,
    k_all,
    v_all,
    acc,
):
    blocks = k_ref.shape[0] // BLOCK
    peers = mine_ref.shape[0]
    half = BLOCK // 2
    core = lax.rem(lax.axis_index("head"), 2)
    seq_index = lax.axis_index("seq")
    step = pl.program_id(0)
    first_random = blocks + 2
    first_global = first_random + peers
    halo_slot = peers + G

    @pl.when(step == 0)
    def _():
        for all_ref, own_ref, which in ((k_all, k_ref, 0), (v_all, v_ref, 1)):
            all_ref[0] = before_ref[which]
            all_ref[blocks + 1] = after_ref[which]
            all_ref[1 : blocks + 1] = own_ref[...].reshape(blocks, BLOCK, DH)
            for j in range(peers):
                all_ref[first_random + j, pl.ds(core * half, half), :] = mine_ref[j, which]
                all_ref[first_random + j, pl.ds((1 - core) * half, half), :] = other_ref[j, which]
            for j in range(G):
                all_ref[first_global + j, pl.ds(core * half, half), :] = glob_mine_ref[j, which]
                all_ref[first_global + j, pl.ds((1 - core) * half, half), :] = glob_other_ref[j, which]
        acc[...] = jnp.zeros_like(acc)

    for u in range(PER_STEP):
        b = step * PER_STEP + u
        q = stack_heads(q_ref[u * BLOCK : (u + 1) * BLOCK, :])
        g = stack_heads(g_ref[u * BLOCK : (u + 1) * BLOCK, :])
        places = [owners[b * R + r] for r in range(R)]

        def listed(all_ref):
            parts = [all_ref[pl.ds(b, WINDOW)].reshape(WINDOW * BLOCK, DH)]
            parts += [all_ref[first_random + o] for o in places]
            parts += [all_ref[first_global + j] for j in range(G)]
            return jnp.concatenate(parts, axis=0)

        s = mm(listed(k_all), q, NT)
        dp = mm(listed(v_all), g, NT)
        no_left = jnp.logical_and(seq_index == 0, b == 0)
        no_right = jnp.logical_and(seq_index == lax.axis_size("seq") - 1, b == blocks - 1)
        left = jnp.where(no_left, MASKED, 0.0)
        right = jnp.where(no_right, MASKED, 0.0)
        spans = [(0, 1, left), (1, 2, None), (2, 3, right), (3, LISTED, None)]
        m = None
        for lo, hi, bias in spans:
            t = jnp.max(s[lo * BLOCK : hi * BLOCK], axis=0, keepdims=True)
            if bias is not None:
                t = t + bias
            m = t if m is None else jnp.maximum(m, t)
        scale = FACTOR * LOG2E
        mc = m * scale
        parts = []
        for lo, hi, bias in spans:
            off = mc if bias is None else mc - bias
            parts.append(jnp.exp2(s[lo * BLOCK : hi * BLOCK] * scale - off))
        e = jnp.concatenate(parts, axis=0)
        l = jnp.sum(e, axis=0, keepdims=True)
        d = jnp.sum(e * dp, axis=0, keepdims=True)
        inv = 1.0 / l
        delta = d * inv
        p = e * inv
        pb = p.astype(jnp.bfloat16)
        ds = (p * (dp - delta)).astype(jnp.bfloat16)
        ds_ref[u] = ds
        pw_ref[u] = pb[: WINDOW * BLOCK]
        tail = WINDOW * BLOCK
        dk = mm(ds[tail:], q, NN)
        dv = mm(pb[tail:], g, NN)
        for i in range(R + G):
            slot = places[i] if i < R else peers + i - R
            acc[slot, 0] += dk[i * BLOCK : (i + 1) * BLOCK]
            acc[slot, 1] += dv[i * BLOCK : (i + 1) * BLOCK]

        if u == 0:

            @pl.when(b == 0)
            def _():
                acc[halo_slot, 0] = mm(ds[:BLOCK], q, NN)
                acc[halo_slot, 1] = mm(pb[:BLOCK], g, NN)

        if u == PER_STEP - 1:

            @pl.when(b == blocks - 1)
            def _():
                acc[halo_slot + 1, 0] = mm(ds[2 * BLOCK : 3 * BLOCK], q, NN)
                acc[halo_slot + 1, 1] = mm(pb[2 * BLOCK : 3 * BLOCK], g, NN)

    @pl.when(step == pl.num_programs(0) - 1)
    def _():
        for which, f in ((0, FACTOR), (1, 1.0)):
            keep_ref[:, which] = acc[:, which, pl.ds(core * half, half), :] * f
            send_ref[:, which] = (acc[:, which, pl.ds((1 - core) * half, half), :] * f).astype(jnp.bfloat16)


def window_kernel(
    owners,
    q_ref,
    g_ref,
    k_ref,
    before_ref,
    after_ref,
    mine_ref,
    other_ref,
    glob_mine_ref,
    glob_other_ref,
    ds_ref,
    pw_ref,
    dq_ref,
    keep_ref,
    send_ref,
    kt_all,
    acc,
):
    blocks = k_ref.shape[0] // BLOCK
    peers = mine_ref.shape[0]
    half = BLOCK // 2
    core = lax.rem(lax.axis_index("head"), 2)
    step = pl.program_id(0)
    first_random = blocks + 2
    first_global = first_random + peers

    @pl.when(step == 0)
    def _():
        kt_all[0] = before_ref[0].T
        kt_all[blocks + 1] = after_ref[0].T

        def own(j, carry):
            kt_all[j + 1] = k_ref[pl.ds(pl.multiple_of(j * BLOCK, BLOCK), BLOCK), :].T
            return carry

        lax.fori_loop(0, blocks, own, 0)

        def joined(a, b):
            low = jnp.where(core == 0, a, b)
            high = jnp.where(core == 0, b, a)
            return jnp.concatenate([low, high], axis=0).T

        def fetched(j, carry):
            kt_all[first_random + j] = joined(mine_ref[j, 0], other_ref[j, 0])
            return carry

        lax.fori_loop(0, peers, fetched, 0)
        for j in range(G):
            kt_all[first_global + j] = joined(glob_mine_ref[j, 0], glob_other_ref[j, 0])
        acc[...] = jnp.zeros_like(acc)

    for u in range(PER_STEP):
        b = step * PER_STEP + u
        q = stack_heads(q_ref[u * BLOCK : (u + 1) * BLOCK, :])
        g = stack_heads(g_ref[u * BLOCK : (u + 1) * BLOCK, :])
        parts = [kt_all[b + w] for w in range(WINDOW)]
        parts += [kt_all[first_random + owners[b * R + r]] for r in range(R)]
        parts += [kt_all[first_global + j] for j in range(G)]
        ds = ds_ref[u]
        dqt = mm(jnp.concatenate(parts, axis=1), ds, NN) * FACTOR
        heads = q_ref.shape[1] // DH
        for h in range(heads):
            dq_ref[u * BLOCK : (u + 1) * BLOCK, h * DH : (h + 1) * DH] = (
                dqt[:, h * BLOCK : (h + 1) * BLOCK].T.astype(jnp.bfloat16)
            )
        dk = mm(ds[: WINDOW * BLOCK], q, NN).reshape(WINDOW, BLOCK, DH)
        dv = mm(pw_ref[u], g, NN).reshape(WINDOW, BLOCK, DH)
        acc[pl.ds(b, WINDOW), 0] += dk
        acc[pl.ds(b, WINDOW), 1] += dv

    @pl.when(step == pl.num_programs(0) - 1)
    def _():
        for which, f in ((0, FACTOR), (1, 1.0)):
            keep_ref[:, which] = acc[1 : blocks + 1, which, pl.ds(core * half, half), :] * f
            send_ref[:, which] = (
                acc[1 : blocks + 1, which, pl.ds((1 - core) * half, half), :] * f
            ).astype(jnp.bfloat16)


def whole(shape):
    return pl.BlockSpec(shape, lambda i, *_: (0,) * len(shape))


def partners(size, stride):
    return [(i, i ^ stride) for i in range(size)]


def body(query_vectors, key_vectors, value_vectors, output_grad, random_blocks, global_blocks):
    seq_count = lax.axis_size("seq")
    seq_index = lax.axis_index("seq")
    head_count = lax.axis_size("head")
    head_index = lax.axis_index("head")
    rows_dev, columns = query_vectors.shape
    blocks = rows_dev // BLOCK
    half = BLOCK // 2
    steps = blocks // PER_STEP
    stacked = PER_STEP * BLOCK
    lanes = columns // DH * BLOCK
    bf16 = jnp.bfloat16
    core = head_index % 2
    core_pairs = partners(head_count, 1)
    slots = seq_count + G + 2

    owners = random_blocks // blocks
    within = random_blocks % blocks
    peer_ids = jnp.arange(seq_count, dtype=jnp.int32)
    matched = owners[:, :, None] == peer_ids[None, None, :]
    wanted = jnp.max(jnp.where(matched, within[:, :, None], -1), axis=(0, 1))
    requested = lax.all_to_all(
        wanted.reshape(seq_count, 1), "seq", split_axis=0, concat_axis=0, tiled=True
    )[:, 0]
    owner_list = owners.reshape(-1)

    up = [(i, i + 1) for i in range(seq_count - 1)]
    down = [(i + 1, i) for i in range(seq_count - 1)]
    last = jnp.stack([key_vectors[-BLOCK:], value_vectors[-BLOCK:]])
    first = jnp.stack([key_vectors[:BLOCK], value_vectors[:BLOCK]])
    before = lax.ppermute(last, "seq", up)
    after = lax.ppermute(first, "seq", down)

    def half_block(index):
        start = index * BLOCK + core * half
        return jnp.stack(
            [lax.dynamic_slice_in_dim(a, start, half, 0) for a in (key_vectors, value_vectors)]
        )

    global_part = jnp.stack([half_block(global_blocks[j] % blocks) for j in range(G)])
    spread = lax.all_to_all(
        jnp.broadcast_to(global_part[None], (seq_count,) + global_part.shape),
        "seq",
        split_axis=0,
        concat_axis=0,
        tiled=True,
    )
    glob_mine = jnp.stack(
        [
            lax.dynamic_index_in_dim(spread[:, j], global_blocks[j] // blocks, 0, keepdims=False)
            for j in range(G)
        ]
    )
    glob_other = lax.ppermute(glob_mine, "head", core_pairs)

    vmem = pl.BlockSpec(memory_space=pltpu.VMEM)
    served = pl.pallas_call(
        serve_kernel,
        out_shape=jax.ShapeDtypeStruct((seq_count, 2, half, DH), bf16),
        in_specs=[pl.BlockSpec(memory_space=pltpu.SMEM), vmem, vmem],
        out_specs=vmem,
        name="serve",
    )(requested, key_vectors, value_vectors)
    mine = lax.all_to_all(served, "seq", split_axis=0, concat_axis=0, tiled=True)
    other = lax.ppermute(mine, "head", core_pairs)

    block_rows = pl.BlockSpec((stacked, columns), lambda i, *_: (i, 0))
    fetched_specs = [
        whole(before.shape),
        whole(after.shape),
        whole(mine.shape),
        whole(other.shape),
        whole(glob_mine.shape),
        whole(glob_other.shape),
    ]
    fetched = (before, after, mine, other, glob_mine, glob_other)
    ds_spec = pl.BlockSpec((PER_STEP, LISTED * BLOCK, lanes), lambda i, *_: (i, 0, 0))
    pw_spec = pl.BlockSpec((PER_STEP, WINDOW * BLOCK, lanes), lambda i, *_: (i, 0, 0))
    piece = (slots, 2, half, DH)
    all_blocks = blocks + 2 + seq_count + G
    unit = 2 * blocks * lanes * LISTED * BLOCK * DH
    params = pltpu.CompilerParams(
        dimension_semantics=("arbitrary",), vmem_limit_bytes=VMEM_LIMIT
    )
    ds, pw, keep, send = pl.pallas_call(
        attend_kernel,
        out_shape=(
            jax.ShapeDtypeStruct((blocks, LISTED * BLOCK, lanes), bf16),
            jax.ShapeDtypeStruct((blocks, WINDOW * BLOCK, lanes), bf16),
            jax.ShapeDtypeStruct(piece, jnp.float32),
            jax.ShapeDtypeStruct(piece, bf16),
        ),
        grid_spec=pltpu.PrefetchScalarGridSpec(
            num_scalar_prefetch=1,
            grid=(steps,),
            in_specs=[block_rows, block_rows, whole(key_vectors.shape), whole(value_vectors.shape)]
            + fetched_specs,
            out_specs=(ds_spec, pw_spec, whole(piece), whole(piece)),
            scratch_shapes=[
                pltpu.VMEM((all_blocks, BLOCK, DH), bf16),
                pltpu.VMEM((all_blocks, BLOCK, DH), bf16),
                pltpu.VMEM((slots, 2, BLOCK, DH), jnp.float32),
            ],
        ),
        compiler_params=params,
        cost_estimate=pl.CostEstimate(
            flops=4 * unit, bytes_accessed=16 << 20, transcendentals=blocks * lanes * LISTED * BLOCK
        ),
        name="attend",
    )(owner_list, query_vectors, output_grad, key_vectors, value_vectors, *fetched)

    piece_w = (blocks, 2, half, DH)
    query_grad, keep_w, send_w = pl.pallas_call(
        window_kernel,
        out_shape=(
            jax.ShapeDtypeStruct(query_vectors.shape, bf16),
            jax.ShapeDtypeStruct(piece_w, jnp.float32),
            jax.ShapeDtypeStruct(piece_w, bf16),
        ),
        grid_spec=pltpu.PrefetchScalarGridSpec(
            num_scalar_prefetch=1,
            grid=(steps,),
            in_specs=[block_rows, block_rows, whole(key_vectors.shape)]
            + fetched_specs
            + [ds_spec, pw_spec],
            out_specs=(block_rows, whole(piece_w), whole(piece_w)),
            scratch_shapes=[
                pltpu.VMEM((all_blocks, BLOCK, DH), bf16),
                pltpu.VMEM((blocks + 2, 2, BLOCK, DH), jnp.float32),
            ],
        ),
        compiler_params=params,
        cost_estimate=pl.CostEstimate(flops=2 * unit, bytes_accessed=16 << 20, transcendentals=0),
        name="window",
    )(owner_list, query_vectors, output_grad, key_vectors, *fetched, ds, pw)

    def reduced(kept, sent):
        total = kept + lax.ppermute(sent, "head", core_pairs).astype(jnp.float32)
        stride = 2
        while stride < head_count:
            size = total.shape[2] // 2
            bit = (head_index // stride) % 2
            away = lax.dynamic_slice_in_dim(total, (1 - bit) * size, size, 2).astype(bf16)
            home = lax.dynamic_slice_in_dim(total, bit * size, size, 2)
            total = home + lax.ppermute(away, "head", partners(head_count, stride)).astype(
                jnp.float32
            )
            stride *= 2
        return total

    shared = reduced(keep, send)
    share = shared.shape[2]
    shared_low = shared.astype(bf16)
    terms = jnp.concatenate(
        [
            shared_low[:seq_count].reshape(seq_count, 2, share, DH),
            jnp.broadcast_to(
                shared_low[seq_count : seq_count + G].reshape(1, 2 * G, share, DH),
                (seq_count, 2 * G, share, DH),
            ),
        ],
        axis=1,
    )
    returned = lax.all_to_all(terms, "seq", split_axis=0, concat_axis=0, tiled=True).astype(
        jnp.float32
    )
    into_last = lax.ppermute(shared_low[seq_count + G], "seq", down).astype(jnp.float32)
    into_first = lax.ppermute(shared_low[seq_count + G + 1], "seq", up).astype(jnp.float32)
    total = reduced(keep_w, send_w)
    block_range = jnp.arange(blocks, dtype=jnp.int32)
    served_hot = (requested[None, :] == block_range[:, None]).astype(jnp.float32)
    total = total + jnp.einsum(
        "je,ewrd->jwrd", served_hot, returned[:, :2], precision=lax.Precision.HIGHEST
    )
    global_sum = jnp.sum(returned[:, 2:], axis=0).reshape(G, 2, share, DH)
    owned = (global_blocks[None, :] == seq_index * blocks + block_range[:, None]).astype(jnp.float32)
    for j in range(G):
        total = total + owned[:, j][:, None, None, None] * global_sum[j][None]
    total = total.at[blocks - 1].add(into_last)
    total = total.at[0].add(into_first)

    held = total.astype(bf16)
    stride = head_count // 2
    while stride >= 1:
        there = lax.ppermute(held, "head", partners(head_count, stride))
        bit = (head_index // stride) % 2
        low = jnp.where(bit == 0, held, there)
        high = jnp.where(bit == 0, there, held)
        held = jnp.concatenate([low, high], axis=2)
        stride //= 2
    return (
        query_grad,
        held[:, 0].reshape(rows_dev, DH),
        held[:, 1].reshape(rows_dev, DH),
    )


def solution(mesh):
    return jax.shard_map(
        body,
        mesh=mesh,
        in_specs=(
            P("seq", "head"),
            P("seq", None),
            P("seq", None),
            P("seq", "head"),
            P("seq", None),
            P(),
        ),
        out_specs=(P("seq", "head"), P("seq", None), P("seq", None)),
        check_vma=False,
    )
```

```python
import functools
import math

import jax
import jax.numpy as jnp
from jax import lax
from jax.experimental import pallas as pl
from jax.experimental.pallas import tpu as pltpu
from jax.sharding import PartitionSpec as P

DH = 128
BLOCK = 128
HALF = BLOCK // 2
R = 3
G = 2
WINDOW = 3
FAR = R + G
LISTED = WINDOW + FAR
MIB = 1024 * 1024
MASKED = -1e30
FACTOR = float(DH) ** -0.5
SCALE = FACTOR * math.log2(math.e)
FOLD = 8

NT = (((1,), (1,)), ((), ()))
NN = (((1,), (0,)), ((), ()))


def mm(a, b, dims):
    return lax.dot_general(a, b, dims, preferred_element_type=jnp.float32)


def stack_heads(ref, u):
    rows = ref[u * BLOCK : (u + 1) * BLOCK, :]
    return jnp.concatenate(
        [rows[:, h * DH : (h + 1) * DH] for h in range(rows.shape[1] // DH)], axis=0
    )


def fold(x):
    return jnp.sum(x.reshape(x.shape[0] // FOLD, FOLD, x.shape[1]), axis=0)


def panel(k, v, q, g):
    s = mm(k, q, NT)
    dp = mm(v, g, NT)
    top = jnp.max(s, axis=0, keepdims=True) * SCALE
    e = jnp.exp2(s * SCALE - top)
    return top, e, dp, fold(e), fold(e * dp)


def places():
    head_index = lax.axis_index("head")
    return lax.rem(head_index, 2), lax.div(head_index, 2)


def ask_kernel(global_blocks, random_ref, k_ref, v_ref, out_ref, low_ref, high_ref, rows, sems):
    tokens = k_ref.shape[0]
    blocks = tokens // BLOCK
    share = BLOCK // lax.axis_size("head")
    core, column = places()
    marks = 2 * G * share
    edges, copies = [], []

    def begin(group, src, dst):
        group.append(pltpu.make_async_copy(src, dst, sems.at[len(edges) + len(copies)]))
        group[-1].start()

    for which, ref in ((0, k_ref), (1, v_ref)):
        for j in range(G):
            start = lax.rem(global_blocks[j], blocks) * BLOCK + core * HALF + column * share
            start = pl.multiple_of(start, share)
            begin(copies, ref.at[pl.ds(start, share), :], rows.at[2 * j + which])
    odd = lax.rem(lax.axis_index("seq"), 2)
    for which, ref in ((0, k_ref), (1, v_ref)):
        for edge_ref, at in ((low_ref, (1 - odd) * (tokens - BLOCK)), (high_ref, odd * (tokens - BLOCK))):
            start = pl.multiple_of(at, BLOCK)
            begin(edges, ref.at[pl.ds(start, BLOCK), :], edge_ref.at[which])
    wanted = random_ref[...]

    def mark(j, carry):
        within = wanted - j * blocks
        mine = jnp.logical_and(within >= 0, within < blocks)
        top = jnp.max(jnp.where(mine, within, -1).astype(jnp.float32))
        out_ref[j, marks:, :] = jnp.full((16, DH), top, jnp.float32).astype(jnp.bfloat16)
        return carry

    peers = out_ref.shape[0]
    lax.fori_loop(0, peers, mark, 0, unroll=min(peers, 8))
    for copy in copies:
        copy.wait()
    for i in range(2 * G):
        out_ref[:, i * share : (i + 1) * share, :] = jnp.broadcast_to(
            rows[i][None], (peers, share, DH)
        )
    for copy in edges:
        copy.wait()


def serve_kernel(global_blocks, asked_ref, k_ref, v_ref, out_ref, glob_ref, requested_ref, sems):
    blocks = k_ref.shape[0] // BLOCK
    share = BLOCK // lax.axis_size("head")
    core, _ = places()
    marks = 2 * G * share
    peers = out_ref.shape[0]
    many = min(peers, 8)

    def copy(j, start, which, ref):
        return pltpu.make_async_copy(
            ref.at[pl.ds(start, HALF), :], out_ref.at[j, which], sems.at[j, which]
        )

    def begin(j, carry):
        wanted = jnp.max(asked_ref[j, marks:, :].astype(jnp.float32)).astype(jnp.int32)
        requested_ref[j] = wanted
        start = pl.multiple_of(jnp.clip(wanted, 0, blocks - 1) * BLOCK + core * HALF, HALF)
        copy(j, start, 0, k_ref).start()
        copy(j, start, 1, v_ref).start()
        return carry

    lax.fori_loop(0, peers, begin, 0, unroll=many)
    for j in range(G):
        owner = lax.div(global_blocks[j], blocks)
        for which in range(2):
            at = (2 * j + which) * share
            glob_ref[j, which] = asked_ref[owner, at : at + share, :]

    def end(j, carry):
        copy(j, 0, 0, k_ref).wait()
        copy(j, 0, 1, v_ref).wait()
        return carry

    lax.fori_loop(0, peers, end, 0, unroll=many)


def glob_kernel(*refs):
    *part_refs, out_ref = refs
    share = part_refs[0].shape[2]
    core, column = places()
    for m, ref in enumerate(part_refs):
        at = (core ^ (m & 1)) * HALF + (column ^ (m >> 1)) * share
        out_ref[:, :, pl.ds(pl.multiple_of(at, share), share), :] = ref[...]


def split_kernel(count, keep_ref, got_ref, out_ref, *send_refs):
    share = out_ref.shape[2]
    _, column = places()
    own = pl.ds(pl.multiple_of(column * share, share), share)
    out_ref[...] = keep_ref[:, :, own, :] + got_ref[:, :, own, :].astype(jnp.float32)
    for m in range(1, count):
        there = pl.ds(pl.multiple_of((column ^ m) * share, share), share)
        send_refs[m - 1][...] = (
            keep_ref[:, :, there, :] + got_ref[:, :, there, :].astype(jnp.float32)
        ).astype(jnp.bfloat16)


def terms_kernel(keep_ref, *refs):
    *got_refs, terms_ref = refs
    peers, _, share, _ = terms_ref.shape
    me = lax.axis_index("seq")

    def total(slot, n=1):
        x = keep_ref[slot : slot + n]
        for ref in got_refs:
            x = x + ref[slot : slot + n].astype(jnp.float32)
        return x.astype(jnp.bfloat16)

    terms_ref[:, :2] = total(0, peers)
    glob = total(peers, G).reshape(1, 2 * G, share, DH)
    terms_ref[:, 2 : 2 + 2 * G] = jnp.broadcast_to(glob, (peers, 2 * G, share, DH))
    to_last = total(peers + G)[0]
    to_first = total(peers + G + 1)[0]

    def halo(j, carry):
        terms_ref[j, 2 + 2 * G :] = jnp.where(j > me, to_first, to_last)
        return carry

    lax.fori_loop(0, peers, halo, 0, unroll=min(peers, 8))


def settle_kernel(requested, global_blocks, back_ref, keep_ref, *refs):
    *got_refs, out_ref, acc = refs
    blocks = keep_ref.shape[0]
    peers, _, share, _ = back_ref.shape
    seq_index = lax.axis_index("seq")
    x = keep_ref[...]
    for ref in got_refs:
        x = x + ref[...].astype(jnp.float32)
    acc[...] = x
    halo = slice(2 + 2 * G, 4 + 2 * G)

    @pl.when(seq_index > 0)
    def _():
        acc[0] += back_ref[jnp.maximum(seq_index - 1, 0), halo].astype(jnp.float32)

    @pl.when(seq_index < peers - 1)
    def _():
        acc[blocks - 1] += back_ref[jnp.minimum(seq_index + 1, peers - 1), halo].astype(jnp.float32)

    def one(j, carry):
        wanted = requested[j]

        @pl.when(wanted >= 0)
        def _():
            acc[wanted] += back_ref[j, :2].astype(jnp.float32)

        return carry

    lax.fori_loop(0, peers, one, 0)
    for j in range(G):

        @pl.when(lax.div(global_blocks[j], blocks) == seq_index)
        def _():
            rows = back_ref[:, 2 + 2 * j : 4 + 2 * j].astype(jnp.float32)
            acc[lax.rem(global_blocks[j], blocks)] += jnp.sum(rows, axis=0)

    out_ref[...] = acc[...].astype(jnp.bfloat16)


def join_kernel(count, *refs):
    *got_refs, dk_ref, dv_ref, dk, dv = refs
    blocks, _, share, _ = got_refs[0].shape
    core, column = places()
    for m in range(count):
        for c in range(2):
            at = (core ^ c) * HALF + (column ^ m) * share
            rows = pl.ds(pl.multiple_of(at, share), share)
            ref = got_refs[2 * m + c]
            dk[:, rows, :] = ref[:, 0]
            dv[:, rows, :] = ref[:, 1]
    dk_ref[...] = dk[...].reshape(dk_ref.shape)
    dv_ref[...] = dv[...].reshape(dv_ref.shape)


def edge_places(blocks):
    odd = lax.rem(lax.axis_index("seq"), 2)
    return (1 - odd) * (blocks + 1), odd * (blocks + 1)


def fill_window(k_ref, v_ref, low_ref, high_ref, k_all, v_all):
    rows = k_ref.shape[0]
    low, high = (pl.ds(pl.multiple_of(i * BLOCK, BLOCK), BLOCK) for i in edge_places(rows // BLOCK))
    for to, own, which in ((k_all, k_ref, 0), (v_all, v_ref, 1)):
        to[low, :] = low_ref[which]
        to[high, :] = high_ref[which]
        to[BLOCK : BLOCK + rows] = own[...]


def near_kernel(q_ref, g_ref, k_ref, v_ref, low_ref, high_ref, st_ref, k_all, v_all):
    step = pl.program_id(0)
    blocks = k_ref.shape[0] // BLOCK
    seq_index = lax.axis_index("seq")
    per = st_ref.shape[0]

    @pl.when(step == 0)
    def _():
        fill_window(k_ref, v_ref, low_ref, high_ref, k_all, v_all)

    for u in range(per):
        b = step * per + u
        q = stack_heads(q_ref, u)
        g = stack_heads(g_ref, u)
        no_left = jnp.logical_and(seq_index == 0, b == 0)
        no_right = jnp.logical_and(seq_index == lax.axis_size("seq") - 1, b == blocks - 1)
        biases = (jnp.where(no_left, MASKED, 0.0), None, jnp.where(no_right, MASKED, 0.0))
        for w in range(WINDOW):
            rows = pl.ds(pl.multiple_of((b + w) * BLOCK, BLOCK), BLOCK)
            top, _, _, l, d = panel(k_all[rows, :], v_all[rows, :], q, g)
            if biases[w] is not None:
                top = top + biases[w]
            st_ref[u, w : w + 1] = top
            st_ref[u, WINDOW + w : WINDOW + w + 1] = jnp.sum(l, axis=0, keepdims=True)
            st_ref[u, 2 * WINDOW + w : 2 * WINDOW + w + 1] = jnp.sum(d, axis=0, keepdims=True)


def far_kernel(
    random_blocks, q_ref, g_ref, mine_ref, other_ref, glob_ref, st_ref, low_ref, high_ref,
    ds_ref, fd_ref, keep_ref, send_ref, k_all, v_all, acc,
):
    step = pl.program_id(0)
    peers = mine_ref.shape[0]
    per = ds_ref.shape[0]
    blocks = per * pl.num_programs(0)
    core = lax.rem(lax.axis_index("head"), 2)
    own, opp = pl.ds(core * HALF, HALF), pl.ds((1 - core) * HALF, HALF)

    @pl.when(step == 0)
    def _():
        for to, which in ((k_all, 0), (v_all, 1)):
            to[:peers, own, :] = mine_ref[:, which]
            to[:peers, opp, :] = other_ref[:, which]
            to[peers:] = glob_ref[:, which]
        acc[...] = jnp.zeros_like(acc)

    for u in range(per):
        b = step * per + u
        q = stack_heads(q_ref, u)
        g = stack_heads(g_ref, u)
        slots = [lax.div(random_blocks[b, r], blocks) for r in range(R)] + [peers + j for j in range(G)]
        parts = [panel(k_all[i], v_all[i], q, g) for i in slots]
        near = [[st_ref[u, i * WINDOW + w : i * WINDOW + w + 1] for w in range(WINDOW)] for i in range(3)]
        top = functools.reduce(jnp.maximum, near[0] + [x[0] for x in parts])
        near_weight = [jnp.exp2(t - top) for t in near[0]]
        weight = [jnp.exp2(x[0] - top) for x in parts]
        l = jnp.sum(sum(w * x[3] for w, x in zip(weight, parts)), axis=0, keepdims=True)
        d = jnp.sum(sum(w * x[4] for w, x in zip(weight, parts)), axis=0, keepdims=True)
        l = l + sum(w * x for w, x in zip(near_weight, near[1]))
        d = d + sum(w * x for w, x in zip(near_weight, near[2]))
        inv = 1.0 / l
        delta = d * inv
        for w in range(WINDOW):
            fd_ref[u, w : w + 1] = near[0][w]
            fd_ref[u, WINDOW + w : WINDOW + w + 1] = near_weight[w] * inv
        fd_ref[u, 2 * WINDOW : 2 * WINDOW + 1] = delta
        for i in range(FAR):
            _, e, dp, _, _ = parts[i]
            p = e * (weight[i] * inv)
            ds = (p * (dp - delta)).astype(jnp.bfloat16)
            ds_ref[u, i * BLOCK : (i + 1) * BLOCK] = ds
            acc[slots[i], 0] += mm(ds, q, NN)
            acc[slots[i], 1] += mm(p.astype(jnp.bfloat16), g, NN)

        def halo(slot, w, swap):
            odd = lax.rem(lax.axis_index("seq"), 2) == swap
            s = mm(jnp.where(odd, low_ref[0], high_ref[0]), q, NT)
            dp = mm(jnp.where(odd, low_ref[1], high_ref[1]), g, NT)
            p = jnp.exp2(s * SCALE - jnp.max(s, axis=0, keepdims=True) * SCALE) * (near_weight[w] * inv)
            ds = (p * (dp - delta)).astype(jnp.bfloat16)
            acc[slot, 0] = mm(ds, q, NN)
            acc[slot, 1] = mm(p.astype(jnp.bfloat16), g, NN)

        if u == 0:
            pl.when(step == 0)(functools.partial(halo, peers + G, 0, 1))
        if u == per - 1:
            pl.when(step == pl.num_programs(0) - 1)(
                functools.partial(halo, peers + G + 1, WINDOW - 1, 0)
            )

    @pl.when(step == pl.num_programs(0) - 1)
    def _():
        for which, f in ((0, FACTOR), (1, 1.0)):
            keep_ref[:, which] = acc[:, which, own, :] * f
            send_ref[:, which] = (acc[:, which, opp, :] * f).astype(jnp.bfloat16)


def window_kernel(
    q_ref, g_ref, k_ref, v_ref, low_ref, high_ref, fd_ref, ds_ref, keep_ref, send_ref, k_all, v_all, acc
):
    step = pl.program_id(0)
    per = ds_ref.shape[0]
    core = lax.rem(lax.axis_index("head"), 2)
    own, opp = pl.ds(core * HALF, HALF), pl.ds((1 - core) * HALF, HALF)

    @pl.when(step == 0)
    def _():
        fill_window(k_ref, v_ref, low_ref, high_ref, k_all, v_all)
        acc[...] = jnp.zeros_like(acc)

    for u in range(per):
        b = step * per + u
        q = stack_heads(q_ref, u)
        g = stack_heads(g_ref, u)
        delta = fd_ref[u, 2 * WINDOW : 2 * WINDOW + 1]
        ds, pb = [], []
        for w in range(WINDOW):
            rows = pl.ds(pl.multiple_of((b + w) * BLOCK, BLOCK), BLOCK)
            s = mm(k_all[rows, :], q, NT)
            dp = mm(v_all[rows, :], g, NT)
            top = fd_ref[u, w : w + 1]
            top = jnp.where(top < MASKED / 2, 0.0, top)
            p = jnp.exp2(s * SCALE - top) * fd_ref[u, WINDOW + w : WINDOW + w + 1]
            ds.append((p * (dp - delta)).astype(jnp.bfloat16))
            ds_ref[u, w * BLOCK : (w + 1) * BLOCK] = ds[w]
            pb.append(p.astype(jnp.bfloat16))
        shape = (WINDOW, BLOCK, DH)
        acc[pl.ds(b, WINDOW), 0] += mm(jnp.concatenate(ds, axis=0), q, NN).reshape(shape)
        acc[pl.ds(b, WINDOW), 1] += mm(jnp.concatenate(pb, axis=0), g, NN).reshape(shape)

    @pl.when(step == pl.num_programs(0) - 1)
    def _():
        for which, f in ((0, FACTOR), (1, 1.0)):
            keep_ref[:, which] = acc[1:-1, which, own, :] * f
            send_ref[:, which] = (acc[1:-1, which, opp, :] * f).astype(jnp.bfloat16)


def queries_kernel(
    random_blocks, k_ref, low_ref, high_ref, mine_ref, other_ref, glob_ref,
    dsw_ref, dsf_ref, dq_ref, kt_all,
):
    blocks = k_ref.shape[0] // BLOCK
    peers = mine_ref.shape[0]
    per = dsw_ref.shape[0]
    core = lax.rem(lax.axis_index("head"), 2)
    step = pl.program_id(0)
    first_random = blocks + 2
    first_global = first_random + peers

    @pl.when(step == 0)
    def _():
        at_low, at_high = edge_places(blocks)
        kt_all[at_low] = low_ref[0].T
        kt_all[at_high] = high_ref[0].T

        def own(j, carry):
            kt_all[j + 1] = k_ref[pl.ds(pl.multiple_of(j * BLOCK, BLOCK), BLOCK), :].T
            return carry

        lax.fori_loop(0, blocks, own, 0)

        def joined(a, b):
            low = jnp.where(core == 0, a, b)
            high = jnp.where(core == 0, b, a)
            return jnp.concatenate([low, high], axis=0).T

        def fetched(j, carry):
            kt_all[first_random + j] = joined(mine_ref[j, 0], other_ref[j, 0])
            return carry

        lax.fori_loop(0, peers, fetched, 0)
        for j in range(G):
            kt_all[first_global + j] = glob_ref[j, 0].T

    for u in range(per):
        b = step * per + u
        near = [kt_all[b + w] for w in range(WINDOW)]
        far = [kt_all[first_random + lax.div(random_blocks[b, r], blocks)] for r in range(R)]
        far += [kt_all[first_global + j] for j in range(G)]
        dqt = mm(jnp.concatenate(near, axis=1), dsw_ref[u], NN)
        dqt = (dqt + mm(jnp.concatenate(far, axis=1), dsf_ref[u], NN)) * FACTOR
        for h in range(dq_ref.shape[1] // DH):
            dq_ref[u * BLOCK : (u + 1) * BLOCK, h * DH : (h + 1) * DH] = (
                dqt[:, h * BLOCK : (h + 1) * BLOCK].T.astype(jnp.bfloat16)
            )


def whole(a):
    return pl.BlockSpec(a.shape, lambda i, *_: (0,) * len(a.shape))


def per_block(per, *rest):
    return pl.BlockSpec((per,) + rest, lambda i, *_: (i,) + (0,) * len(rest))


def partners(size, stride):
    return [(i, i ^ stride) for i in range(size)]


def body(query_vectors, key_vectors, value_vectors, output_grad, random_blocks, global_blocks):
    seq_count = lax.axis_size("seq")
    head_count = lax.axis_size("head")
    rows_dev, columns = query_vectors.shape
    blocks = rows_dev // BLOCK
    per = math.gcd(blocks, 4)
    steps = blocks // per
    lanes = columns // DH * BLOCK
    bf16 = jnp.bfloat16
    f32 = jnp.float32
    sds = jax.ShapeDtypeStruct
    core_pairs = partners(head_count, 1)
    limit = (16 + seq_count // 2) * MIB
    params = pltpu.CompilerParams(dimension_semantics=("arbitrary",), vmem_limit_bytes=limit)
    unit = 2 * blocks * lanes * BLOCK * DH

    vmem = pl.BlockSpec(memory_space=pltpu.VMEM)
    smem = pl.BlockSpec(memory_space=pltpu.SMEM)
    hbm = pl.BlockSpec(memory_space=pltpu.HBM)
    small = pltpu.CompilerParams(vmem_limit_bytes=limit)
    large = pltpu.CompilerParams(vmem_limit_bytes=60 * MIB)
    share = BLOCK // head_count
    columns_count = head_count // 2

    edge = (2, BLOCK, DH)
    asking, to_low, to_high = pl.pallas_call(
        ask_kernel,
        out_shape=(
            sds((seq_count, 2 * G * share + 16, DH), bf16),
            sds(edge, bf16),
            sds(edge, bf16),
        ),
        in_specs=[smem, vmem, hbm, hbm],
        out_specs=(vmem, vmem, vmem),
        scratch_shapes=[
            pltpu.VMEM((2 * G, share, DH), bf16),
            pltpu.SemaphoreType.DMA((2 * G + 4,)),
        ],
        compiler_params=large,
        name="ask",
    )(global_blocks, random_blocks.T, key_vectors, value_vectors)
    asked = lax.all_to_all(asking, "seq", split_axis=0, concat_axis=0, tiled=True)

    low_pairs = [(i, i ^ 1) for i in range(seq_count)]
    high_pairs = [(i, i + 1 if i % 2 else i - 1) for i in range(1, seq_count - 1)]
    low = lax.ppermute(to_low, "seq", low_pairs)
    high = lax.ppermute(to_high, "seq", high_pairs)
    asked, low, high = lax.optimization_barrier((asked, low, high))

    served, glob_part, requested = pl.pallas_call(
        serve_kernel,
        out_shape=(
            sds((seq_count, 2, HALF, DH), bf16),
            sds((G, 2, share, DH), bf16),
            sds((seq_count,), jnp.int32),
        ),
        in_specs=[smem, vmem, hbm, hbm],
        out_specs=(vmem, vmem, smem),
        scratch_shapes=[pltpu.SemaphoreType.DMA((seq_count, 2))],
        compiler_params=large,
        name="serve",
    )(global_blocks, asked, key_vectors, value_vectors)
    mine = lax.all_to_all(served, "seq", split_axis=0, concat_axis=0, tiled=True)
    glob_parts = [glob_part] + [
        lax.ppermute(glob_part, "head", partners(head_count, m)) for m in range(1, head_count)
    ]
    glob = pl.pallas_call(
        glob_kernel,
        out_shape=sds((G, 2, BLOCK, DH), bf16),
        in_specs=[vmem] * head_count,
        out_specs=vmem,
        compiler_params=large,
        name="glob",
    )(*glob_parts)

    rows_spec = pl.BlockSpec((per * BLOCK, columns), lambda i, *_: (i, 0))
    near_spec = per_block(per, WINDOW * BLOCK, lanes)
    far_spec = per_block(per, FAR * BLOCK, lanes)
    st_spec = per_block(per, 2 * FOLD, lanes)
    fd_spec = per_block(per, FOLD, lanes)
    near_shape = sds((blocks, WINDOW * BLOCK, lanes), bf16)
    far_shape = sds((blocks, FAR * BLOCK, lanes), bf16)

    nearby = (key_vectors, value_vectors, low, high)
    window_scratch = [pltpu.VMEM(((blocks + 2) * BLOCK, DH), bf16)] * 2
    st = pl.pallas_call(
        near_kernel,
        out_shape=sds((blocks, 2 * FOLD, lanes), f32),
        grid=(steps,),
        in_specs=[rows_spec, rows_spec] + [whole(a) for a in nearby],
        out_specs=st_spec,
        scratch_shapes=window_scratch,
        compiler_params=large,
        cost_estimate=pl.CostEstimate(
            flops=2 * WINDOW * unit, bytes_accessed=4 * MIB, transcendentals=blocks * lanes * WINDOW * BLOCK
        ),
        name="near",
    )(query_vectors, output_grad, *nearby)
    mine, st, glob = lax.optimization_barrier((mine, st, glob))
    other = lax.ppermute(mine, "head", core_pairs)
    fetched = (mine, other, glob)
    slots = seq_count + G + 2
    piece = (slots, 2, HALF, DH)
    dsf, fd, keep, send = pl.pallas_call(
        far_kernel,
        out_shape=(far_shape, sds((blocks, FOLD, lanes), f32), sds(piece, f32), sds(piece, bf16)),
        grid_spec=pltpu.PrefetchScalarGridSpec(
            num_scalar_prefetch=1,
            grid=(steps,),
            in_specs=[rows_spec, rows_spec] + [whole(a) for a in fetched] + [st_spec, whole(low), whole(high)],
            out_specs=(far_spec, fd_spec, whole(sds(piece, f32)), whole(sds(piece, bf16))),
            scratch_shapes=[pltpu.VMEM((seq_count + G, BLOCK, DH), bf16)] * 2
            + [pltpu.VMEM((slots, 2, BLOCK, DH), f32)],
        ),
        compiler_params=params,
        cost_estimate=pl.CostEstimate(
            flops=4 * FAR * unit, bytes_accessed=8 * MIB, transcendentals=blocks * lanes * FAR * BLOCK
        ),
        name="far",
    )(random_blocks, query_vectors, output_grad, *fetched, st, low, high)

    piece_w = (blocks, 2, HALF, DH)
    dsw, keep_w, send_w = pl.pallas_call(
        window_kernel,
        out_shape=(near_shape, sds(piece_w, f32), sds(piece_w, bf16)),
        grid=(steps,),
        in_specs=[rows_spec, rows_spec] + [whole(a) for a in nearby] + [fd_spec],
        out_specs=(near_spec, whole(sds(piece_w, f32)), whole(sds(piece_w, bf16))),
        scratch_shapes=window_scratch + [pltpu.VMEM((blocks + 2, 2, BLOCK, DH), f32)],
        compiler_params=params,
        cost_estimate=pl.CostEstimate(flops=2 * WINDOW * unit, bytes_accessed=8 * MIB, transcendentals=0),
        name="window",
    )(query_vectors, output_grad, *nearby, fd)

    query_grad = pl.pallas_call(
        queries_kernel,
        out_shape=sds(query_vectors.shape, bf16),
        grid_spec=pltpu.PrefetchScalarGridSpec(
            num_scalar_prefetch=1,
            grid=(steps,),
            in_specs=[whole(a) for a in (key_vectors, low, high) + fetched] + [near_spec, far_spec],
            out_specs=rows_spec,
            scratch_shapes=[pltpu.VMEM((blocks + 2 + slots, BLOCK, DH), bf16)],
        ),
        compiler_params=params,
        cost_estimate=pl.CostEstimate(flops=LISTED * unit, bytes_accessed=8 * MIB, transcendentals=0),
        name="queries",
    )(random_blocks, key_vectors, low, high, *fetched, dsw, dsf)

    others = [m << 1 for m in range(1, columns_count)]

    def reduced(kept, sent, name):
        got = lax.ppermute(sent, "head", core_pairs)
        part = (kept.shape[0], 2, share, DH)
        home, *away = pl.pallas_call(
            functools.partial(split_kernel, columns_count),
            out_shape=(sds(part, f32),) + (sds(part, bf16),) * len(others),
            in_specs=[vmem, vmem],
            out_specs=(vmem,) * (1 + len(others)),
            compiler_params=small,
            name=name,
        )(kept, got)
        return [home] + [
            lax.ppermute(a, "head", partners(head_count, m)) for a, m in zip(away, others)
        ]

    parts = reduced(keep, send, "split_far")
    parts[-1], send_w = lax.optimization_barrier((parts[-1], send_w))
    parts_w = reduced(keep_w, send_w, "split_window")
    terms = pl.pallas_call(
        terms_kernel,
        out_shape=sds((seq_count, 4 + 2 * G, share, DH), bf16),
        in_specs=[vmem] * len(parts),
        out_specs=vmem,
        compiler_params=small,
        name="terms",
    )(*parts)
    back = lax.all_to_all(terms, "seq", split_axis=0, concat_axis=0, tiled=True)
    back, query_grad = lax.optimization_barrier((back, query_grad))
    held = pl.pallas_call(
        settle_kernel,
        out_shape=sds((blocks, 2, share, DH), bf16),
        in_specs=[smem, smem] + [vmem] * (1 + len(parts_w)),
        out_specs=vmem,
        scratch_shapes=[pltpu.VMEM((blocks, 2, share, DH), f32)],
        compiler_params=small,
        name="settle",
    )(requested, global_blocks, back, *parts_w)

    rows = [held] + [lax.ppermute(held, "head", partners(head_count, m)) for m in others]
    pieces = []
    for a in rows:
        pieces += [a, lax.ppermute(a, "head", core_pairs)]
    key_grad, value_grad = pl.pallas_call(
        functools.partial(join_kernel, columns_count),
        out_shape=(sds(key_vectors.shape, bf16),) * 2,
        in_specs=[vmem] * len(pieces),
        out_specs=(vmem, vmem),
        scratch_shapes=[pltpu.VMEM((blocks, BLOCK, DH), bf16)] * 2,
        compiler_params=small,
        name="join",
    )(*pieces)
    return query_grad, key_grad, value_grad


def solution(mesh):
    return jax.shard_map(
        body,
        mesh=mesh,
        in_specs=(
            P("seq", "head"),
            P("seq", None),
            P("seq", None),
            P("seq", "head"),
            P("seq", None),
            P(),
        ),
        out_specs=(P("seq", "head"), P("seq", None), P("seq", None)),
        check_vma=False,
    )
```

```python
import functools
import math

import jax
import jax.numpy as jnp
from jax import lax
from jax.experimental import pallas as pl
from jax.experimental.pallas import tpu as pltpu
from jax.sharding import PartitionSpec as P

DH = 128
BLOCK = 128
HALF = BLOCK // 2
R = 3
G = 2
WINDOW = 3
FAR = R + G
LISTED = WINDOW + FAR
MIB = 1024 * 1024
MASKED = -1e30
FACTOR = float(DH) ** -0.5
SCALE = FACTOR * math.log2(math.e)
FOLD = 8
MARKS = 16

NT = (((1,), (1,)), ((), ()))
NN = (((1,), (0,)), ((), ()))
TN = (((0,), (0,)), ((), ()))


def mm(a, b, dims):
    return lax.dot_general(a, b, dims, preferred_element_type=jnp.float32)


def stack_heads(ref, u):
    rows = ref[u * BLOCK : (u + 1) * BLOCK, :]
    return jnp.concatenate(
        [rows[:, h * DH : (h + 1) * DH] for h in range(rows.shape[1] // DH)], axis=0
    )


def fold(x):
    return jnp.sum(x.reshape(x.shape[0] // FOLD, FOLD, x.shape[1]), axis=0)


def panel(k, v, q, g):
    s = mm(k, q, NT)
    dp = mm(v, g, NT)
    top = jnp.max(s, axis=0, keepdims=True) * SCALE
    e = jnp.exp2(s * SCALE - top)
    return top, e, dp, fold(e), fold(e * dp)


def places():
    head_index = lax.axis_index("head")
    return lax.rem(head_index, 2), lax.div(head_index, 2)


def glob_slices(peers):
    rows = 2 * G * HALF
    size = max(MARKS, rows // peers)
    return rows // size, size


def ask_kernel(
    global_blocks, random_blocks, random_ref, k_ref, v_ref, out_ref, low_ref, high_ref, owners, rows, sems
):
    tokens = k_ref.shape[0]
    blocks = tokens // BLOCK
    peers = out_ref.shape[0]
    core, _ = places()
    slices, size = glob_slices(peers)
    edges, copies = [], []

    def begin(group, src, dst):
        group.append(pltpu.make_async_copy(src, dst, sems.at[len(edges) + len(copies)]))
        group[-1].start()

    for j in range(G):
        start = lax.rem(global_blocks[j], blocks) * BLOCK + core * HALF
        start = pl.multiple_of(start, HALF)
        for which, ref in ((0, k_ref), (1, v_ref)):
            at = (2 * j + which) * HALF
            begin(copies, ref.at[pl.ds(start, HALF), :], rows.at[pl.ds(at, HALF), :])
    odd = lax.rem(lax.axis_index("seq"), 2)
    for which, ref in ((0, k_ref), (1, v_ref)):
        for edge_ref, at in ((low_ref, (1 - odd) * (tokens - BLOCK)), (high_ref, odd * (tokens - BLOCK))):
            start = pl.multiple_of(at, BLOCK)
            begin(edges, ref.at[pl.ds(start, BLOCK), :], edge_ref.at[which])
    wanted = random_ref[...]

    def mark(j, carry):
        within = wanted - j * blocks
        mine = jnp.logical_and(within >= 0, within < blocks)
        top = jnp.max(jnp.where(mine, within, -1).astype(jnp.float32))
        out_ref[j, :MARKS, :] = jnp.full((MARKS, DH), top, jnp.float32).astype(jnp.bfloat16)
        return carry

    lax.fori_loop(0, peers, mark, 0, unroll=min(peers, 8))
    for b in range(blocks):
        for r in range(R):
            owners[b * R + r] = lax.div(random_blocks[r, b], blocks)
    for copy in copies:
        copy.wait()
    out_ref[:slices, MARKS:, :] = rows[...].reshape(slices, size, DH)
    if slices < peers:
        out_ref[slices:, MARKS:, :] = jnp.zeros((peers - slices, size, DH), jnp.bfloat16)
    for copy in edges:
        copy.wait()


def serve_kernel(global_blocks, asked_ref, k_ref, v_ref, out_ref, requested_ref, sems):
    blocks = k_ref.shape[0] // BLOCK
    core, _ = places()
    peers = out_ref.shape[0]
    many = min(peers, 8)
    slices, size = glob_slices(peers)

    def copy(j, start, which, ref):
        return pltpu.make_async_copy(
            ref.at[pl.ds(start, HALF), :],
            out_ref.at[j, pl.ds(which * HALF, HALF), :],
            sems.at[j, which],
        )

    def begin(j, carry):
        wanted = jnp.max(asked_ref[j, :MARKS, :].astype(jnp.float32)).astype(jnp.int32)
        requested_ref[j] = wanted
        start = pl.multiple_of(jnp.clip(wanted, 0, blocks - 1) * BLOCK + core * HALF, HALF)
        copy(j, start, 0, k_ref).start()
        copy(j, start, 1, v_ref).start()
        return carry

    lax.fori_loop(0, peers, begin, 0, unroll=many)
    index = jnp.minimum(lax.axis_index("seq"), slices - 1)
    owner = lax.div(global_blocks[lax.div(index * size, 2 * HALF)], blocks)
    out_ref[:, 2 * HALF :, :] = jnp.broadcast_to(
        asked_ref[owner, MARKS:, :][None], (peers, size, DH)
    )

    def end(j, carry):
        copy(j, 0, 0, k_ref).wait()
        copy(j, 0, 1, v_ref).wait()
        return carry

    lax.fori_loop(0, peers, end, 0, unroll=many)


def split_kernel(count, keep_ref, got_ref, out_ref, *send_refs):
    share = out_ref.shape[2]
    _, column = places()
    own = pl.ds(pl.multiple_of(column * share, share), share)
    total = keep_ref[:, :, own, :].astype(jnp.float32) + got_ref[:, :, own, :].astype(jnp.float32)
    out_ref[...] = total.astype(out_ref.dtype)
    for m in range(1, count):
        there = pl.ds(pl.multiple_of((column ^ m) * share, share), share)
        send_refs[m - 1][...] = (
            keep_ref[:, :, there, :].astype(jnp.float32) + got_ref[:, :, there, :].astype(jnp.float32)
        ).astype(jnp.bfloat16)


def terms_kernel(keep_ref, *refs):
    *got_refs, terms_ref, low_ref, high_ref = refs
    peers, _, share, _ = terms_ref.shape
    odd = lax.rem(lax.axis_index("seq"), 2) == 1

    def total(slot, n=1):
        x = keep_ref[slot : slot + n].astype(jnp.float32)
        for ref in got_refs:
            x = x + ref[slot : slot + n].astype(jnp.float32)
        return x.astype(jnp.bfloat16)

    terms_ref[:, :2] = total(0, peers)
    glob = total(peers, G).reshape(1, 2 * G, share, DH)
    terms_ref[:, 2:] = jnp.broadcast_to(glob, (peers, 2 * G, share, DH))
    previous = total(peers + G)[0]
    following = total(peers + G + 1)[0]
    low_ref[...] = jnp.where(odd, previous, following)
    high_ref[...] = jnp.where(odd, following, previous)


def settle_kernel(requested, global_blocks, back_ref, low_ref, high_ref, *refs):
    *got_refs, out_ref, acc = refs
    blocks = out_ref.shape[0]
    peers, _, share, _ = back_ref.shape
    seq_index = lax.axis_index("seq")
    acc[...] = sum(ref[...].astype(jnp.float32) for ref in got_refs)
    at_low, at_high = edge_places(blocks)
    acc[jnp.clip(at_low - 1, 0, blocks - 1)] += low_ref[...].astype(jnp.float32)
    acc[jnp.clip(at_high - 1, 0, blocks - 1)] += high_ref[...].astype(jnp.float32)

    def one(j, carry):
        wanted = requested[j]

        @pl.when(wanted >= 0)
        def _():
            acc[wanted] += back_ref[j, :2].astype(jnp.float32)

        return carry

    lax.fori_loop(0, peers, one, 0)
    for j in range(G):

        @pl.when(lax.div(global_blocks[j], blocks) == seq_index)
        def _():
            rows = back_ref[:, 2 + 2 * j : 4 + 2 * j].astype(jnp.float32)
            acc[lax.rem(global_blocks[j], blocks)] += jnp.sum(rows, axis=0)

    out_ref[...] = acc[...].astype(jnp.bfloat16)


def join_kernel(count, *refs):
    *got_refs, dk_ref, dv_ref, dk, dv = refs
    blocks, _, share, _ = got_refs[0].shape
    core, column = places()
    for m in range(count):
        for c in range(2):
            at = (core ^ c) * HALF + (column ^ m) * share
            rows = pl.ds(pl.multiple_of(at, share), share)
            ref = got_refs[2 * m + c]
            dk[:, rows, :] = ref[:, 0]
            dv[:, rows, :] = ref[:, 1]
    dk_ref[...] = dk[...].reshape(dk_ref.shape)
    dv_ref[...] = dv[...].reshape(dv_ref.shape)


def edge_places(blocks):
    odd = lax.rem(lax.axis_index("seq"), 2)
    return (1 - odd) * (blocks + 1), odd * (blocks + 1)


def fill_window(k_ref, v_ref, low_ref, high_ref, k_all, v_all):
    rows = k_ref.shape[0]
    low, high = (pl.ds(pl.multiple_of(i * BLOCK, BLOCK), BLOCK) for i in edge_places(rows // BLOCK))
    for to, own, which in ((k_all, k_ref, 0), (v_all, v_ref, 1)):
        to[low, :] = low_ref[which]
        to[high, :] = high_ref[which]
        to[BLOCK : BLOCK + rows] = own[...]


def near_kernel(q_ref, g_ref, k_ref, v_ref, low_ref, high_ref, st_ref, k_all, v_all):
    step = pl.program_id(0)
    blocks = k_ref.shape[0] // BLOCK
    seq_index = lax.axis_index("seq")
    per = st_ref.shape[0]

    @pl.when(step == 0)
    def _():
        fill_window(k_ref, v_ref, low_ref, high_ref, k_all, v_all)

    for u in range(per):
        b = step * per + u
        q = stack_heads(q_ref, u)
        g = stack_heads(g_ref, u)
        no_left = jnp.logical_and(seq_index == 0, b == 0)
        no_right = jnp.logical_and(seq_index == lax.axis_size("seq") - 1, b == blocks - 1)
        biases = (jnp.where(no_left, MASKED, 0.0), None, jnp.where(no_right, MASKED, 0.0))
        for w in range(WINDOW):
            rows = pl.ds(pl.multiple_of((b + w) * BLOCK, BLOCK), BLOCK)
            top, _, _, l, d = panel(k_all[rows, :], v_all[rows, :], q, g)
            if biases[w] is not None:
                top = top + biases[w]
            st_ref[u, w : w + 1] = top
            st_ref[u, WINDOW + w : WINDOW + w + 1] = jnp.sum(l, axis=0, keepdims=True)
            st_ref[u, 2 * WINDOW + w : 2 * WINDOW + w + 1] = jnp.sum(d, axis=0, keepdims=True)


def far_kernel(
    owners, q_ref, g_ref, mine_ref, other_ref, st_ref, low_ref, high_ref,
    ds_ref, fd_ref, *refs,
):
    *share_refs, q_all, g_all, k_all, v_all, acc, e_all, dp_all, ds_all, in_sems, out_sems = refs
    blocks = q_ref.shape[0] // BLOCK
    peers = mine_ref.shape[0]
    core, column = places()
    own, opp = pl.ds(core * HALF, HALF), pl.ds((1 - core) * HALF, HALF)
    slices, size = glob_slices(peers)

    def at(b):
        return pl.ds(pl.multiple_of(b * BLOCK, BLOCK), BLOCK)

    def fetch(b, which):
        src, dst = ((q_ref, q_all), (g_ref, g_all))[which]
        return pltpu.make_async_copy(src.at[at(b), :], dst.at[at(b), :], in_sems.at[b, which])

    def put(b):
        return pltpu.make_async_copy(ds_all.at[b], ds_ref.at[b], out_sems.at[b])

    for b in range(blocks):
        fetch(b, 0).start()
        fetch(b, 1).start()
    for to, which in ((k_all, 0), (v_all, 1)):
        rows = slice(which * HALF, (which + 1) * HALF)
        to[:peers, own, :] = mine_ref[:, rows, :]
        to[:peers, opp, :] = other_ref[:, rows, :]
    for i in range(slices):
        unit, offset = divmod(i * size, HALF)
        to = (k_all, v_all)[unit % 2]
        slot = peers + unit // 2
        to[slot, pl.ds(pl.multiple_of(core * HALF + offset, MARKS), size), :] = mine_ref[i, 2 * HALF :, :]
        to[slot, pl.ds(pl.multiple_of((1 - core) * HALF + offset, MARKS), size), :] = other_ref[i, 2 * HALF :, :]
    acc[...] = jnp.zeros_like(acc)

    def heads(ref, b):
        rows = ref[at(b), :]
        return jnp.concatenate(
            [rows[:, h * DH : (h + 1) * DH] for h in range(rows.shape[1] // DH)], axis=0
        )

    def slots_of(b):
        return [owners[b * R + r] for r in range(R)] + [peers + j for j in range(G)]

    def work(new, new_slot, old, old_slot, stats):
        if new is not None:
            fetch(new, 0).wait()
            fetch(new, 1).wait()
            q1, g1, slots1 = heads(q_all, new), heads(g_all, new), slots_of(new)
        if old is not None:
            q2, g2, slots2 = heads(q_all, old), heads(g_all, old), slots_of(old)
        tops, ls, dd = [], [], []
        for i in range(FAR):
            rows = slice(i * BLOCK, (i + 1) * BLOCK)
            if new is not None:
                s = mm(k_all[slots1[i]], q1, NT)
                dp = mm(v_all[slots1[i]], g1, NT)
            if old is not None:
                p = e_all[old_slot, rows] * stats[i]
                ds = (p * (dp_all[old_slot, rows] - stats[FAR])).astype(jnp.bfloat16)
                ds_all[old, rows] = ds
                acc[slots2[i], 0] += mm(ds, q2, NN)
                acc[slots2[i], 1] += mm(p.astype(jnp.bfloat16), g2, NN)
            if new is not None:
                top = jnp.max(s, axis=0, keepdims=True) * SCALE
                e = jnp.exp2(s * SCALE - top)
                e_all[new_slot, rows] = e
                dp_all[new_slot, rows] = dp
                tops.append(top)
                ls.append(fold(e))
                dd.append(fold(e * dp))
        if old is not None:
            put(old).start()
        if new is None:
            return None
        near = [[st_ref[new, i * WINDOW + w : i * WINDOW + w + 1] for w in range(WINDOW)] for i in range(3)]
        top = functools.reduce(jnp.maximum, near[0] + tops)
        near_weight = [jnp.exp2(t - top) for t in near[0]]
        weight = [jnp.exp2(t - top) for t in tops]
        l = jnp.sum(sum(w * x for w, x in zip(weight, ls)), axis=0, keepdims=True)
        d = jnp.sum(sum(w * x for w, x in zip(weight, dd)), axis=0, keepdims=True)
        l = l + sum(w * x for w, x in zip(near_weight, near[1]))
        d = d + sum(w * x for w, x in zip(near_weight, near[2]))
        inv = 1.0 / l
        delta = d * inv
        for w in range(WINDOW):
            fd_ref[new, w : w + 1] = near[0][w]
            fd_ref[new, WINDOW + w : WINDOW + w + 1] = near_weight[w] * inv
        fd_ref[new, 2 * WINDOW : 2 * WINDOW + 1] = delta
        return tuple(w * inv for w in weight) + (delta,)

    def pair(t, stats):
        stats = work(2 * t + 1, 1, 2 * t, 0, stats)
        return work(2 * t + 2, 0, 2 * t + 1, 1, stats)

    stats = work(0, 0, None, None, None)
    stats = lax.fori_loop(0, blocks // 2 - 1, pair, stats)
    stats = work(blocks - 1, 1, blocks - 2, 0, stats)
    work(None, None, blocks - 1, 1, stats)

    for slot, w, b, swap in ((peers + G, 0, 0, 1), (peers + G + 1, WINDOW - 1, blocks - 1, 0)):
        odd = lax.rem(lax.axis_index("seq"), 2) == swap
        q, g = heads(q_all, b), heads(g_all, b)
        s = mm(jnp.where(odd, low_ref[0], high_ref[0]), q, NT)
        dp = mm(jnp.where(odd, low_ref[1], high_ref[1]), g, NT)
        p = jnp.exp2(s * SCALE - jnp.max(s, axis=0, keepdims=True) * SCALE)
        p = p * fd_ref[b, WINDOW + w : WINDOW + w + 1]
        ds = (p * (dp - fd_ref[b, 2 * WINDOW : 2 * WINDOW + 1])).astype(jnp.bfloat16)
        acc[slot, 0] = mm(ds, q, NN)
        acc[slot, 1] = mm(p.astype(jnp.bfloat16), g, NN)

    share = share_refs[0].shape[2]
    for m, ref in enumerate(share_refs):
        start = (core ^ (m & 1)) * HALF + (column ^ (m >> 1)) * share
        rows = pl.ds(pl.multiple_of(start, share), share)
        for which, f in ((0, FACTOR), (1, 1.0)):
            ref[:, which] = (acc[:, which, rows, :] * f).astype(ref.dtype)
    for b in range(blocks):
        put(b).wait()


def close_kernel(
    q_ref, g_ref, k_ref, v_ref, low_ref, high_ref, fd_ref, ds_ref, keep_ref, send_ref, k_all, v_all, acc
):
    step = pl.program_id(0)
    per = fd_ref.shape[0]
    core, _ = places()
    own, opp = pl.ds(core * HALF, HALF), pl.ds((1 - core) * HALF, HALF)

    @pl.when(step == 0)
    def _():
        fill_window(k_ref, v_ref, low_ref, high_ref, k_all, v_all)
        acc[...] = jnp.zeros_like(acc)

    for u in range(per):
        b = step * per + u
        q = stack_heads(q_ref, u)
        g = stack_heads(g_ref, u)
        delta = fd_ref[u, 2 * WINDOW : 2 * WINDOW + 1]
        ds, pb = [], []
        for w in range(WINDOW):
            rows = pl.ds(pl.multiple_of((b + w) * BLOCK, BLOCK), BLOCK)
            s = mm(k_all[rows, :], q, NT)
            dp = mm(v_all[rows, :], g, NT)
            top = fd_ref[u, w : w + 1]
            top = jnp.where(top < MASKED / 2, 0.0, top)
            p = jnp.exp2(s * SCALE - top) * fd_ref[u, WINDOW + w : WINDOW + w + 1]
            ds.append((p * (dp - delta)).astype(jnp.bfloat16))
            pb.append(p.astype(jnp.bfloat16))
        ds = jnp.concatenate(ds, axis=0)
        pb = jnp.concatenate(pb, axis=0)
        ds_ref[u] = ds
        shape = (WINDOW, BLOCK, DH)
        acc[pl.ds(b, WINDOW), 0] += mm(ds, q, NN).reshape(shape)
        acc[pl.ds(b, WINDOW), 1] += mm(pb, g, NN).reshape(shape)

    @pl.when(step == pl.num_programs(0) - 1)
    def _():
        for which, f in ((0, FACTOR), (1, 1.0)):
            keep_ref[:, which] = (acc[1:-1, which, own, :] * f).astype(keep_ref.dtype)
            send_ref[:, which] = (acc[1:-1, which, opp, :] * f).astype(jnp.bfloat16)


def queries_kernel(
    owners, k_ref, low_ref, high_ref, mine_ref, other_ref, dsw_ref, dsf_ref, dq_ref, k_all, kt_all
):
    blocks = k_ref.shape[0] // BLOCK
    peers = mine_ref.shape[0]
    per = dsw_ref.shape[0]
    core, _ = places()
    step = pl.program_id(0)
    first_random = blocks + 2
    first_global = first_random + peers
    slices, size = glob_slices(peers)

    @pl.when(step == 0)
    def _():
        at_low, at_high = edge_places(blocks)
        k_all[at_low] = low_ref[0]
        k_all[at_high] = high_ref[0]
        k_all[1 : blocks + 1] = k_ref[...].reshape(blocks, BLOCK, DH)
        for ref, c in ((mine_ref, core), (other_ref, 1 - core)):
            k_all[first_random:first_global, pl.ds(c * HALF, HALF), :] = ref[:, :HALF, :]
            for i in range(slices):
                unit, offset = divmod(i * size, HALF)
                if unit % 2 == 0:
                    rows = pl.ds(pl.multiple_of(c * HALF + offset, MARKS), size)
                    k_all[first_global + unit // 2, rows, :] = ref[i, 2 * HALF :, :]

        def turn(j, carry):
            kt_all[j] = k_all[j].T
            return carry

        lax.fori_loop(0, first_global + G, turn, 0, unroll=4)

    for u in range(per):
        b = step * per + u
        panels = [b + w for w in range(WINDOW)]
        panels += [first_random + owners[b * R + r] for r in range(R)]
        panels += [first_global + j for j in range(G)]
        turned = [kt_all[i] for i in panels]
        dqt = mm(jnp.concatenate(turned[:WINDOW], axis=1), dsw_ref[u], NN)
        dqt = (dqt + mm(jnp.concatenate(turned[WINDOW:], axis=1), dsf_ref[u], NN)) * FACTOR
        for h in range(dq_ref.shape[1] // DH):
            dq_ref[u * BLOCK : (u + 1) * BLOCK, h * DH : (h + 1) * DH] = (
                dqt[:, h * BLOCK : (h + 1) * BLOCK].T.astype(jnp.bfloat16)
            )


def whole(a):
    return pl.BlockSpec(a.shape, lambda i, *_: (0,) * len(a.shape))


def per_block(per, *rest):
    return pl.BlockSpec((per,) + rest, lambda i, *_: (i,) + (0,) * len(rest))


def partners(size, stride):
    return [(i, i ^ stride) for i in range(size)]


def body(query_vectors, key_vectors, value_vectors, output_grad, random_blocks, global_blocks):
    seq_count = lax.axis_size("seq")
    head_count = lax.axis_size("head")
    rows_dev, columns = query_vectors.shape
    blocks = rows_dev // BLOCK
    per = math.gcd(blocks, 4)
    steps = blocks // per
    lanes = columns // DH * BLOCK
    bf16 = jnp.bfloat16
    f32 = jnp.float32
    sds = jax.ShapeDtypeStruct
    core_pairs = partners(head_count, 1)
    limit = (16 + seq_count // 2) * MIB
    params = pltpu.CompilerParams(dimension_semantics=("arbitrary",), vmem_limit_bytes=limit)
    unit = 2 * blocks * lanes * BLOCK * DH

    vmem = pl.BlockSpec(memory_space=pltpu.VMEM)
    smem = pl.BlockSpec(memory_space=pltpu.SMEM)
    hbm = pl.BlockSpec(memory_space=pltpu.HBM)
    small = pltpu.CompilerParams(vmem_limit_bytes=limit)
    large = pltpu.CompilerParams(vmem_limit_bytes=60 * MIB)
    share = BLOCK // head_count
    columns_count = head_count // 2

    edge = (2, BLOCK, DH)
    _, size = glob_slices(seq_count)
    asking, to_low, to_high, owners = pl.pallas_call(
        ask_kernel,
        out_shape=(
            sds((seq_count, MARKS + size, DH), bf16),
            sds(edge, bf16),
            sds(edge, bf16),
            sds((blocks * R,), jnp.int32),
        ),
        in_specs=[smem, smem, vmem, hbm, hbm],
        out_specs=(vmem, vmem, vmem, smem),
        scratch_shapes=[
            pltpu.VMEM((2 * G * HALF, DH), bf16),
            pltpu.SemaphoreType.DMA((2 * G + 4,)),
        ],
        compiler_params=large,
        name="ask",
    )(global_blocks, random_blocks.T, random_blocks.T, key_vectors, value_vectors)
    asked = lax.all_to_all(asking, "seq", split_axis=0, concat_axis=0, tiled=True)

    low_pairs = [(i, i ^ 1) for i in range(seq_count)]
    high_pairs = [(i, i + 1 if i % 2 else i - 1) for i in range(1, seq_count - 1)]
    low = lax.ppermute(to_low, "seq", low_pairs)
    high = lax.ppermute(to_high, "seq", high_pairs)
    asked, low, high = lax.optimization_barrier((asked, low, high))

    served, requested = pl.pallas_call(
        serve_kernel,
        out_shape=(sds((seq_count, 2 * HALF + size, DH), bf16), sds((seq_count,), jnp.int32)),
        in_specs=[smem, vmem, hbm, hbm],
        out_specs=(vmem, smem),
        scratch_shapes=[pltpu.SemaphoreType.DMA((seq_count, 2))],
        compiler_params=large,
        name="serve",
    )(global_blocks, asked, key_vectors, value_vectors)
    mine = lax.all_to_all(served, "seq", split_axis=0, concat_axis=0, tiled=True)

    rows_spec = pl.BlockSpec((per * BLOCK, columns), lambda i, *_: (i, 0))
    st_spec = per_block(per, 2 * FOLD, lanes)
    fd_spec = per_block(per, FOLD, lanes)
    nearby = (key_vectors, value_vectors, low, high)
    window_scratch = [pltpu.VMEM(((blocks + 2) * BLOCK, DH), bf16)] * 2
    st = pl.pallas_call(
        near_kernel,
        out_shape=sds((blocks, 2 * FOLD, lanes), f32),
        grid=(steps,),
        in_specs=[rows_spec, rows_spec] + [whole(a) for a in nearby],
        out_specs=st_spec,
        scratch_shapes=window_scratch,
        compiler_params=large,
        cost_estimate=pl.CostEstimate(
            flops=2 * WINDOW * unit, bytes_accessed=4 * MIB, transcendentals=blocks * lanes * WINDOW * BLOCK
        ),
        name="near",
    )(query_vectors, output_grad, *nearby)
    mine, st = lax.optimization_barrier((mine, st))
    other = lax.ppermute(mine, "head", core_pairs)

    slots = seq_count + G + 2
    piece = (slots, 2, share, DH)
    dsf, fd, *pieces = pl.pallas_call(
        far_kernel,
        out_shape=(
            sds((blocks, FAR * BLOCK, lanes), bf16),
            sds((blocks, FOLD, lanes), f32),
        )
        + (sds(piece, bf16),) * head_count,
        in_specs=[smem, hbm, hbm] + [vmem] * 5,
        out_specs=(hbm, vmem) + (vmem,) * head_count,
        scratch_shapes=[pltpu.VMEM(query_vectors.shape, bf16)] * 2
        + [pltpu.VMEM((seq_count + G, BLOCK, DH), bf16)] * 2
        + [pltpu.VMEM((slots, 2, BLOCK, DH), f32)]
        + [pltpu.VMEM((2, FAR * BLOCK, lanes), f32)] * 2
        + [
            pltpu.VMEM((blocks, FAR * BLOCK, lanes), bf16),
            pltpu.SemaphoreType.DMA((blocks, 2)),
            pltpu.SemaphoreType.DMA((blocks,)),
        ],
        compiler_params=large,
        cost_estimate=pl.CostEstimate(
            flops=5 * FAR * unit, bytes_accessed=8 * MIB, transcendentals=blocks * lanes * FAR * BLOCK
        ),
        name="far",
    )(owners, query_vectors, output_grad, mine, other, st, low, high)

    piece_w = (blocks, 2, HALF, DH)
    near_spec = per_block(per, WINDOW * BLOCK, lanes)
    far_spec = per_block(per, FAR * BLOCK, lanes)
    dsw, keep_w, send_w = pl.pallas_call(
        close_kernel,
        out_shape=(sds((blocks, WINDOW * BLOCK, lanes), bf16), sds(piece_w, bf16), sds(piece_w, bf16)),
        grid=(steps,),
        in_specs=[rows_spec, rows_spec] + [whole(a) for a in nearby] + [fd_spec],
        out_specs=(near_spec, whole(sds(piece_w, bf16)), whole(sds(piece_w, bf16))),
        scratch_shapes=window_scratch + [pltpu.VMEM((blocks + 2, 2, BLOCK, DH), f32)],
        compiler_params=large,
        cost_estimate=pl.CostEstimate(flops=4 * WINDOW * unit, bytes_accessed=8 * MIB, transcendentals=0),
        name="close",
    )(query_vectors, output_grad, *nearby, fd)

    others = [m << 1 for m in range(1, columns_count)]

    def reduced(kept, sent, name, dtype):
        got = lax.ppermute(sent, "head", core_pairs)
        part = (kept.shape[0], 2, share, DH)
        home, *away = pl.pallas_call(
            functools.partial(split_kernel, columns_count),
            out_shape=(sds(part, dtype),) + (sds(part, bf16),) * len(others),
            in_specs=[vmem, vmem],
            out_specs=(vmem,) * (1 + len(others)),
            compiler_params=small,
            name=name,
        )(kept, got)
        return [home] + [
            lax.ppermute(a, "head", partners(head_count, m)) for a, m in zip(away, others)
        ]

    parts = pieces[:1] + [
        lax.ppermute(pieces[m], "head", partners(head_count, m)) for m in range(1, head_count)
    ]
    parts[-1], send_w = lax.optimization_barrier((parts[-1], send_w))
    terms, to_low, to_high = pl.pallas_call(
        terms_kernel,
        out_shape=(
            sds((seq_count, 2 + 2 * G, share, DH), bf16),
            sds((2, share, DH), bf16),
            sds((2, share, DH), bf16),
        ),
        in_specs=[vmem] * len(parts),
        out_specs=(vmem,) * 3,
        compiler_params=small,
        name="terms",
    )(*parts)
    parts_w = reduced(keep_w, send_w, "split_close", bf16)
    dsw, to_low = lax.optimization_barrier((dsw, to_low))
    query_grad = pl.pallas_call(
        queries_kernel,
        out_shape=sds(query_vectors.shape, bf16),
        grid_spec=pltpu.PrefetchScalarGridSpec(
            num_scalar_prefetch=1,
            grid=(steps,),
            in_specs=[whole(a) for a in (key_vectors, low, high, mine, other)] + [near_spec, far_spec],
            out_specs=rows_spec,
            scratch_shapes=[pltpu.VMEM((blocks + 2 + seq_count + G, BLOCK, DH), bf16)] * 2,
        ),
        compiler_params=large,
        cost_estimate=pl.CostEstimate(flops=LISTED * unit, bytes_accessed=8 * MIB, transcendentals=0),
        name="queries",
    )(owners, key_vectors, low, high, mine, other, dsw, dsf)
    back = lax.all_to_all(terms, "seq", split_axis=0, concat_axis=0, tiled=True)
    from_low = lax.ppermute(to_low, "seq", low_pairs)
    from_high = lax.ppermute(to_high, "seq", high_pairs)
    back, query_grad = lax.optimization_barrier((back, query_grad))
    held = pl.pallas_call(
        settle_kernel,
        out_shape=sds((blocks, 2, share, DH), bf16),
        in_specs=[smem, smem] + [vmem] * (3 + len(parts_w)),
        out_specs=vmem,
        scratch_shapes=[pltpu.VMEM((blocks, 2, share, DH), f32)],
        compiler_params=small,
        name="settle",
    )(requested, global_blocks, back, from_low, from_high, *parts_w)

    rows = [held] + [lax.ppermute(held, "head", partners(head_count, m)) for m in others]
    pieces = []
    for a in rows:
        pieces += [a, lax.ppermute(a, "head", core_pairs)]
    key_grad, value_grad = pl.pallas_call(
        functools.partial(join_kernel, columns_count),
        out_shape=(sds(key_vectors.shape, bf16),) * 2,
        in_specs=[vmem] * len(pieces),
        out_specs=(vmem, vmem),
        scratch_shapes=[pltpu.VMEM((blocks, BLOCK, DH), bf16)] * 2,
        compiler_params=small,
        name="join",
    )(*pieces)
    return query_grad, key_grad, value_grad


def solution(mesh):
    return jax.shard_map(
        body,
        mesh=mesh,
        in_specs=(
            P("seq", "head"),
            P("seq", None),
            P("seq", None),
            P("seq", "head"),
            P("seq", None),
            P(),
        ),
        out_specs=(P("seq", "head"), P("seq", None), P("seq", None)),
        check_vma=False,
    )
```

```python
import functools
import math

import jax
import jax.numpy as jnp
from jax import lax
from jax.experimental import pallas as pl
from jax.experimental.pallas import tpu as pltpu
from jax.sharding import PartitionSpec as P

DH = 128
BLOCK = 128
HALF = BLOCK // 2
R = 3
G = 2
WINDOW = 3
FAR = R + G
LISTED = WINDOW + FAR
MIB = 1024 * 1024
MASKED = -1e30
FACTOR = float(DH) ** -0.5
SCALE = FACTOR * math.log2(math.e)
FOLD = 8
MARKS = 16

NT = (((1,), (1,)), ((), ()))
NN = (((1,), (0,)), ((), ()))
TN = (((0,), (0,)), ((), ()))


def mm(a, b, dims):
    return lax.dot_general(a, b, dims, preferred_element_type=jnp.float32)


def stack_heads(ref, u):
    rows = ref[u * BLOCK : (u + 1) * BLOCK, :]
    return jnp.concatenate(
        [rows[:, h * DH : (h + 1) * DH] for h in range(rows.shape[1] // DH)], axis=0
    )


def fold(x):
    return jnp.sum(x.reshape(x.shape[0] // FOLD, FOLD, x.shape[1]), axis=0)


def panel(k, v, q, g):
    s = mm(k, q, NT)
    dp = mm(v, g, NT)
    top = jnp.max(s, axis=0, keepdims=True) * SCALE
    e = jnp.exp2(s * SCALE - top)
    return top, e, dp, fold(e), fold(e * dp)


def places():
    head_index = lax.axis_index("head")
    return lax.rem(head_index, 2), lax.div(head_index, 2)


def glob_slices(peers):
    rows = 2 * G * HALF
    size = max(MARKS, rows // peers)
    return rows // size, size


def ask_kernel(
    global_blocks, random_blocks, random_ref, k_ref, v_ref, out_ref, low_ref, high_ref, owners, rows, sems
):
    tokens = k_ref.shape[0]
    blocks = tokens // BLOCK
    peers = out_ref.shape[0]
    core, _ = places()
    slices, size = glob_slices(peers)
    edges, copies = [], []

    def begin(group, src, dst):
        group.append(pltpu.make_async_copy(src, dst, sems.at[len(edges) + len(copies)]))
        group[-1].start()

    for j in range(G):
        start = lax.rem(global_blocks[j], blocks) * BLOCK + core * HALF
        start = pl.multiple_of(start, HALF)
        for which, ref in ((0, k_ref), (1, v_ref)):
            at = (2 * j + which) * HALF
            begin(copies, ref.at[pl.ds(start, HALF), :], rows.at[pl.ds(at, HALF), :])
    odd = lax.rem(lax.axis_index("seq"), 2)
    for which, ref in ((0, k_ref), (1, v_ref)):
        for edge_ref, at in ((low_ref, (1 - odd) * (tokens - BLOCK)), (high_ref, odd * (tokens - BLOCK))):
            start = pl.multiple_of(at, BLOCK)
            begin(edges, ref.at[pl.ds(start, BLOCK), :], edge_ref.at[which])
    wanted = random_ref[...]

    def mark(j, carry):
        within = wanted - j * blocks
        mine = jnp.logical_and(within >= 0, within < blocks)
        top = jnp.max(jnp.where(mine, within, -1).astype(jnp.float32))
        out_ref[j, :MARKS, :] = jnp.full((MARKS, DH), top, jnp.float32).astype(jnp.bfloat16)
        return carry

    lax.fori_loop(0, peers, mark, 0, unroll=min(peers, 8))
    for b in range(blocks):
        for r in range(R):
            owners[b * R + r] = lax.div(random_blocks[r, b], blocks)
    for copy in copies:
        copy.wait()
    out_ref[:slices, MARKS:, :] = rows[...].reshape(slices, size, DH)
    if slices < peers:
        out_ref[slices:, MARKS:, :] = jnp.zeros((peers - slices, size, DH), jnp.bfloat16)
    for copy in edges:
        copy.wait()


def serve_kernel(global_blocks, asked_ref, k_ref, v_ref, out_ref, requested_ref, sems):
    blocks = k_ref.shape[0] // BLOCK
    core, _ = places()
    peers = out_ref.shape[0]
    many = min(peers, 8)
    slices, size = glob_slices(peers)

    def copy(j, start, which, ref):
        return pltpu.make_async_copy(
            ref.at[pl.ds(start, HALF), :],
            out_ref.at[j, pl.ds(which * HALF, HALF), :],
            sems.at[j, which],
        )

    def begin(j, carry):
        wanted = jnp.max(asked_ref[j, :MARKS, :].astype(jnp.float32)).astype(jnp.int32)
        requested_ref[j] = wanted
        start = pl.multiple_of(jnp.clip(wanted, 0, blocks - 1) * BLOCK + core * HALF, HALF)
        copy(j, start, 0, k_ref).start()
        copy(j, start, 1, v_ref).start()
        return carry

    lax.fori_loop(0, peers, begin, 0, unroll=many)
    index = jnp.minimum(lax.axis_index("seq"), slices - 1)
    owner = lax.div(global_blocks[lax.div(index * size, 2 * HALF)], blocks)
    out_ref[:, 2 * HALF :, :] = jnp.broadcast_to(
        asked_ref[owner, MARKS:, :][None], (peers, size, DH)
    )

    def end(j, carry):
        copy(j, 0, 0, k_ref).wait()
        copy(j, 0, 1, v_ref).wait()
        return carry

    lax.fori_loop(0, peers, end, 0, unroll=many)


def split_kernel(count, keep_ref, got_ref, out_ref, *send_refs):
    share = out_ref.shape[2]
    _, column = places()
    own = pl.ds(pl.multiple_of(column * share, share), share)
    total = keep_ref[:, :, own, :].astype(jnp.float32) + got_ref[:, :, own, :].astype(jnp.float32)
    out_ref[...] = total.astype(out_ref.dtype)
    for m in range(1, count):
        there = pl.ds(pl.multiple_of((column ^ m) * share, share), share)
        send_refs[m - 1][...] = (
            keep_ref[:, :, there, :].astype(jnp.float32) + got_ref[:, :, there, :].astype(jnp.float32)
        ).astype(jnp.bfloat16)


def terms_kernel(keep_ref, *refs):
    *got_refs, terms_ref, low_ref, high_ref = refs
    peers, _, share, _ = terms_ref.shape
    odd = lax.rem(lax.axis_index("seq"), 2) == 1

    def total(slot, n=1):
        x = keep_ref[slot : slot + n].astype(jnp.float32)
        for ref in got_refs:
            x = x + ref[slot : slot + n].astype(jnp.float32)
        return x.astype(jnp.bfloat16)

    terms_ref[:, :2] = total(0, peers)
    glob = total(peers, G).reshape(1, 2 * G, share, DH)
    terms_ref[:, 2:] = jnp.broadcast_to(glob, (peers, 2 * G, share, DH))
    previous = total(peers + G)[0]
    following = total(peers + G + 1)[0]
    low_ref[...] = jnp.where(odd, previous, following)
    high_ref[...] = jnp.where(odd, following, previous)


def settle_kernel(requested, global_blocks, back_ref, low_ref, high_ref, *refs):
    *got_refs, out_ref, acc = refs
    blocks = out_ref.shape[0]
    peers, _, share, _ = back_ref.shape
    seq_index = lax.axis_index("seq")
    acc[...] = sum(ref[...].astype(jnp.float32) for ref in got_refs)
    at_low, at_high = edge_places(blocks)
    acc[jnp.clip(at_low - 1, 0, blocks - 1)] += low_ref[...].astype(jnp.float32)
    acc[jnp.clip(at_high - 1, 0, blocks - 1)] += high_ref[...].astype(jnp.float32)

    def one(j, carry):
        wanted = requested[j]

        @pl.when(wanted >= 0)
        def _():
            acc[wanted] += back_ref[j, :2].astype(jnp.float32)

        return carry

    lax.fori_loop(0, peers, one, 0)
    for j in range(G):

        @pl.when(lax.div(global_blocks[j], blocks) == seq_index)
        def _():
            rows = back_ref[:, 2 + 2 * j : 4 + 2 * j].astype(jnp.float32)
            acc[lax.rem(global_blocks[j], blocks)] += jnp.sum(rows, axis=0)

    out_ref[...] = acc[...].astype(jnp.bfloat16)


def join_kernel(count, *refs):
    *got_refs, dk_ref, dv_ref, dk, dv = refs
    blocks, _, share, _ = got_refs[0].shape
    core, column = places()
    for m in range(count):
        for c in range(2):
            at = (core ^ c) * HALF + (column ^ m) * share
            rows = pl.ds(pl.multiple_of(at, share), share)
            ref = got_refs[2 * m + c]
            dk[:, rows, :] = ref[:, 0]
            dv[:, rows, :] = ref[:, 1]
    dk_ref[...] = dk[...].reshape(dk_ref.shape)
    dv_ref[...] = dv[...].reshape(dv_ref.shape)


def edge_places(blocks):
    odd = lax.rem(lax.axis_index("seq"), 2)
    return (1 - odd) * (blocks + 1), odd * (blocks + 1)


def fill_window(k_ref, v_ref, low_ref, high_ref, k_all, v_all):
    rows = k_ref.shape[0]
    low, high = (pl.ds(pl.multiple_of(i * BLOCK, BLOCK), BLOCK) for i in edge_places(rows // BLOCK))
    for to, own, which in ((k_all, k_ref, 0), (v_all, v_ref, 1)):
        to[low, :] = low_ref[which]
        to[high, :] = high_ref[which]
        to[BLOCK : BLOCK + rows] = own[...]


def near_kernel(q_ref, g_ref, k_ref, v_ref, low_ref, high_ref, st_ref, k_all, v_all):
    step = pl.program_id(0)
    blocks = k_ref.shape[0] // BLOCK
    seq_index = lax.axis_index("seq")
    per = st_ref.shape[0]

    @pl.when(step == 0)
    def _():
        fill_window(k_ref, v_ref, low_ref, high_ref, k_all, v_all)

    for u in range(per):
        b = step * per + u
        q = stack_heads(q_ref, u)
        g = stack_heads(g_ref, u)
        no_left = jnp.logical_and(seq_index == 0, b == 0)
        no_right = jnp.logical_and(seq_index == lax.axis_size("seq") - 1, b == blocks - 1)
        biases = (jnp.where(no_left, MASKED, 0.0), None, jnp.where(no_right, MASKED, 0.0))
        for w in range(WINDOW):
            rows = pl.ds(pl.multiple_of((b + w) * BLOCK, BLOCK), BLOCK)
            top, _, _, l, d = panel(k_all[rows, :], v_all[rows, :], q, g)
            if biases[w] is not None:
                top = top + biases[w]
            st_ref[u, w : w + 1] = top
            st_ref[u, WINDOW + w : WINDOW + w + 1] = jnp.sum(l, axis=0, keepdims=True)
            st_ref[u, 2 * WINDOW + w : 2 * WINDOW + w + 1] = jnp.sum(d, axis=0, keepdims=True)


def far_kernel(
    owners, q_ref, g_ref, mine_ref, other_ref, st_ref, low_ref, high_ref,
    ds_ref, fd_ref, *refs,
):
    *share_refs, q_all, g_all, k_all, v_all, acc, e_all, dp_all, ds_all, in_sems, out_sems = refs
    blocks = q_ref.shape[0] // BLOCK
    peers = mine_ref.shape[0]
    core, column = places()
    own, opp = pl.ds(core * HALF, HALF), pl.ds((1 - core) * HALF, HALF)
    slices, size = glob_slices(peers)

    def at(b):
        return pl.ds(pl.multiple_of(b * BLOCK, BLOCK), BLOCK)

    def fetch(b, which):
        src, dst = ((q_ref, q_all), (g_ref, g_all))[which]
        return pltpu.make_async_copy(src.at[at(b), :], dst.at[at(b), :], in_sems.at[b, which])

    def put(b):
        return pltpu.make_async_copy(ds_all.at[b], ds_ref.at[b], out_sems.at[b])

    for b in range(blocks):
        fetch(b, 0).start()
        fetch(b, 1).start()
    for to, which in ((k_all, 0), (v_all, 1)):
        rows = slice(which * HALF, (which + 1) * HALF)
        to[:peers, own, :] = mine_ref[:, rows, :]
        to[:peers, opp, :] = other_ref[:, rows, :]
    for i in range(slices):
        unit, offset = divmod(i * size, HALF)
        to = (k_all, v_all)[unit % 2]
        slot = peers + unit // 2
        to[slot, pl.ds(pl.multiple_of(core * HALF + offset, MARKS), size), :] = mine_ref[i, 2 * HALF :, :]
        to[slot, pl.ds(pl.multiple_of((1 - core) * HALF + offset, MARKS), size), :] = other_ref[i, 2 * HALF :, :]
    acc[...] = jnp.zeros_like(acc)

    def heads(ref, b):
        rows = ref[at(b), :]
        return jnp.concatenate(
            [rows[:, h * DH : (h + 1) * DH] for h in range(rows.shape[1] // DH)], axis=0
        )

    def slots_of(b):
        return [owners[b * R + r] for r in range(R)] + [peers + j for j in range(G)]

    def work(new, new_slot, old, old_slot, stats):
        if new is not None:
            fetch(new, 0).wait()
            fetch(new, 1).wait()
            q1, g1, slots1 = heads(q_all, new), heads(g_all, new), slots_of(new)
        if old is not None:
            q2, g2, slots2 = heads(q_all, old), heads(g_all, old), slots_of(old)
        tops, ls, dd = [], [], []

        def dots(i):
            return mm(k_all[slots1[i]], q1, NT), mm(v_all[slots1[i]], g1, NT)

        if new is not None:
            ready = dots(0)
        for i in range(FAR):
            rows = slice(i * BLOCK, (i + 1) * BLOCK)
            if new is not None:
                s, dp = ready
                if i + 1 < FAR:
                    ready = dots(i + 1)
            if old is not None:
                p = e_all[old_slot, rows] * stats[i]
                ds = (p * (dp_all[old_slot, rows] - stats[FAR])).astype(jnp.bfloat16)
                ds_all[old, rows] = ds
            if new is not None:
                top = jnp.max(s, axis=0, keepdims=True) * SCALE
                e = jnp.exp2(s * SCALE - top)
                e_all[new_slot, rows] = e
                dp_all[new_slot, rows] = dp
                tops.append(top)
                ls.append(fold(e))
                dd.append(fold(e * dp))
            if old is not None:
                acc[slots2[i], 0] += mm(ds, q2, NN)
                acc[slots2[i], 1] += mm(p.astype(jnp.bfloat16), g2, NN)
        if old is not None:
            put(old).start()
        if new is None:
            return None
        near = [[st_ref[new, i * WINDOW + w : i * WINDOW + w + 1] for w in range(WINDOW)] for i in range(3)]
        top = functools.reduce(jnp.maximum, near[0] + tops)
        near_weight = [jnp.exp2(t - top) for t in near[0]]
        weight = [jnp.exp2(t - top) for t in tops]
        l = jnp.sum(sum(w * x for w, x in zip(weight, ls)), axis=0, keepdims=True)
        d = jnp.sum(sum(w * x for w, x in zip(weight, dd)), axis=0, keepdims=True)
        l = l + sum(w * x for w, x in zip(near_weight, near[1]))
        d = d + sum(w * x for w, x in zip(near_weight, near[2]))
        inv = 1.0 / l
        delta = d * inv
        for w in range(WINDOW):
            fd_ref[new, w : w + 1] = near[0][w]
            fd_ref[new, WINDOW + w : WINDOW + w + 1] = near_weight[w] * inv
        fd_ref[new, 2 * WINDOW : 2 * WINDOW + 1] = delta
        return tuple(w * inv for w in weight) + (delta,)

    turn = math.gcd(blocks, 4)

    def several(t, stats, last=False):
        for j in range(turn - last):
            b = t * turn + j
            stats = work(b + 1, (j + 1) % 2, b, j % 2, stats)
        return stats

    stats = work(0, 0, None, None, None)
    stats = lax.fori_loop(0, blocks // turn - 1, several, stats)
    stats = several(blocks // turn - 1, stats, True)
    work(None, None, blocks - 1, 1, stats)

    for slot, w, b, swap in ((peers + G, 0, 0, 1), (peers + G + 1, WINDOW - 1, blocks - 1, 0)):
        odd = lax.rem(lax.axis_index("seq"), 2) == swap
        q, g = heads(q_all, b), heads(g_all, b)
        s = mm(jnp.where(odd, low_ref[0], high_ref[0]), q, NT)
        dp = mm(jnp.where(odd, low_ref[1], high_ref[1]), g, NT)
        p = jnp.exp2(s * SCALE - jnp.max(s, axis=0, keepdims=True) * SCALE)
        p = p * fd_ref[b, WINDOW + w : WINDOW + w + 1]
        ds = (p * (dp - fd_ref[b, 2 * WINDOW : 2 * WINDOW + 1])).astype(jnp.bfloat16)
        acc[slot, 0] = mm(ds, q, NN)
        acc[slot, 1] = mm(p.astype(jnp.bfloat16), g, NN)

    share = share_refs[0].shape[2]
    for m, ref in enumerate(share_refs):
        start = (core ^ (m & 1)) * HALF + (column ^ (m >> 1)) * share
        rows = pl.ds(pl.multiple_of(start, share), share)
        for which, f in ((0, FACTOR), (1, 1.0)):
            ref[:, which] = (acc[:, which, rows, :] * f).astype(ref.dtype)
    for b in range(blocks):
        put(b).wait()


def close_kernel(
    q_ref, g_ref, k_ref, v_ref, low_ref, high_ref, fd_ref, ds_ref, keep_ref, send_ref, k_all, v_all, acc
):
    step = pl.program_id(0)
    per = fd_ref.shape[0]
    core, _ = places()
    own, opp = pl.ds(core * HALF, HALF), pl.ds((1 - core) * HALF, HALF)

    @pl.when(step == 0)
    def _():
        fill_window(k_ref, v_ref, low_ref, high_ref, k_all, v_all)
        acc[...] = jnp.zeros_like(acc)

    for u in range(per):
        b = step * per + u
        q = stack_heads(q_ref, u)
        g = stack_heads(g_ref, u)
        delta = fd_ref[u, 2 * WINDOW : 2 * WINDOW + 1]
        ds, pb = [], []
        for w in range(WINDOW):
            rows = pl.ds(pl.multiple_of((b + w) * BLOCK, BLOCK), BLOCK)
            s = mm(k_all[rows, :], q, NT)
            dp = mm(v_all[rows, :], g, NT)
            top = fd_ref[u, w : w + 1]
            top = jnp.where(top < MASKED / 2, 0.0, top)
            p = jnp.exp2(s * SCALE - top) * fd_ref[u, WINDOW + w : WINDOW + w + 1]
            ds.append((p * (dp - delta)).astype(jnp.bfloat16))
            pb.append(p.astype(jnp.bfloat16))
        ds = jnp.concatenate(ds, axis=0)
        pb = jnp.concatenate(pb, axis=0)
        ds_ref[u] = ds
        shape = (WINDOW, BLOCK, DH)
        acc[pl.ds(b, WINDOW), 0] += mm(ds, q, NN).reshape(shape)
        acc[pl.ds(b, WINDOW), 1] += mm(pb, g, NN).reshape(shape)

    @pl.when(step == pl.num_programs(0) - 1)
    def _():
        for which, f in ((0, FACTOR), (1, 1.0)):
            keep_ref[:, which] = (acc[1:-1, which, own, :] * f).astype(keep_ref.dtype)
            send_ref[:, which] = (acc[1:-1, which, opp, :] * f).astype(jnp.bfloat16)


def queries_kernel(
    first, owners, k_ref, low_ref, high_ref, mine_ref, other_ref, dsw_ref, dsf_ref, *refs
):
    *_, dq_ref, k_all, kt_all = refs
    blocks = k_ref.shape[0] // BLOCK
    peers = mine_ref.shape[0]
    per = dsw_ref.shape[0]
    core, _ = places()
    step = pl.program_id(0)
    first_random = blocks + 2
    first_global = first_random + peers
    slices, size = glob_slices(peers)

    @pl.when(step == 0)
    def _():
        at_low, at_high = edge_places(blocks)
        k_all[at_low] = low_ref[0]
        k_all[at_high] = high_ref[0]
        k_all[1 : blocks + 1] = k_ref[...].reshape(blocks, BLOCK, DH)
        for ref, c in ((mine_ref, core), (other_ref, 1 - core)):
            k_all[first_random:first_global, pl.ds(c * HALF, HALF), :] = ref[:, :HALF, :]
            for i in range(slices):
                unit, offset = divmod(i * size, HALF)
                if unit % 2 == 0:
                    rows = pl.ds(pl.multiple_of(c * HALF + offset, MARKS), size)
                    k_all[first_global + unit // 2, rows, :] = ref[i, 2 * HALF :, :]

        def turn(j, carry):
            kt_all[j] = k_all[j].T
            return carry

        lax.fori_loop(0, first_global + G, turn, 0, unroll=4)

    for u in range(per):
        b = first + step * per + u
        panels = [b + w for w in range(WINDOW)]
        panels += [first_random + owners[b * R + r] for r in range(R)]
        panels += [first_global + j for j in range(G)]
        turned = [kt_all[i] for i in panels]
        dqt = mm(jnp.concatenate(turned[:WINDOW], axis=1), dsw_ref[u], NN)
        dqt = (dqt + mm(jnp.concatenate(turned[WINDOW:], axis=1), dsf_ref[u], NN)) * FACTOR
        for h in range(dq_ref.shape[1] // DH):
            dq_ref[u * BLOCK : (u + 1) * BLOCK, h * DH : (h + 1) * DH] = (
                dqt[:, h * BLOCK : (h + 1) * BLOCK].T.astype(jnp.bfloat16)
            )


def whole(a):
    return pl.BlockSpec(a.shape, lambda i, *_: (0,) * len(a.shape))


def per_block(per, *rest):
    return pl.BlockSpec((per,) + rest, lambda i, *_: (i,) + (0,) * len(rest))


def partners(size, stride):
    return [(i, i ^ stride) for i in range(size)]


def body(query_vectors, key_vectors, value_vectors, output_grad, random_blocks, global_blocks):
    seq_count = lax.axis_size("seq")
    head_count = lax.axis_size("head")
    rows_dev, columns = query_vectors.shape
    blocks = rows_dev // BLOCK
    per = math.gcd(blocks, 4)
    steps = blocks // per
    lanes = columns // DH * BLOCK
    bf16 = jnp.bfloat16
    f32 = jnp.float32
    sds = jax.ShapeDtypeStruct
    core_pairs = partners(head_count, 1)
    limit = (16 + seq_count // 2) * MIB
    params = pltpu.CompilerParams(dimension_semantics=("arbitrary",), vmem_limit_bytes=limit)
    unit = 2 * blocks * lanes * BLOCK * DH

    vmem = pl.BlockSpec(memory_space=pltpu.VMEM)
    smem = pl.BlockSpec(memory_space=pltpu.SMEM)
    hbm = pl.BlockSpec(memory_space=pltpu.HBM)
    small = pltpu.CompilerParams(vmem_limit_bytes=limit)
    large = pltpu.CompilerParams(vmem_limit_bytes=60 * MIB)
    share = BLOCK // head_count
    columns_count = head_count // 2

    edge = (2, BLOCK, DH)
    _, size = glob_slices(seq_count)
    asking, to_low, to_high, owners = pl.pallas_call(
        ask_kernel,
        out_shape=(
            sds((seq_count, MARKS + size, DH), bf16),
            sds(edge, bf16),
            sds(edge, bf16),
            sds((blocks * R,), jnp.int32),
        ),
        in_specs=[smem, smem, vmem, hbm, hbm],
        out_specs=(vmem, vmem, vmem, smem),
        scratch_shapes=[
            pltpu.VMEM((2 * G * HALF, DH), bf16),
            pltpu.SemaphoreType.DMA((2 * G + 4,)),
        ],
        compiler_params=large,
        name="ask",
    )(global_blocks, random_blocks.T, random_blocks.T, key_vectors, value_vectors)
    asked = lax.all_to_all(asking, "seq", split_axis=0, concat_axis=0, tiled=True)

    low_pairs = [(i, i ^ 1) for i in range(seq_count)]
    high_pairs = [(i, i + 1 if i % 2 else i - 1) for i in range(1, seq_count - 1)]
    low = lax.ppermute(to_low, "seq", low_pairs)
    high = lax.ppermute(to_high, "seq", high_pairs)
    asked, low, high = lax.optimization_barrier((asked, low, high))

    served, requested = pl.pallas_call(
        serve_kernel,
        out_shape=(sds((seq_count, 2 * HALF + size, DH), bf16), sds((seq_count,), jnp.int32)),
        in_specs=[smem, vmem, hbm, hbm],
        out_specs=(vmem, smem),
        scratch_shapes=[pltpu.SemaphoreType.DMA((seq_count, 2))],
        compiler_params=large,
        name="serve",
    )(global_blocks, asked, key_vectors, value_vectors)
    mine = lax.all_to_all(served, "seq", split_axis=0, concat_axis=0, tiled=True)

    rows_spec = pl.BlockSpec((per * BLOCK, columns), lambda i, *_: (i, 0))
    st_spec = per_block(per, 2 * FOLD, lanes)
    fd_spec = per_block(per, FOLD, lanes)
    nearby = (key_vectors, value_vectors, low, high)
    window_scratch = [pltpu.VMEM(((blocks + 2) * BLOCK, DH), bf16)] * 2
    st = pl.pallas_call(
        near_kernel,
        out_shape=sds((blocks, 2 * FOLD, lanes), f32),
        grid=(steps,),
        in_specs=[rows_spec, rows_spec] + [whole(a) for a in nearby],
        out_specs=st_spec,
        scratch_shapes=window_scratch,
        compiler_params=large,
        cost_estimate=pl.CostEstimate(
            flops=2 * WINDOW * unit, bytes_accessed=4 * MIB, transcendentals=blocks * lanes * WINDOW * BLOCK
        ),
        name="near",
    )(query_vectors, output_grad, *nearby)
    mine, st = lax.optimization_barrier((mine, st))
    other = lax.ppermute(mine, "head", core_pairs)

    slots = seq_count + G + 2
    piece = (slots, 2, share, DH)
    dsf, fd, *pieces = pl.pallas_call(
        far_kernel,
        out_shape=(
            sds((blocks, FAR * BLOCK, lanes), bf16),
            sds((blocks, FOLD, lanes), f32),
        )
        + (sds(piece, bf16),) * head_count,
        in_specs=[smem, hbm, hbm] + [vmem] * 5,
        out_specs=(hbm, vmem) + (vmem,) * head_count,
        scratch_shapes=[pltpu.VMEM(query_vectors.shape, bf16)] * 2
        + [pltpu.VMEM((seq_count + G, BLOCK, DH), bf16)] * 2
        + [pltpu.VMEM((slots, 2, BLOCK, DH), f32)]
        + [pltpu.VMEM((2, FAR * BLOCK, lanes), f32)] * 2
        + [
            pltpu.VMEM((blocks, FAR * BLOCK, lanes), bf16),
            pltpu.SemaphoreType.DMA((blocks, 2)),
            pltpu.SemaphoreType.DMA((blocks,)),
        ],
        compiler_params=large,
        cost_estimate=pl.CostEstimate(
            flops=5 * FAR * unit, bytes_accessed=8 * MIB, transcendentals=blocks * lanes * FAR * BLOCK
        ),
        name="far",
    )(owners, query_vectors, output_grad, mine, other, st, low, high)

    piece_w = (blocks, 2, HALF, DH)
    near_spec = per_block(per, WINDOW * BLOCK, lanes)
    far_spec = per_block(per, FAR * BLOCK, lanes)
    dsw, keep_w, send_w = pl.pallas_call(
        close_kernel,
        out_shape=(sds((blocks, WINDOW * BLOCK, lanes), bf16), sds(piece_w, bf16), sds(piece_w, bf16)),
        grid=(steps,),
        in_specs=[rows_spec, rows_spec] + [whole(a) for a in nearby] + [fd_spec],
        out_specs=(near_spec, whole(sds(piece_w, bf16)), whole(sds(piece_w, bf16))),
        scratch_shapes=window_scratch + [pltpu.VMEM((blocks + 2, 2, BLOCK, DH), f32)],
        compiler_params=large,
        cost_estimate=pl.CostEstimate(flops=4 * WINDOW * unit, bytes_accessed=8 * MIB, transcendentals=0),
        name="close",
    )(query_vectors, output_grad, *nearby, fd)

    others = [m << 1 for m in range(1, columns_count)]

    def reduced(kept, sent, name, dtype):
        got = lax.ppermute(sent, "head", core_pairs)
        part = (kept.shape[0], 2, share, DH)
        home, *away = pl.pallas_call(
            functools.partial(split_kernel, columns_count),
            out_shape=(sds(part, dtype),) + (sds(part, bf16),) * len(others),
            in_specs=[vmem, vmem],
            out_specs=(vmem,) * (1 + len(others)),
            compiler_params=small,
            name=name,
        )(kept, got)
        return [home] + [
            lax.ppermute(a, "head", partners(head_count, m)) for a, m in zip(away, others)
        ]

    parts = pieces[:1] + [
        lax.ppermute(pieces[m], "head", partners(head_count, m)) for m in range(1, head_count)
    ]
    parts[-1], send_w = lax.optimization_barrier((parts[-1], send_w))
    terms, to_low, to_high = pl.pallas_call(
        terms_kernel,
        out_shape=(
            sds((seq_count, 2 + 2 * G, share, DH), bf16),
            sds((2, share, DH), bf16),
            sds((2, share, DH), bf16),
        ),
        in_specs=[vmem] * len(parts),
        out_specs=(vmem,) * 3,
        compiler_params=small,
        name="terms",
    )(*parts)
    parts_w = reduced(keep_w, send_w, "split_close", bf16)
    dsw, to_low = lax.optimization_barrier((dsw, to_low))

    def queries(half, dsw, done):
        shift = half * (steps // 2)
        part = lambda *rest: pl.BlockSpec((per,) + rest, lambda i, *_: (i + shift,) + (0,) * len(rest))
        return pl.pallas_call(
            functools.partial(queries_kernel, shift * per),
            out_shape=sds(query_vectors.shape, bf16),
            grid_spec=pltpu.PrefetchScalarGridSpec(
                num_scalar_prefetch=1,
                grid=(steps // 2,),
                in_specs=[whole(a) for a in (key_vectors, low, high, mine, other)]
                + [part(WINDOW * BLOCK, lanes), part(FAR * BLOCK, lanes)]
                + [hbm] * len(done),
                out_specs=pl.BlockSpec((per * BLOCK, columns), lambda i, *_: (i + shift, 0)),
                scratch_shapes=[pltpu.VMEM((blocks + 2 + seq_count + G, BLOCK, DH), bf16)] * 2,
            ),
            input_output_aliases={8: 0} if done else {},
            compiler_params=large,
            cost_estimate=pl.CostEstimate(
                flops=LISTED * unit // 2, bytes_accessed=4 * MIB, transcendentals=0
            ),
            name="queries",
        )(owners, key_vectors, low, high, mine, other, dsw, dsf, *done)

    query_grad = queries(0, dsw, ())
    back = lax.all_to_all(terms, "seq", split_axis=0, concat_axis=0, tiled=True)
    from_low = lax.ppermute(to_low, "seq", low_pairs)
    from_high = lax.ppermute(to_high, "seq", high_pairs)
    back, query_grad = lax.optimization_barrier((back, query_grad))
    held = pl.pallas_call(
        settle_kernel,
        out_shape=sds((blocks, 2, share, DH), bf16),
        in_specs=[smem, smem] + [vmem] * (3 + len(parts_w)),
        out_specs=vmem,
        scratch_shapes=[pltpu.VMEM((blocks, 2, share, DH), f32)],
        compiler_params=small,
        name="settle",
    )(requested, global_blocks, back, from_low, from_high, *parts_w)

    dsw, query_grad, held = lax.optimization_barrier((dsw, query_grad, held))
    query_grad = queries(1, dsw, (query_grad,))
    rows = [held] + [lax.ppermute(held, "head", partners(head_count, m)) for m in others]
    rows[-1], query_grad = lax.optimization_barrier((rows[-1], query_grad))
    pieces = []
    for a in rows:
        pieces += [a, lax.ppermute(a, "head", core_pairs)]
    key_grad, value_grad = pl.pallas_call(
        functools.partial(join_kernel, columns_count),
        out_shape=(sds(key_vectors.shape, bf16),) * 2,
        in_specs=[vmem] * len(pieces),
        out_specs=(vmem, vmem),
        scratch_shapes=[pltpu.VMEM((blocks, BLOCK, DH), bf16)] * 2,
        compiler_params=small,
        name="join",
    )(*pieces)
    return query_grad, key_grad, value_grad


def solution(mesh):
    return jax.shard_map(
        body,
        mesh=mesh,
        in_specs=(
            P("seq", "head"),
            P("seq", None),
            P("seq", None),
            P("seq", "head"),
            P("seq", None),
            P(),
        ),
        out_specs=(P("seq", "head"), P("seq", None), P("seq", None)),
        check_vma=False,
    )
```

```python
import functools
import math

import jax
import jax.numpy as jnp
from jax import lax
from jax.experimental import pallas as pl
from jax.experimental.pallas import tpu as pltpu
from jax.sharding import PartitionSpec as P

DH = 128
BLOCK = 128
HALF = BLOCK // 2
R = 3
G = 2
WINDOW = 3
FAR = R + G
LISTED = WINDOW + FAR
MIB = 1024 * 1024
MASKED = -1e30
FACTOR = float(DH) ** -0.5
SCALE = FACTOR * math.log2(math.e)
FOLD = 8
SPARE = 9
MARKS = 16

NT = (((1,), (1,)), ((), ()))
NN = (((1,), (0,)), ((), ()))
TN = (((0,), (0,)), ((), ()))


def mm(a, b, dims):
    return lax.dot_general(a, b, dims, preferred_element_type=jnp.float32)


def stack_heads(ref, u):
    rows = ref[u * BLOCK : (u + 1) * BLOCK, :]
    return jnp.concatenate(
        [rows[:, h * DH : (h + 1) * DH] for h in range(rows.shape[1] // DH)], axis=0
    )


def fold(x):
    return jnp.sum(x.reshape(x.shape[0] // FOLD, FOLD, x.shape[1]), axis=0)


def panel(k, v, q, g):
    s = mm(k, q, NT)
    dp = mm(v, g, NT)
    top = jnp.max(s, axis=0, keepdims=True) * SCALE
    e = jnp.exp2(s * SCALE - top)
    return top, e, dp, fold(e), fold(e * dp)


def places():
    head_index = lax.axis_index("head")
    return lax.rem(head_index, 2), lax.div(head_index, 2)


def glob_slices(peers):
    rows = 2 * G * HALF
    size = max(MARKS, rows // peers)
    return rows // size, size


def ask_kernel(
    global_blocks, random_blocks, random_ref, k_ref, v_ref, out_ref, low_ref, high_ref, owners, rows, sems
):
    tokens = k_ref.shape[0]
    blocks = tokens // BLOCK
    peers = out_ref.shape[0]
    core, _ = places()
    slices, size = glob_slices(peers)
    edges, copies = [], []

    def begin(group, src, dst):
        group.append(pltpu.make_async_copy(src, dst, sems.at[len(edges) + len(copies)]))
        group[-1].start()

    for j in range(G):
        start = lax.rem(global_blocks[j], blocks) * BLOCK + core * HALF
        start = pl.multiple_of(start, HALF)
        for which, ref in ((0, k_ref), (1, v_ref)):
            at = (2 * j + which) * HALF
            begin(copies, ref.at[pl.ds(start, HALF), :], rows.at[pl.ds(at, HALF), :])
    odd = lax.rem(lax.axis_index("seq"), 2)
    for which, ref in ((0, k_ref), (1, v_ref)):
        for edge_ref, at in ((low_ref, (1 - odd) * (tokens - BLOCK)), (high_ref, odd * (tokens - BLOCK))):
            start = pl.multiple_of(at, BLOCK)
            begin(edges, ref.at[pl.ds(start, BLOCK), :], edge_ref.at[which])
    wanted = random_ref[...]

    def mark(j, carry):
        within = wanted - j * blocks
        mine = jnp.logical_and(within >= 0, within < blocks)
        top = jnp.max(jnp.where(mine, within, -1).astype(jnp.float32))
        out_ref[j, :MARKS, :] = jnp.full((MARKS, DH), top, jnp.float32).astype(jnp.bfloat16)
        return carry

    lax.fori_loop(0, peers, mark, 0, unroll=min(peers, 8))
    for b in range(blocks):
        for r in range(R):
            owners[b * R + r] = lax.div(random_blocks[r, b], blocks)
    for copy in copies:
        copy.wait()
    out_ref[:slices, MARKS:, :] = rows[...].reshape(slices, size, DH)
    if slices < peers:
        out_ref[slices:, MARKS:, :] = jnp.zeros((peers - slices, size, DH), jnp.bfloat16)
    for copy in edges:
        copy.wait()


def serve_kernel(global_blocks, asked_ref, k_ref, v_ref, out_ref, requested_ref, sems):
    blocks = k_ref.shape[0] // BLOCK
    core, _ = places()
    peers = out_ref.shape[0]
    many = min(peers, 8)
    slices, size = glob_slices(peers)

    def copy(j, start, which, ref):
        return pltpu.make_async_copy(
            ref.at[pl.ds(start, HALF), :],
            out_ref.at[j, pl.ds(which * HALF, HALF), :],
            sems.at[j, which],
        )

    def begin(j, carry):
        wanted = jnp.max(asked_ref[j, :MARKS, :].astype(jnp.float32)).astype(jnp.int32)
        requested_ref[j] = wanted
        start = pl.multiple_of(jnp.clip(wanted, 0, blocks - 1) * BLOCK + core * HALF, HALF)
        copy(j, start, 0, k_ref).start()
        copy(j, start, 1, v_ref).start()
        return carry

    lax.fori_loop(0, peers, begin, 0, unroll=many)
    index = jnp.minimum(lax.axis_index("seq"), slices - 1)
    owner = lax.div(global_blocks[lax.div(index * size, 2 * HALF)], blocks)
    out_ref[:, 2 * HALF :, :] = jnp.broadcast_to(
        asked_ref[owner, MARKS:, :][None], (peers, size, DH)
    )

    def end(j, carry):
        copy(j, 0, 0, k_ref).wait()
        copy(j, 0, 1, v_ref).wait()
        return carry

    lax.fori_loop(0, peers, end, 0, unroll=many)


def split_kernel(count, keep_ref, got_ref, out_ref, *send_refs):
    share = out_ref.shape[2]
    _, column = places()
    own = pl.ds(pl.multiple_of(column * share, share), share)
    total = keep_ref[:, :, own, :].astype(jnp.float32) + got_ref[:, :, own, :].astype(jnp.float32)
    out_ref[...] = total.astype(out_ref.dtype)
    for m in range(1, count):
        there = pl.ds(pl.multiple_of((column ^ m) * share, share), share)
        send_refs[m - 1][...] = (
            keep_ref[:, :, there, :].astype(jnp.float32) + got_ref[:, :, there, :].astype(jnp.float32)
        ).astype(jnp.bfloat16)


def terms_kernel(keep_ref, *refs):
    *got_refs, terms_ref, low_ref, high_ref = refs
    peers, _, share, _ = terms_ref.shape
    odd = lax.rem(lax.axis_index("seq"), 2) == 1

    def total(slot, n=1):
        x = keep_ref[slot : slot + n].astype(jnp.float32)
        for ref in got_refs:
            x = x + ref[slot : slot + n].astype(jnp.float32)
        return x.astype(jnp.bfloat16)

    terms_ref[:, :2] = total(0, peers)
    glob = total(peers, G).reshape(1, 2 * G, share, DH)
    terms_ref[:, 2:] = jnp.broadcast_to(glob, (peers, 2 * G, share, DH))
    previous = total(peers + G)[0]
    following = total(peers + G + 1)[0]
    low_ref[...] = jnp.where(odd, previous, following)
    high_ref[...] = jnp.where(odd, following, previous)


def settle_kernel(requested, global_blocks, back_ref, low_ref, high_ref, *refs):
    *got_refs, out_ref, acc = refs
    blocks = out_ref.shape[0]
    peers, _, share, _ = back_ref.shape
    seq_index = lax.axis_index("seq")
    acc[...] = sum(ref[...].astype(jnp.float32) for ref in got_refs)
    at_low, at_high = edge_places(blocks)
    acc[jnp.clip(at_low - 1, 0, blocks - 1)] += low_ref[...].astype(jnp.float32)
    acc[jnp.clip(at_high - 1, 0, blocks - 1)] += high_ref[...].astype(jnp.float32)

    def one(j, carry):
        wanted = requested[j]

        @pl.when(wanted >= 0)
        def _():
            acc[wanted] += back_ref[j, :2].astype(jnp.float32)

        return carry

    lax.fori_loop(0, peers, one, 0)
    for j in range(G):

        @pl.when(lax.div(global_blocks[j], blocks) == seq_index)
        def _():
            rows = back_ref[:, 2 + 2 * j : 4 + 2 * j].astype(jnp.float32)
            acc[lax.rem(global_blocks[j], blocks)] += jnp.sum(rows, axis=0)

    out_ref[...] = acc[...].astype(jnp.bfloat16)


def join_kernel(count, *refs):
    *got_refs, dk_ref, dv_ref, dk, dv = refs
    blocks, _, share, _ = got_refs[0].shape
    core, column = places()
    for m in range(count):
        for c in range(2):
            at = (core ^ c) * HALF + (column ^ m) * share
            rows = pl.ds(pl.multiple_of(at, share), share)
            ref = got_refs[2 * m + c]
            dk[:, rows, :] = ref[:, 0]
            dv[:, rows, :] = ref[:, 1]
    dk_ref[...] = dk[...].reshape(dk_ref.shape)
    dv_ref[...] = dv[...].reshape(dv_ref.shape)


def edge_places(blocks):
    odd = lax.rem(lax.axis_index("seq"), 2)
    return (1 - odd) * (blocks + 1), odd * (blocks + 1)


def fill_window(k_ref, v_ref, low_ref, high_ref, k_all, v_all):
    rows = k_ref.shape[0]
    low, high = (pl.ds(pl.multiple_of(i * BLOCK, BLOCK), BLOCK) for i in edge_places(rows // BLOCK))
    for to, own, which in ((k_all, k_ref, 0), (v_all, v_ref, 1)):
        to[low, :] = low_ref[which]
        to[high, :] = high_ref[which]
        to[BLOCK : BLOCK + rows] = own[...]


def near_kernel(q_ref, g_ref, k_ref, v_ref, low_ref, high_ref, st_ref, k_all, v_all):
    step = pl.program_id(0)
    blocks = k_ref.shape[0] // BLOCK
    seq_index = lax.axis_index("seq")
    per = st_ref.shape[0]

    @pl.when(step == 0)
    def _():
        fill_window(k_ref, v_ref, low_ref, high_ref, k_all, v_all)

    for u in range(per):
        b = step * per + u
        q = stack_heads(q_ref, u)
        g = stack_heads(g_ref, u)
        no_left = jnp.logical_and(seq_index == 0, b == 0)
        no_right = jnp.logical_and(seq_index == lax.axis_size("seq") - 1, b == blocks - 1)
        biases = (jnp.where(no_left, MASKED, 0.0), None, jnp.where(no_right, MASKED, 0.0))
        for w in range(WINDOW):
            rows = pl.ds(pl.multiple_of((b + w) * BLOCK, BLOCK), BLOCK)
            top, _, _, l, d = panel(k_all[rows, :], v_all[rows, :], q, g)
            if biases[w] is not None:
                top = top + biases[w]
            st_ref[u, w : w + 1] = top
            st_ref[u, WINDOW + w : WINDOW + w + 1] = jnp.sum(l, axis=0, keepdims=True)
            st_ref[u, 2 * WINDOW + w : 2 * WINDOW + w + 1] = jnp.sum(d, axis=0, keepdims=True)


def far_kernel(
    owners, q_ref, g_ref, mine_ref, other_ref, st_ref, low_ref, high_ref,
    ds_ref, fd_ref, *refs,
):
    *share_refs, k_all, v_all, acc, e_all, dp_all, ds_all, out_sems = refs
    blocks = q_ref.shape[0] // BLOCK
    peers = mine_ref.shape[0]
    core, column = places()
    own, opp = pl.ds(core * HALF, HALF), pl.ds((1 - core) * HALF, HALF)
    slices, size = glob_slices(peers)

    def at(b):
        return pl.ds(pl.multiple_of(b * BLOCK, BLOCK), BLOCK)

    def put(b):
        return pltpu.make_async_copy(ds_all.at[b], ds_ref.at[b], out_sems.at[b])

    for to, which in ((k_all, 0), (v_all, 1)):
        rows = slice(which * HALF, (which + 1) * HALF)
        to[:peers, own, :] = mine_ref[:, rows, :]
        to[:peers, opp, :] = other_ref[:, rows, :]
    for i in range(slices):
        unit, offset = divmod(i * size, HALF)
        to = (k_all, v_all)[unit % 2]
        slot = peers + unit // 2
        to[slot, pl.ds(pl.multiple_of(core * HALF + offset, MARKS), size), :] = mine_ref[i, 2 * HALF :, :]
        to[slot, pl.ds(pl.multiple_of((1 - core) * HALF + offset, MARKS), size), :] = other_ref[i, 2 * HALF :, :]
    acc[...] = jnp.zeros_like(acc)

    def heads(ref, b):
        rows = ref[at(b), :]
        return jnp.concatenate(
            [rows[:, h * DH : (h + 1) * DH] for h in range(rows.shape[1] // DH)], axis=0
        )

    def slots_of(b):
        return [owners[b * R + r] for r in range(R)] + [peers + j for j in range(G)]

    def work(new, new_slot, old, old_slot, stats):
        if new is not None:
            q1, g1, slots1 = heads(q_ref, new), heads(g_ref, new), slots_of(new)
        if old is not None:
            q2, g2, slots2 = heads(q_ref, old), heads(g_ref, old), slots_of(old)
        tops, ls, dd = [], [], []

        def dots(i):
            return mm(k_all[slots1[i]], q1, NT), mm(v_all[slots1[i]], g1, NT)

        if new is not None:
            ready = dots(0)
        for i in range(FAR):
            rows = slice(i * BLOCK, (i + 1) * BLOCK)
            if new is not None:
                s, dp = ready
                if i + 1 < FAR:
                    ready = dots(i + 1)
            if old is not None:
                p = e_all[old_slot, rows] * stats[i]
                ds = (p * (dp_all[old_slot, rows] - stats[FAR])).astype(jnp.bfloat16)
                ds_all[old, rows] = ds
            if new is not None:
                top = jnp.max(s, axis=0, keepdims=True) * SCALE
                e = jnp.exp2(s * SCALE - top)
                e_all[new_slot, rows] = e
                dp_all[new_slot, rows] = dp
                tops.append(top)
                ls.append(fold(e))
                dd.append(fold(e * dp))
            if old is not None:
                acc[slots2[i], 0] += mm(ds, q2, NN)
                acc[slots2[i], 1] += mm(p.astype(jnp.bfloat16), g2, NN)
        if old is not None:
            put(old).start()
        if new is None:
            return None
        near = [[st_ref[new, i * WINDOW + w : i * WINDOW + w + 1] for w in range(WINDOW)] for i in range(3)]
        top = functools.reduce(jnp.maximum, near[0] + tops)
        near_weight = [jnp.exp2(t - top) for t in near[0]]
        weight = [jnp.exp2(t - top) for t in tops]
        l = jnp.sum(sum(w * x for w, x in zip(weight, ls)), axis=0, keepdims=True)
        d = jnp.sum(sum(w * x for w, x in zip(weight, dd)), axis=0, keepdims=True)
        l = l + sum(w * x for w, x in zip(near_weight, near[1]))
        d = d + sum(w * x for w, x in zip(near_weight, near[2]))
        inv = 1.0 / l
        delta = d * inv
        for w in range(WINDOW):
            fd_ref[new, w : w + 1] = near[0][w]
            fd_ref[new, WINDOW + w : WINDOW + w + 1] = near_weight[w] * inv
        fd_ref[new, 2 * WINDOW : 2 * WINDOW + 1] = delta
        return tuple(w * inv for w in weight) + (delta,)

    turn = math.gcd(blocks, 4)

    def several(t, stats, last=False):
        for j in range(turn - last):
            b = t * turn + j
            stats = work(b + 1, (j + 1) % 2, b, j % 2, stats)
        return stats

    stats = work(0, 0, None, None, None)
    stats = lax.fori_loop(0, blocks // turn - 1, several, stats)
    stats = several(blocks // turn - 1, stats, True)
    work(None, None, blocks - 1, 1, stats)

    for slot, w, b, swap in ((peers + G, 0, 0, 1), (peers + G + 1, WINDOW - 1, blocks - 1, 0)):
        odd = lax.rem(lax.axis_index("seq"), 2) == swap
        q, g = heads(q_ref, b), heads(g_ref, b)
        s = mm(jnp.where(odd, low_ref[0], high_ref[0]), q, NT)
        dp = mm(jnp.where(odd, low_ref[1], high_ref[1]), g, NT)
        p = jnp.exp2(s * SCALE - jnp.max(s, axis=0, keepdims=True) * SCALE)
        p = p * fd_ref[b, WINDOW + w : WINDOW + w + 1]
        ds = (p * (dp - fd_ref[b, 2 * WINDOW : 2 * WINDOW + 1])).astype(jnp.bfloat16)
        acc[slot, 0] = mm(ds, q, NN)
        acc[slot, 1] = mm(p.astype(jnp.bfloat16), g, NN)

    share = share_refs[0].shape[2]
    for m, ref in enumerate(share_refs):
        start = (core ^ (m & 1)) * HALF + (column ^ (m >> 1)) * share
        rows = pl.ds(pl.multiple_of(start, share), share)
        for which, f in ((0, FACTOR), (1, 1.0)):
            ref[:, which] = (acc[:, which, rows, :] * f).astype(ref.dtype)
    for b in range(blocks):
        put(b).wait()


def close_kernel(
    q_ref, g_ref, k_ref, v_ref, low_ref, high_ref, fd_ref, ds_ref, keep_ref, send_ref, k_all, v_all, acc
):
    step = pl.program_id(0)
    per = fd_ref.shape[0]
    core, _ = places()
    own, opp = pl.ds(core * HALF, HALF), pl.ds((1 - core) * HALF, HALF)

    @pl.when(step == 0)
    def _():
        fill_window(k_ref, v_ref, low_ref, high_ref, k_all, v_all)
        acc[...] = jnp.zeros_like(acc)

    for u in range(per):
        b = step * per + u
        q = stack_heads(q_ref, u)
        g = stack_heads(g_ref, u)
        delta = fd_ref[u, 2 * WINDOW : 2 * WINDOW + 1]
        ds, pb = [], []
        for w in range(WINDOW):
            rows = pl.ds(pl.multiple_of((b + w) * BLOCK, BLOCK), BLOCK)
            s = mm(k_all[rows, :], q, NT)
            dp = mm(v_all[rows, :], g, NT)
            top = fd_ref[u, w : w + 1]
            top = jnp.where(top < MASKED / 2, 0.0, top)
            p = jnp.exp2(s * SCALE - top) * fd_ref[u, WINDOW + w : WINDOW + w + 1]
            ds.append((p * (dp - delta)).astype(jnp.bfloat16))
            pb.append(p.astype(jnp.bfloat16))
        ds = jnp.concatenate(ds, axis=0)
        pb = jnp.concatenate(pb, axis=0)
        ds_ref[u] = ds
        shape = (WINDOW, BLOCK, DH)
        acc[pl.ds(b, WINDOW), 0] += mm(ds, q, NN).reshape(shape)
        acc[pl.ds(b, WINDOW), 1] += mm(pb, g, NN).reshape(shape)

    @pl.when(step == pl.num_programs(0) - 1)
    def _():
        for which, f in ((0, FACTOR), (1, 1.0)):
            keep_ref[:, which] = (acc[1:-1, which, own, :] * f).astype(keep_ref.dtype)
            send_ref[:, which] = (acc[1:-1, which, opp, :] * f).astype(jnp.bfloat16)


def queries_kernel(
    first, owners, k_ref, low_ref, high_ref, mine_ref, other_ref, dsw_ref, dsf_ref, *refs
):
    *_, dq_ref, k_all, kt_all = refs
    blocks = k_ref.shape[0] // BLOCK
    peers = mine_ref.shape[0]
    per = dsw_ref.shape[0]
    core, _ = places()
    step = pl.program_id(0)
    first_random = blocks + 2
    first_global = first_random + peers
    slices, size = glob_slices(peers)

    @pl.when(step == 0)
    def _():
        at_low, at_high = edge_places(blocks)
        k_all[at_low] = low_ref[0]
        k_all[at_high] = high_ref[0]
        k_all[1 : blocks + 1] = k_ref[...].reshape(blocks, BLOCK, DH)
        for ref, c in ((mine_ref, core), (other_ref, 1 - core)):
            k_all[first_random:first_global, pl.ds(c * HALF, HALF), :] = ref[:, :HALF, :]
            for i in range(slices):
                unit, offset = divmod(i * size, HALF)
                if unit % 2 == 0:
                    rows = pl.ds(pl.multiple_of(c * HALF + offset, MARKS), size)
                    k_all[first_global + unit // 2, rows, :] = ref[i, 2 * HALF :, :]

        def turn(j, carry):
            kt_all[j] = k_all[j].T
            return carry

        lax.fori_loop(0, first_global + G, turn, 0, unroll=4)

    for u in range(per):
        b = first + step * per + u
        panels = [b + w for w in range(WINDOW)]
        panels += [first_random + owners[b * R + r] for r in range(R)]
        panels += [first_global + j for j in range(G)]
        turned = [kt_all[i] for i in panels]
        dqt = mm(jnp.concatenate(turned[:WINDOW], axis=1), dsw_ref[u], NN)
        dqt = (dqt + mm(jnp.concatenate(turned[WINDOW:], axis=1), dsf_ref[u], NN)) * FACTOR
        for h in range(dq_ref.shape[1] // DH):
            dq_ref[u * BLOCK : (u + 1) * BLOCK, h * DH : (h + 1) * DH] = (
                dqt[:, h * BLOCK : (h + 1) * BLOCK].T.astype(jnp.bfloat16)
            )


def whole(a):
    return pl.BlockSpec(a.shape, lambda i, *_: (0,) * len(a.shape))


def per_block(per, *rest):
    return pl.BlockSpec((per,) + rest, lambda i, *_: (i,) + (0,) * len(rest))


def partners(size, stride):
    return [(i, i ^ stride) for i in range(size)]


def body(query_vectors, key_vectors, value_vectors, output_grad, random_blocks, global_blocks):
    seq_count = lax.axis_size("seq")
    head_count = lax.axis_size("head")
    rows_dev, columns = query_vectors.shape
    blocks = rows_dev // BLOCK
    per = math.gcd(blocks, 4)
    steps = blocks // per
    lanes = columns // DH * BLOCK
    bf16 = jnp.bfloat16
    f32 = jnp.float32
    sds = jax.ShapeDtypeStruct
    core_pairs = partners(head_count, 1)
    limit = (16 + seq_count // 2) * MIB
    params = pltpu.CompilerParams(dimension_semantics=("arbitrary",), vmem_limit_bytes=limit)
    unit = 2 * blocks * lanes * BLOCK * DH

    vmem = pl.BlockSpec(memory_space=pltpu.VMEM)
    smem = pl.BlockSpec(memory_space=pltpu.SMEM)
    hbm = pl.BlockSpec(memory_space=pltpu.HBM)
    small = pltpu.CompilerParams(vmem_limit_bytes=limit)
    large = pltpu.CompilerParams(vmem_limit_bytes=60 * MIB)
    share = BLOCK // head_count
    columns_count = head_count // 2

    edge = (2, BLOCK, DH)
    _, size = glob_slices(seq_count)
    asking, to_low, to_high, owners = pl.pallas_call(
        ask_kernel,
        out_shape=(
            sds((seq_count, MARKS + size, DH), bf16),
            sds(edge, bf16),
            sds(edge, bf16),
            sds((blocks * R,), jnp.int32),
        ),
        in_specs=[smem, smem, vmem, hbm, hbm],
        out_specs=(vmem, vmem, vmem, smem),
        scratch_shapes=[
            pltpu.VMEM((2 * G * HALF, DH), bf16),
            pltpu.SemaphoreType.DMA((2 * G + 4,)),
        ],
        compiler_params=large,
        name="ask",
    )(global_blocks, random_blocks.T, random_blocks.T, key_vectors, value_vectors)
    asked = lax.all_to_all(asking, "seq", split_axis=0, concat_axis=0, tiled=True)

    low_pairs = [(i, i ^ 1) for i in range(seq_count)]
    high_pairs = [(i, i + 1 if i % 2 else i - 1) for i in range(1, seq_count - 1)]
    low = lax.ppermute(to_low, "seq", low_pairs)
    high = lax.ppermute(to_high, "seq", high_pairs)
    asked, low, high = lax.optimization_barrier((asked, low, high))

    served, requested = pl.pallas_call(
        serve_kernel,
        out_shape=(sds((seq_count, 2 * HALF + size, DH), bf16), sds((seq_count,), jnp.int32)),
        in_specs=[smem, vmem, hbm, hbm],
        out_specs=(vmem, smem),
        scratch_shapes=[pltpu.SemaphoreType.DMA((seq_count, 2))],
        compiler_params=large,
        name="serve",
    )(global_blocks, asked, key_vectors, value_vectors)
    mine = lax.all_to_all(served, "seq", split_axis=0, concat_axis=0, tiled=True)

    rows_spec = pl.BlockSpec((per * BLOCK, columns), lambda i, *_: (i, 0))
    st_spec = per_block(per, 2 * FOLD, lanes)
    fd_spec = per_block(per, FOLD, lanes)
    nearby = (key_vectors, value_vectors, low, high)
    window_scratch = [pltpu.VMEM(((blocks + 2) * BLOCK, DH), bf16)] * 2
    st = pl.pallas_call(
        near_kernel,
        out_shape=sds((blocks, 2 * FOLD, lanes), f32),
        grid=(steps,),
        in_specs=[rows_spec, rows_spec] + [whole(a) for a in nearby],
        out_specs=st_spec,
        scratch_shapes=window_scratch,
        compiler_params=params,
        cost_estimate=pl.CostEstimate(
            flops=2 * WINDOW * unit, bytes_accessed=4 * MIB, transcendentals=blocks * lanes * WINDOW * BLOCK
        ),
        name="near",
    )(query_vectors, output_grad, *nearby)
    mine, st = lax.optimization_barrier((mine, st))
    queries_in, grads_in, mine = lax.optimization_barrier((query_vectors, output_grad, mine))
    here = lax.axis_index("seq") < seq_count
    queries_in = jnp.where(here, queries_in, 0).astype(bf16)
    grads_in = jnp.where(here, grads_in, 0).astype(bf16)
    other = lax.ppermute(mine, "head", core_pairs)

    slots = seq_count + G + 2
    piece = (slots, 2, share, DH)
    dsf, fd, *pieces = pl.pallas_call(
        far_kernel,
        out_shape=(
            sds((blocks * SPARE, FAR * BLOCK, lanes), bf16),
            sds((blocks, FOLD, lanes), f32),
        )
        + (sds(piece, bf16),) * head_count,
        in_specs=[smem] + [vmem] * 7,
        out_specs=(hbm, vmem) + (vmem,) * head_count,
        scratch_shapes=[pltpu.VMEM((seq_count + G, BLOCK, DH), bf16)] * 2
        + [pltpu.VMEM((slots, 2, BLOCK, DH), f32)]
        + [pltpu.VMEM((2, FAR * BLOCK, lanes), f32)] * 2
        + [
            pltpu.VMEM((blocks, FAR * BLOCK, lanes), bf16),
            pltpu.SemaphoreType.DMA((blocks,)),
        ],
        compiler_params=small,
        cost_estimate=pl.CostEstimate(
            flops=5 * FAR * unit, bytes_accessed=8 * MIB, transcendentals=blocks * lanes * FAR * BLOCK
        ),
        name="far",
    )(owners, queries_in, grads_in, mine, other, st, low, high)

    piece_w = (blocks, 2, HALF, DH)
    near_spec = per_block(per, WINDOW * BLOCK, lanes)
    far_spec = per_block(per, FAR * BLOCK, lanes)
    dsw, keep_w, send_w = pl.pallas_call(
        close_kernel,
        out_shape=(sds((blocks, WINDOW * BLOCK, lanes), bf16), sds(piece_w, bf16), sds(piece_w, bf16)),
        grid=(steps,),
        in_specs=[rows_spec, rows_spec] + [whole(a) for a in nearby] + [fd_spec],
        out_specs=(near_spec, whole(sds(piece_w, bf16)), whole(sds(piece_w, bf16))),
        scratch_shapes=window_scratch + [pltpu.VMEM((blocks + 2, 2, BLOCK, DH), f32)],
        compiler_params=large,
        cost_estimate=pl.CostEstimate(flops=4 * WINDOW * unit, bytes_accessed=8 * MIB, transcendentals=0),
        name="close",
    )(query_vectors, output_grad, *nearby, fd)

    others = [m << 1 for m in range(1, columns_count)]

    def reduced(kept, sent, name, dtype):
        got = lax.ppermute(sent, "head", core_pairs)
        part = (kept.shape[0], 2, share, DH)
        home, *away = pl.pallas_call(
            functools.partial(split_kernel, columns_count),
            out_shape=(sds(part, dtype),) + (sds(part, bf16),) * len(others),
            in_specs=[vmem, vmem],
            out_specs=(vmem,) * (1 + len(others)),
            compiler_params=small,
            name=name,
        )(kept, got)
        return [home] + [
            lax.ppermute(a, "head", partners(head_count, m)) for a, m in zip(away, others)
        ]

    parts = pieces[:1] + [
        lax.ppermute(pieces[m], "head", partners(head_count, m)) for m in range(1, head_count)
    ]
    parts[-1], send_w = lax.optimization_barrier((parts[-1], send_w))
    terms, to_low, to_high = pl.pallas_call(
        terms_kernel,
        out_shape=(
            sds((seq_count, 2 + 2 * G, share, DH), bf16),
            sds((2, share, DH), bf16),
            sds((2, share, DH), bf16),
        ),
        in_specs=[vmem] * len(parts),
        out_specs=(vmem,) * 3,
        compiler_params=small,
        name="terms",
    )(*parts)
    parts_w = reduced(keep_w, send_w, "split_close", bf16)
    dsw, to_low = lax.optimization_barrier((dsw, to_low))

    def queries(half, dsw, done):
        shift = half * (steps // 2)
        part = lambda *rest: pl.BlockSpec((per,) + rest, lambda i, *_: (i + shift,) + (0,) * len(rest))
        return pl.pallas_call(
            functools.partial(queries_kernel, shift * per),
            out_shape=sds(query_vectors.shape, bf16),
            grid_spec=pltpu.PrefetchScalarGridSpec(
                num_scalar_prefetch=1,
                grid=(steps // 2,),
                in_specs=[whole(a) for a in (key_vectors, low, high, mine, other)]
                + [part(WINDOW * BLOCK, lanes), part(FAR * BLOCK, lanes)]
                + [hbm] * len(done),
                out_specs=pl.BlockSpec((per * BLOCK, columns), lambda i, *_: (i + shift, 0)),
                scratch_shapes=[pltpu.VMEM((blocks + 2 + seq_count + G, BLOCK, DH), bf16)] * 2,
            ),
            input_output_aliases={8: 0} if done else {},
            compiler_params=large,
            cost_estimate=pl.CostEstimate(
                flops=LISTED * unit // 2, bytes_accessed=4 * MIB, transcendentals=0
            ),
            name="queries",
        )(owners, key_vectors, low, high, mine, other, dsw, dsf, *done)

    query_grad = queries(0, dsw, ())
    back = lax.all_to_all(terms, "seq", split_axis=0, concat_axis=0, tiled=True)
    from_low = lax.ppermute(to_low, "seq", low_pairs)
    from_high = lax.ppermute(to_high, "seq", high_pairs)
    back, query_grad = lax.optimization_barrier((back, query_grad))
    held = pl.pallas_call(
        settle_kernel,
        out_shape=sds((blocks, 2, share, DH), bf16),
        in_specs=[smem, smem] + [vmem] * (3 + len(parts_w)),
        out_specs=vmem,
        scratch_shapes=[pltpu.VMEM((blocks, 2, share, DH), f32)],
        compiler_params=small,
        name="settle",
    )(requested, global_blocks, back, from_low, from_high, *parts_w)

    dsw, query_grad, held = lax.optimization_barrier((dsw, query_grad, held))
    query_grad = queries(1, dsw, (query_grad,))
    rows = [held] + [lax.ppermute(held, "head", partners(head_count, m)) for m in others]
    rows[-1], query_grad = lax.optimization_barrier((rows[-1], query_grad))
    pieces = []
    for a in rows:
        pieces += [a, lax.ppermute(a, "head", core_pairs)]
    key_grad, value_grad = pl.pallas_call(
        functools.partial(join_kernel, columns_count),
        out_shape=(sds(key_vectors.shape, bf16),) * 2,
        in_specs=[vmem] * len(pieces),
        out_specs=(vmem, vmem),
        scratch_shapes=[pltpu.VMEM((blocks, BLOCK, DH), bf16)] * 2,
        compiler_params=small,
        name="join",
    )(*pieces)
    return query_grad, key_grad, value_grad


def solution(mesh):
    return jax.shard_map(
        body,
        mesh=mesh,
        in_specs=(
            P("seq", "head"),
            P("seq", None),
            P("seq", None),
            P("seq", "head"),
            P("seq", None),
            P(),
        ),
        out_specs=(P("seq", "head"), P("seq", None), P("seq", None)),
        check_vma=False,
    )
```

```python
import functools
import math

import jax
import jax.numpy as jnp
from jax import lax
from jax.experimental import pallas as pl
from jax.experimental.pallas import tpu as pltpu
from jax.sharding import PartitionSpec as P

DH = 128
BLOCK = 128
HALF = BLOCK // 2
R = 3
G = 2
WINDOW = 3
FAR = R + G
LISTED = WINDOW + FAR
MIB = 1024 * 1024
MASKED = -1e30
FACTOR = float(DH) ** -0.5
SCALE = FACTOR * math.log2(math.e)
FOLD = 8
SPARE = 5
MARKS = 16

NT = (((1,), (1,)), ((), ()))
NN = (((1,), (0,)), ((), ()))
TN = (((0,), (0,)), ((), ()))


def mm(a, b, dims):
    return lax.dot_general(a, b, dims, preferred_element_type=jnp.float32)


def stack_heads(ref, u):
    rows = ref[u * BLOCK : (u + 1) * BLOCK, :]
    return jnp.concatenate(
        [rows[:, h * DH : (h + 1) * DH] for h in range(rows.shape[1] // DH)], axis=0
    )


def fold(x):
    return jnp.sum(x.reshape(x.shape[0] // FOLD, FOLD, x.shape[1]), axis=0)


def panel(k, v, q, g):
    s = mm(k, q, NT)
    dp = mm(v, g, NT)
    top = jnp.max(s, axis=0, keepdims=True) * SCALE
    e = jnp.exp2(s * SCALE - top)
    return top, e, dp, fold(e), fold(e * dp)


def places():
    head_index = lax.axis_index("head")
    return lax.rem(head_index, 2), lax.div(head_index, 2)


def glob_slices(peers):
    rows = 2 * G * HALF
    size = max(MARKS, rows // peers)
    return rows // size, size


def ask_kernel(
    global_blocks, random_blocks, random_ref, k_ref, v_ref, out_ref, low_ref, high_ref, owners, rows, sems
):
    tokens = k_ref.shape[0]
    blocks = tokens // BLOCK
    peers = out_ref.shape[0]
    core, _ = places()
    slices, size = glob_slices(peers)
    edges, copies = [], []

    def begin(group, src, dst):
        group.append(pltpu.make_async_copy(src, dst, sems.at[len(edges) + len(copies)]))
        group[-1].start()

    for j in range(G):
        start = lax.rem(global_blocks[j], blocks) * BLOCK + core * HALF
        start = pl.multiple_of(start, HALF)
        for which, ref in ((0, k_ref), (1, v_ref)):
            at = (2 * j + which) * HALF
            begin(copies, ref.at[pl.ds(start, HALF), :], rows.at[pl.ds(at, HALF), :])
    odd = lax.rem(lax.axis_index("seq"), 2)
    for which, ref in ((0, k_ref), (1, v_ref)):
        for edge_ref, at in ((low_ref, (1 - odd) * (tokens - BLOCK)), (high_ref, odd * (tokens - BLOCK))):
            start = pl.multiple_of(at, BLOCK)
            begin(edges, ref.at[pl.ds(start, BLOCK), :], edge_ref.at[which])
    wanted = random_ref[...]

    def mark(j, carry):
        within = wanted - j * blocks
        mine = jnp.logical_and(within >= 0, within < blocks)
        top = jnp.max(jnp.where(mine, within, -1).astype(jnp.float32))
        out_ref[j, :MARKS, :] = jnp.full((MARKS, DH), top, jnp.float32).astype(jnp.bfloat16)
        return carry

    lax.fori_loop(0, peers, mark, 0, unroll=min(peers, 8))
    for b in range(blocks):
        for r in range(R):
            owners[b * R + r] = lax.div(random_blocks[r, b], blocks)
    for copy in copies:
        copy.wait()
    out_ref[:slices, MARKS:, :] = rows[...].reshape(slices, size, DH)
    if slices < peers:
        out_ref[slices:, MARKS:, :] = jnp.zeros((peers - slices, size, DH), jnp.bfloat16)
    for copy in edges:
        copy.wait()


def serve_kernel(global_blocks, asked_ref, k_ref, v_ref, out_ref, requested_ref, sems):
    blocks = k_ref.shape[0] // BLOCK
    core, _ = places()
    peers = out_ref.shape[0]
    many = min(peers, 8)
    slices, size = glob_slices(peers)

    def copy(j, start, which, ref):
        return pltpu.make_async_copy(
            ref.at[pl.ds(start, HALF), :],
            out_ref.at[j, pl.ds(which * HALF, HALF), :],
            sems.at[j, which],
        )

    def begin(j, carry):
        wanted = jnp.max(asked_ref[j, :MARKS, :].astype(jnp.float32)).astype(jnp.int32)
        requested_ref[j] = wanted
        start = pl.multiple_of(jnp.clip(wanted, 0, blocks - 1) * BLOCK + core * HALF, HALF)
        copy(j, start, 0, k_ref).start()
        copy(j, start, 1, v_ref).start()
        return carry

    lax.fori_loop(0, peers, begin, 0, unroll=many)
    index = jnp.minimum(lax.axis_index("seq"), slices - 1)
    owner = lax.div(global_blocks[lax.div(index * size, 2 * HALF)], blocks)
    out_ref[:, 2 * HALF :, :] = jnp.broadcast_to(
        asked_ref[owner, MARKS:, :][None], (peers, size, DH)
    )

    def end(j, carry):
        copy(j, 0, 0, k_ref).wait()
        copy(j, 0, 1, v_ref).wait()
        return carry

    lax.fori_loop(0, peers, end, 0, unroll=many)


def split_kernel(count, keep_ref, got_ref, out_ref, *send_refs):
    share = out_ref.shape[2]
    _, column = places()
    own = pl.ds(pl.multiple_of(column * share, share), share)
    total = keep_ref[:, :, own, :].astype(jnp.float32) + got_ref[:, :, own, :].astype(jnp.float32)
    out_ref[...] = total.astype(out_ref.dtype)
    for m in range(1, count):
        there = pl.ds(pl.multiple_of((column ^ m) * share, share), share)
        send_refs[m - 1][...] = (
            keep_ref[:, :, there, :].astype(jnp.float32) + got_ref[:, :, there, :].astype(jnp.float32)
        ).astype(jnp.bfloat16)


def terms_kernel(keep_ref, *refs):
    *got_refs, terms_ref, low_ref, high_ref = refs
    peers, _, share, _ = terms_ref.shape
    odd = lax.rem(lax.axis_index("seq"), 2) == 1

    def total(slot, n=1):
        x = keep_ref[slot : slot + n].astype(jnp.float32)
        for ref in got_refs:
            x = x + ref[slot : slot + n].astype(jnp.float32)
        return x.astype(jnp.bfloat16)

    terms_ref[:, :2] = total(0, peers)
    glob = total(peers, G).reshape(1, 2 * G, share, DH)
    terms_ref[:, 2:] = jnp.broadcast_to(glob, (peers, 2 * G, share, DH))
    previous = total(peers + G)[0]
    following = total(peers + G + 1)[0]
    low_ref[...] = jnp.where(odd, previous, following)
    high_ref[...] = jnp.where(odd, following, previous)


def settle_kernel(requested, global_blocks, back_ref, low_ref, high_ref, *refs):
    *got_refs, out_ref, acc = refs
    blocks = out_ref.shape[0]
    peers, _, share, _ = back_ref.shape
    seq_index = lax.axis_index("seq")
    acc[...] = sum(ref[...].astype(jnp.float32) for ref in got_refs)
    at_low, at_high = edge_places(blocks)
    acc[jnp.clip(at_low - 1, 0, blocks - 1)] += low_ref[...].astype(jnp.float32)
    acc[jnp.clip(at_high - 1, 0, blocks - 1)] += high_ref[...].astype(jnp.float32)

    def one(j, carry):
        wanted = requested[j]

        @pl.when(wanted >= 0)
        def _():
            acc[wanted] += back_ref[j, :2].astype(jnp.float32)

        return carry

    lax.fori_loop(0, peers, one, 0)
    for j in range(G):

        @pl.when(lax.div(global_blocks[j], blocks) == seq_index)
        def _():
            rows = back_ref[:, 2 + 2 * j : 4 + 2 * j].astype(jnp.float32)
            acc[lax.rem(global_blocks[j], blocks)] += jnp.sum(rows, axis=0)

    out_ref[...] = acc[...].astype(jnp.bfloat16)


def join_kernel(count, *refs):
    *got_refs, dk_ref, dv_ref, dk, dv = refs
    blocks, _, share, _ = got_refs[0].shape
    core, column = places()
    for m in range(count):
        for c in range(2):
            at = (core ^ c) * HALF + (column ^ m) * share
            rows = pl.ds(pl.multiple_of(at, share), share)
            ref = got_refs[2 * m + c]
            dk[:, rows, :] = ref[:, 0]
            dv[:, rows, :] = ref[:, 1]
    dk_ref[...] = dk[...].reshape(dk_ref.shape)
    dv_ref[...] = dv[...].reshape(dv_ref.shape)


def edge_places(blocks):
    odd = lax.rem(lax.axis_index("seq"), 2)
    return (1 - odd) * (blocks + 1), odd * (blocks + 1)


def fill_window(k_ref, v_ref, low_ref, high_ref, k_all, v_all):
    rows = k_ref.shape[0]
    low, high = (pl.ds(pl.multiple_of(i * BLOCK, BLOCK), BLOCK) for i in edge_places(rows // BLOCK))
    for to, own, which in ((k_all, k_ref, 0), (v_all, v_ref, 1)):
        to[low, :] = low_ref[which]
        to[high, :] = high_ref[which]
        to[BLOCK : BLOCK + rows] = own[...]


def near_kernel(q_ref, g_ref, k_ref, v_ref, low_ref, high_ref, st_ref, k_all, v_all):
    step = pl.program_id(0)
    blocks = k_ref.shape[0] // BLOCK
    seq_index = lax.axis_index("seq")
    per = st_ref.shape[0]

    @pl.when(step == 0)
    def _():
        fill_window(k_ref, v_ref, low_ref, high_ref, k_all, v_all)

    for u in range(per):
        b = step * per + u
        q = stack_heads(q_ref, u)
        g = stack_heads(g_ref, u)
        no_left = jnp.logical_and(seq_index == 0, b == 0)
        no_right = jnp.logical_and(seq_index == lax.axis_size("seq") - 1, b == blocks - 1)
        biases = (jnp.where(no_left, MASKED, 0.0), None, jnp.where(no_right, MASKED, 0.0))
        for w in range(WINDOW):
            rows = pl.ds(pl.multiple_of((b + w) * BLOCK, BLOCK), BLOCK)
            top, _, _, l, d = panel(k_all[rows, :], v_all[rows, :], q, g)
            if biases[w] is not None:
                top = top + biases[w]
            st_ref[u, w : w + 1] = top
            st_ref[u, WINDOW + w : WINDOW + w + 1] = jnp.sum(l, axis=0, keepdims=True)
            st_ref[u, 2 * WINDOW + w : 2 * WINDOW + w + 1] = jnp.sum(d, axis=0, keepdims=True)


def far_kernel(
    random_blocks, q_ref, g_ref, mine_ref, other_ref, st_ref, low_ref, high_ref,
    ds_ref, sums_ref, *refs,
):
    *share_refs, k_all, v_all, acc, e_all, dp_all, ds_all, fd_ref, out_sems, sums_sem = refs
    blocks = q_ref.shape[0] // BLOCK
    peers = mine_ref.shape[0]
    core, column = places()
    own, opp = pl.ds(core * HALF, HALF), pl.ds((1 - core) * HALF, HALF)
    slices, size = glob_slices(peers)

    def at(b):
        return pl.ds(pl.multiple_of(b * BLOCK, BLOCK), BLOCK)

    def put(b):
        return pltpu.make_async_copy(ds_all.at[b], ds_ref.at[b], out_sems.at[b])

    for to, which in ((k_all, 0), (v_all, 1)):
        rows = slice(which * HALF, (which + 1) * HALF)
        to[:peers, own, :] = mine_ref[:, rows, :]
        to[:peers, opp, :] = other_ref[:, rows, :]
    for i in range(slices):
        unit, offset = divmod(i * size, HALF)
        to = (k_all, v_all)[unit % 2]
        slot = peers + unit // 2
        to[slot, pl.ds(pl.multiple_of(core * HALF + offset, MARKS), size), :] = mine_ref[i, 2 * HALF :, :]
        to[slot, pl.ds(pl.multiple_of((1 - core) * HALF + offset, MARKS), size), :] = other_ref[i, 2 * HALF :, :]
    acc[...] = jnp.zeros_like(acc)

    def heads(ref, b):
        rows = ref[at(b), :]
        return jnp.concatenate(
            [rows[:, h * DH : (h + 1) * DH] for h in range(rows.shape[1] // DH)], axis=0
        )

    def slots_of(b):
        return [lax.div(random_blocks[r, b], blocks) for r in range(R)] + [peers + j for j in range(G)]

    def work(new, new_slot, old, old_slot, stats):
        if new is not None:
            q1, g1, slots1 = heads(q_ref, new), heads(g_ref, new), slots_of(new)
        if old is not None:
            q2, g2, slots2 = heads(q_ref, old), heads(g_ref, old), slots_of(old)
        tops, ls, dd = [], [], []

        def dots(i):
            return mm(k_all[slots1[i]], q1, NT), mm(v_all[slots1[i]], g1, NT)

        if new is not None:
            ready = dots(0)
        for i in range(FAR):
            rows = slice(i * BLOCK, (i + 1) * BLOCK)
            if new is not None:
                s, dp = ready
                if i + 1 < FAR:
                    ready = dots(i + 1)
            if old is not None:
                p = e_all[old_slot, rows] * stats[i]
                ds = (p * (dp_all[old_slot, rows] - stats[FAR])).astype(jnp.bfloat16)
                ds_all[old, rows] = ds
            if new is not None:
                top = jnp.max(s, axis=0, keepdims=True) * SCALE
                e = jnp.exp2(s * SCALE - top)
                e_all[new_slot, rows] = e
                dp_all[new_slot, rows] = dp
                tops.append(top)
                ls.append(fold(e))
                dd.append(fold(e * dp))
            if old is not None:
                acc[slots2[i], 0] += mm(ds, q2, NN)
                acc[slots2[i], 1] += mm(p.astype(jnp.bfloat16), g2, NN)
        if old is not None:
            put(old).start()
        if new is None:
            return None
        near = [[st_ref[new, i * WINDOW + w : i * WINDOW + w + 1] for w in range(WINDOW)] for i in range(3)]
        top = functools.reduce(jnp.maximum, near[0] + tops)
        near_weight = [jnp.exp2(t - top) for t in near[0]]
        weight = [jnp.exp2(t - top) for t in tops]
        l = jnp.sum(sum(w * x for w, x in zip(weight, ls)), axis=0, keepdims=True)
        d = jnp.sum(sum(w * x for w, x in zip(weight, dd)), axis=0, keepdims=True)
        l = l + sum(w * x for w, x in zip(near_weight, near[1]))
        d = d + sum(w * x for w, x in zip(near_weight, near[2]))
        inv = 1.0 / l
        delta = d * inv
        for w in range(WINDOW):
            fd_ref[new, w : w + 1] = near[0][w]
            fd_ref[new, WINDOW + w : WINDOW + w + 1] = near_weight[w] * inv
        fd_ref[new, 2 * WINDOW : 2 * WINDOW + 1] = delta
        return tuple(w * inv for w in weight) + (delta,)

    turn = math.gcd(blocks, 4)

    def several(t, stats, last=False):
        for j in range(turn - last):
            b = t * turn + j
            stats = work(b + 1, (j + 1) % 2, b, j % 2, stats)
        return stats

    stats = work(0, 0, None, None, None)
    stats = lax.fori_loop(0, blocks // turn - 1, several, stats)
    stats = several(blocks // turn - 1, stats, True)
    sums = pltpu.make_async_copy(fd_ref, sums_ref.at[pl.ds(0, blocks)], sums_sem)
    sums.start()
    work(None, None, blocks - 1, 1, stats)

    for slot, w, b, swap in ((peers + G, 0, 0, 1), (peers + G + 1, WINDOW - 1, blocks - 1, 0)):
        odd = lax.rem(lax.axis_index("seq"), 2) == swap
        q, g = heads(q_ref, b), heads(g_ref, b)
        s = mm(jnp.where(odd, low_ref[0], high_ref[0]), q, NT)
        dp = mm(jnp.where(odd, low_ref[1], high_ref[1]), g, NT)
        p = jnp.exp2(s * SCALE - jnp.max(s, axis=0, keepdims=True) * SCALE)
        p = p * fd_ref[b, WINDOW + w : WINDOW + w + 1]
        ds = (p * (dp - fd_ref[b, 2 * WINDOW : 2 * WINDOW + 1])).astype(jnp.bfloat16)
        acc[slot, 0] = mm(ds, q, NN)
        acc[slot, 1] = mm(p.astype(jnp.bfloat16), g, NN)

    share = share_refs[0].shape[2]
    for m, ref in enumerate(share_refs):
        start = (core ^ (m & 1)) * HALF + (column ^ (m >> 1)) * share
        rows = pl.ds(pl.multiple_of(start, share), share)
        for which, f in ((0, FACTOR), (1, 1.0)):
            ref[:, which] = (acc[:, which, rows, :] * f).astype(ref.dtype)
    sums.wait()
    for b in range(blocks):
        put(b).wait()


def close_kernel(
    q_ref, g_ref, k_ref, v_ref, low_ref, high_ref, fd_ref, ds_ref, keep_ref, send_ref, k_all, v_all, acc
):
    step = pl.program_id(0)
    per = fd_ref.shape[0]
    core, _ = places()
    own, opp = pl.ds(core * HALF, HALF), pl.ds((1 - core) * HALF, HALF)

    @pl.when(step == 0)
    def _():
        fill_window(k_ref, v_ref, low_ref, high_ref, k_all, v_all)
        acc[...] = jnp.zeros_like(acc)

    for u in range(per):
        b = step * per + u
        q = stack_heads(q_ref, u)
        g = stack_heads(g_ref, u)
        delta = fd_ref[u, 2 * WINDOW : 2 * WINDOW + 1]
        ds, pb = [], []
        for w in range(WINDOW):
            rows = pl.ds(pl.multiple_of((b + w) * BLOCK, BLOCK), BLOCK)
            s = mm(k_all[rows, :], q, NT)
            dp = mm(v_all[rows, :], g, NT)
            top = fd_ref[u, w : w + 1]
            top = jnp.where(top < MASKED / 2, 0.0, top)
            p = jnp.exp2(s * SCALE - top) * fd_ref[u, WINDOW + w : WINDOW + w + 1]
            ds.append((p * (dp - delta)).astype(jnp.bfloat16))
            pb.append(p.astype(jnp.bfloat16))
        ds = jnp.concatenate(ds, axis=0)
        pb = jnp.concatenate(pb, axis=0)
        ds_ref[u] = ds
        shape = (WINDOW, BLOCK, DH)
        acc[pl.ds(b, WINDOW), 0] += mm(ds, q, NN).reshape(shape)
        acc[pl.ds(b, WINDOW), 1] += mm(pb, g, NN).reshape(shape)

    @pl.when(step == pl.num_programs(0) - 1)
    def _():
        for which, f in ((0, FACTOR), (1, 1.0)):
            keep_ref[:, which] = (acc[1:-1, which, own, :] * f).astype(keep_ref.dtype)
            send_ref[:, which] = (acc[1:-1, which, opp, :] * f).astype(jnp.bfloat16)


def queries_kernel(
    first, owners, k_ref, low_ref, high_ref, mine_ref, other_ref, dsw_ref, dsf_ref, *refs
):
    *_, dq_ref, k_all, kt_all = refs
    blocks = k_ref.shape[0] // BLOCK
    peers = mine_ref.shape[0]
    per = dsw_ref.shape[0]
    core, _ = places()
    step = pl.program_id(0)
    first_random = blocks + 2
    first_global = first_random + peers
    slices, size = glob_slices(peers)

    @pl.when(step == 0)
    def _():
        at_low, at_high = edge_places(blocks)
        k_all[at_low] = low_ref[0]
        k_all[at_high] = high_ref[0]
        k_all[1 : blocks + 1] = k_ref[...].reshape(blocks, BLOCK, DH)
        for ref, c in ((mine_ref, core), (other_ref, 1 - core)):
            k_all[first_random:first_global, pl.ds(c * HALF, HALF), :] = ref[:, :HALF, :]
            for i in range(slices):
                unit, offset = divmod(i * size, HALF)
                if unit % 2 == 0:
                    rows = pl.ds(pl.multiple_of(c * HALF + offset, MARKS), size)
                    k_all[first_global + unit // 2, rows, :] = ref[i, 2 * HALF :, :]

        def turn(j, carry):
            kt_all[j] = k_all[j].T
            return carry

        lax.fori_loop(0, first_global + G, turn, 0, unroll=4)

    for u in range(per):
        b = first + step * per + u
        panels = [b + w for w in range(WINDOW)]
        panels += [first_random + owners[b * R + r] for r in range(R)]
        panels += [first_global + j for j in range(G)]
        turned = [kt_all[i] for i in panels]
        dqt = mm(jnp.concatenate(turned[:WINDOW], axis=1), dsw_ref[u], NN)
        dqt = (dqt + mm(jnp.concatenate(turned[WINDOW:], axis=1), dsf_ref[u], NN)) * FACTOR
        for h in range(dq_ref.shape[1] // DH):
            dq_ref[u * BLOCK : (u + 1) * BLOCK, h * DH : (h + 1) * DH] = (
                dqt[:, h * BLOCK : (h + 1) * BLOCK].T.astype(jnp.bfloat16)
            )


def whole(a):
    return pl.BlockSpec(a.shape, lambda i, *_: (0,) * len(a.shape))


def per_block(per, *rest):
    return pl.BlockSpec((per,) + rest, lambda i, *_: (i,) + (0,) * len(rest))


def partners(size, stride):
    return [(i, i ^ stride) for i in range(size)]


def body(query_vectors, key_vectors, value_vectors, output_grad, random_blocks, global_blocks):
    seq_count = lax.axis_size("seq")
    head_count = lax.axis_size("head")
    rows_dev, columns = query_vectors.shape
    blocks = rows_dev // BLOCK
    per = math.gcd(blocks, 4)
    steps = blocks // per
    lanes = columns // DH * BLOCK
    bf16 = jnp.bfloat16
    f32 = jnp.float32
    sds = jax.ShapeDtypeStruct
    core_pairs = partners(head_count, 1)
    limit = (16 + seq_count // 2) * MIB
    params = pltpu.CompilerParams(dimension_semantics=("arbitrary",), vmem_limit_bytes=limit)
    unit = 2 * blocks * lanes * BLOCK * DH

    vmem = pl.BlockSpec(memory_space=pltpu.VMEM)
    smem = pl.BlockSpec(memory_space=pltpu.SMEM)
    hbm = pl.BlockSpec(memory_space=pltpu.HBM)
    small = pltpu.CompilerParams(vmem_limit_bytes=limit)
    large = pltpu.CompilerParams(vmem_limit_bytes=60 * MIB)
    share = BLOCK // head_count
    columns_count = head_count // 2

    edge = (2, BLOCK, DH)
    _, size = glob_slices(seq_count)
    asking, to_low, to_high, owners = pl.pallas_call(
        ask_kernel,
        out_shape=(
            sds((seq_count, MARKS + size, DH), bf16),
            sds(edge, bf16),
            sds(edge, bf16),
            sds((blocks * R,), jnp.int32),
        ),
        in_specs=[smem, smem, vmem, hbm, hbm],
        out_specs=(vmem, vmem, vmem, smem),
        scratch_shapes=[
            pltpu.VMEM((2 * G * HALF, DH), bf16),
            pltpu.SemaphoreType.DMA((2 * G + 4,)),
        ],
        compiler_params=large,
        name="ask",
    )(global_blocks, random_blocks.T, random_blocks.T, key_vectors, value_vectors)
    asked = lax.all_to_all(asking, "seq", split_axis=0, concat_axis=0, tiled=True)

    low_pairs = [(i, i ^ 1) for i in range(seq_count)]
    high_pairs = [(i, i + 1 if i % 2 else i - 1) for i in range(1, seq_count - 1)]
    low = lax.ppermute(to_low, "seq", low_pairs)
    high = lax.ppermute(to_high, "seq", high_pairs)
    asked, low, high = lax.optimization_barrier((asked, low, high))

    served, requested = pl.pallas_call(
        serve_kernel,
        out_shape=(sds((seq_count, 2 * HALF + size, DH), bf16), sds((seq_count,), jnp.int32)),
        in_specs=[smem, vmem, hbm, hbm],
        out_specs=(vmem, smem),
        scratch_shapes=[pltpu.SemaphoreType.DMA((seq_count, 2))],
        compiler_params=large,
        name="serve",
    )(global_blocks, asked, key_vectors, value_vectors)
    mine = lax.all_to_all(served, "seq", split_axis=0, concat_axis=0, tiled=True)

    rows_spec = pl.BlockSpec((per * BLOCK, columns), lambda i, *_: (i, 0))
    st_spec = per_block(per, 2 * FOLD, lanes)
    fd_spec = per_block(per, FOLD, lanes)
    nearby = (key_vectors, value_vectors, low, high)
    window_scratch = [pltpu.VMEM(((blocks + 2) * BLOCK, DH), bf16)] * 2
    st = pl.pallas_call(
        near_kernel,
        out_shape=sds((blocks, 2 * FOLD, lanes), f32),
        grid=(steps,),
        in_specs=[rows_spec, rows_spec] + [whole(a) for a in nearby],
        out_specs=st_spec,
        scratch_shapes=window_scratch,
        compiler_params=params,
        cost_estimate=pl.CostEstimate(
            flops=2 * WINDOW * unit, bytes_accessed=4 * MIB, transcendentals=blocks * lanes * WINDOW * BLOCK
        ),
        name="near",
    )(query_vectors, output_grad, *nearby)
    mine, st = lax.optimization_barrier((mine, st))
    queries_in, grads_in, mine = lax.optimization_barrier((query_vectors, output_grad, mine))
    here = lax.axis_index("seq") < seq_count
    queries_in = jnp.where(here, queries_in, 0).astype(bf16)
    grads_in = jnp.where(here, grads_in, 0).astype(bf16)
    other = lax.ppermute(mine, "head", core_pairs)

    slots = seq_count + G + 2
    piece = (slots, 2, share, DH)
    dsf, fd, *pieces = pl.pallas_call(
        far_kernel,
        out_shape=(
            sds((blocks * SPARE, FAR * BLOCK, lanes), bf16),
            sds((blocks * SPARE * 20, FOLD, lanes), f32),
        )
        + (sds(piece, bf16),) * head_count,
        in_specs=[smem] + [vmem] * 7,
        out_specs=(hbm, hbm) + (vmem,) * head_count,
        scratch_shapes=[pltpu.VMEM((seq_count + G, BLOCK, DH), bf16)] * 2
        + [pltpu.VMEM((slots, 2, BLOCK, DH), f32)]
        + [pltpu.VMEM((2, FAR * BLOCK, lanes), f32)] * 2
        + [
            pltpu.VMEM((blocks, FAR * BLOCK, lanes), bf16),
            pltpu.VMEM((blocks, FOLD, lanes), f32),
            pltpu.SemaphoreType.DMA((blocks,)),
            pltpu.SemaphoreType.DMA(()),
        ],
        compiler_params=pltpu.CompilerParams(vmem_limit_bytes=max(limit, 42 * MIB)),
        cost_estimate=pl.CostEstimate(
            flops=5 * FAR * unit, bytes_accessed=8 * MIB, transcendentals=blocks * lanes * FAR * BLOCK
        ),
        name="far",
    )(random_blocks.T, queries_in, grads_in, mine, other, st, low, high)

    piece_w = (blocks, 2, HALF, DH)
    near_spec = per_block(per, WINDOW * BLOCK, lanes)
    far_spec = per_block(per, FAR * BLOCK, lanes)
    dsw, keep_w, send_w = pl.pallas_call(
        close_kernel,
        out_shape=(sds((blocks, WINDOW * BLOCK, lanes), bf16), sds(piece_w, bf16), sds(piece_w, bf16)),
        grid=(steps,),
        in_specs=[rows_spec, rows_spec] + [whole(a) for a in nearby] + [fd_spec],
        out_specs=(near_spec, whole(sds(piece_w, bf16)), whole(sds(piece_w, bf16))),
        scratch_shapes=window_scratch + [pltpu.VMEM((blocks + 2, 2, BLOCK, DH), f32)],
        compiler_params=large,
        cost_estimate=pl.CostEstimate(flops=4 * WINDOW * unit, bytes_accessed=8 * MIB, transcendentals=0),
        name="close",
    )(query_vectors, output_grad, *nearby, fd)

    others = [m << 1 for m in range(1, columns_count)]

    def reduced(kept, sent, name, dtype):
        got = lax.ppermute(sent, "head", core_pairs)
        part = (kept.shape[0], 2, share, DH)
        home, *away = pl.pallas_call(
            functools.partial(split_kernel, columns_count),
            out_shape=(sds(part, dtype),) + (sds(part, bf16),) * len(others),
            in_specs=[vmem, vmem],
            out_specs=(vmem,) * (1 + len(others)),
            compiler_params=small,
            name=name,
        )(kept, got)
        return [home] + [
            lax.ppermute(a, "head", partners(head_count, m)) for a, m in zip(away, others)
        ]

    parts = pieces[:1] + [
        lax.ppermute(pieces[m], "head", partners(head_count, m)) for m in range(1, head_count)
    ]
    parts[-1], send_w = lax.optimization_barrier((parts[-1], send_w))
    terms, to_low, to_high = pl.pallas_call(
        terms_kernel,
        out_shape=(
            sds((seq_count, 2 + 2 * G, share, DH), bf16),
            sds((2, share, DH), bf16),
            sds((2, share, DH), bf16),
        ),
        in_specs=[vmem] * len(parts),
        out_specs=(vmem,) * 3,
        compiler_params=small,
        name="terms",
    )(*parts)
    parts_w = reduced(keep_w, send_w, "split_close", bf16)
    dsw, to_low = lax.optimization_barrier((dsw, to_low))

    def queries(half, dsw, done):
        shift = half * (steps // 2)
        part = lambda *rest: pl.BlockSpec((per,) + rest, lambda i, *_: (i + shift,) + (0,) * len(rest))
        return pl.pallas_call(
            functools.partial(queries_kernel, shift * per),
            out_shape=sds(query_vectors.shape, bf16),
            grid_spec=pltpu.PrefetchScalarGridSpec(
                num_scalar_prefetch=1,
                grid=(steps // 2,),
                in_specs=[whole(a) for a in (key_vectors, low, high, mine, other)]
                + [part(WINDOW * BLOCK, lanes), part(FAR * BLOCK, lanes)]
                + [hbm] * len(done),
                out_specs=pl.BlockSpec((per * BLOCK, columns), lambda i, *_: (i + shift, 0)),
                scratch_shapes=[pltpu.VMEM((blocks + 2 + seq_count + G, BLOCK, DH), bf16)] * 2,
            ),
            input_output_aliases={8: 0} if done else {},
            compiler_params=large,
            cost_estimate=pl.CostEstimate(
                flops=LISTED * unit // 2, bytes_accessed=4 * MIB, transcendentals=0
            ),
            name="queries",
        )(owners, key_vectors, low, high, mine, other, dsw, dsf, *done)

    query_grad = queries(0, dsw, ())
    back = lax.all_to_all(terms, "seq", split_axis=0, concat_axis=0, tiled=True)
    from_low = lax.ppermute(to_low, "seq", low_pairs)
    from_high = lax.ppermute(to_high, "seq", high_pairs)
    back, query_grad = lax.optimization_barrier((back, query_grad))
    held = pl.pallas_call(
        settle_kernel,
        out_shape=sds((blocks, 2, share, DH), bf16),
        in_specs=[smem, smem] + [vmem] * (3 + len(parts_w)),
        out_specs=vmem,
        scratch_shapes=[pltpu.VMEM((blocks, 2, share, DH), f32)],
        compiler_params=small,
        name="settle",
    )(requested, global_blocks, back, from_low, from_high, *parts_w)

    dsw, query_grad, held = lax.optimization_barrier((dsw, query_grad, held))
    query_grad = queries(1, dsw, (query_grad,))
    rows = [held] + [lax.ppermute(held, "head", partners(head_count, m)) for m in others]
    rows[-1], query_grad = lax.optimization_barrier((rows[-1], query_grad))
    pieces = []
    for a in rows:
        pieces += [a, lax.ppermute(a, "head", core_pairs)]
    key_grad, value_grad = pl.pallas_call(
        functools.partial(join_kernel, columns_count),
        out_shape=(sds(key_vectors.shape, bf16),) * 2,
        in_specs=[vmem] * len(pieces),
        out_specs=(vmem, vmem),
        scratch_shapes=[pltpu.VMEM((blocks, BLOCK, DH), bf16)] * 2,
        compiler_params=small,
        name="join",
    )(*pieces)
    return query_grad, key_grad, value_grad


def solution(mesh):
    return jax.shard_map(
        body,
        mesh=mesh,
        in_specs=(
            P("seq", "head"),
            P("seq", None),
            P("seq", None),
            P("seq", "head"),
            P("seq", None),
            P(),
        ),
        out_specs=(P("seq", "head"), P("seq", None), P("seq", None)),
        check_vma=False,
    )
```

```python
import functools
import math

import jax
import jax.numpy as jnp
from jax import lax
from jax.experimental import pallas as pl
from jax.experimental.pallas import tpu as pltpu
from jax.sharding import PartitionSpec as P

DH = 128
BLOCK = 128
HALF = BLOCK // 2
R = 3
G = 2
WINDOW = 3
FAR = R + G
LISTED = WINDOW + FAR
MIB = 1024 * 1024
MASKED = -1e30
FACTOR = float(DH) ** -0.5
SCALE = FACTOR * math.log2(math.e)
FOLD = 8
SPARE = 5
MARKS = 16

NT = (((1,), (1,)), ((), ()))
NN = (((1,), (0,)), ((), ()))
TN = (((0,), (0,)), ((), ()))


def mm(a, b, dims):
    return lax.dot_general(a, b, dims, preferred_element_type=jnp.float32)


def stack_heads(ref, u):
    rows = ref[u * BLOCK : (u + 1) * BLOCK, :]
    return jnp.concatenate(
        [rows[:, h * DH : (h + 1) * DH] for h in range(rows.shape[1] // DH)], axis=0
    )


def fold(x):
    return jnp.sum(x.reshape(x.shape[0] // FOLD, FOLD, x.shape[1]), axis=0)


def panel(k, v, q, g):
    s = mm(k, q, NT)
    dp = mm(v, g, NT)
    top = jnp.max(s, axis=0, keepdims=True) * SCALE
    e = jnp.exp2(s * SCALE - top)
    return top, e, dp, fold(e), fold(e * dp)


def places():
    head_index = lax.axis_index("head")
    return lax.rem(head_index, 2), lax.div(head_index, 2)


def glob_slices(peers):
    rows = 2 * G * HALF
    size = max(MARKS, rows // peers)
    return rows // size, size


def ask_kernel(
    global_blocks, random_ref, k_ref, v_ref, out_ref, low_ref, high_ref, rows, sems
):
    tokens = k_ref.shape[0]
    blocks = tokens // BLOCK
    peers = out_ref.shape[0]
    core, _ = places()
    slices, size = glob_slices(peers)
    edges, copies = [], []

    def begin(group, src, dst):
        group.append(pltpu.make_async_copy(src, dst, sems.at[len(edges) + len(copies)]))
        group[-1].start()

    for j in range(G):
        start = lax.rem(global_blocks[j], blocks) * BLOCK + core * HALF
        start = pl.multiple_of(start, HALF)
        for which, ref in ((0, k_ref), (1, v_ref)):
            at = (2 * j + which) * HALF
            begin(copies, ref.at[pl.ds(start, HALF), :], rows.at[pl.ds(at, HALF), :])
    odd = lax.rem(lax.axis_index("seq"), 2)
    for which, ref in ((0, k_ref), (1, v_ref)):
        for edge_ref, at in ((low_ref, (1 - odd) * (tokens - BLOCK)), (high_ref, odd * (tokens - BLOCK))):
            start = pl.multiple_of(at, BLOCK)
            begin(edges, ref.at[pl.ds(start, BLOCK), :], edge_ref.at[which])
    wanted = random_ref[...]

    def mark(j, carry):
        within = wanted - j * blocks
        mine = jnp.logical_and(within >= 0, within < blocks)
        top = jnp.max(jnp.where(mine, within, -1).astype(jnp.float32))
        out_ref[j, :MARKS, :] = jnp.full((MARKS, DH), top, jnp.float32).astype(jnp.bfloat16)
        return carry

    lax.fori_loop(0, peers, mark, 0, unroll=min(peers, 8))
    for copy in copies:
        copy.wait()
    out_ref[:slices, MARKS:, :] = rows[...].reshape(slices, size, DH)
    if slices < peers:
        out_ref[slices:, MARKS:, :] = jnp.zeros((peers - slices, size, DH), jnp.bfloat16)
    for copy in edges:
        copy.wait()


def serve_kernel(global_blocks, asked_ref, k_ref, v_ref, out_ref, requested_ref, sems):
    blocks = k_ref.shape[0] // BLOCK
    core, _ = places()
    peers = out_ref.shape[0]
    many = min(peers, 8)
    slices, size = glob_slices(peers)

    def copy(j, start, which, ref):
        return pltpu.make_async_copy(
            ref.at[pl.ds(start, HALF), :],
            out_ref.at[j, pl.ds(which * HALF, HALF), :],
            sems.at[j, which],
        )

    def begin(j, carry):
        wanted = jnp.max(asked_ref[j, :MARKS, :].astype(jnp.float32)).astype(jnp.int32)
        requested_ref[j] = wanted
        start = pl.multiple_of(jnp.clip(wanted, 0, blocks - 1) * BLOCK + core * HALF, HALF)
        copy(j, start, 0, k_ref).start()
        copy(j, start, 1, v_ref).start()
        return carry

    lax.fori_loop(0, peers, begin, 0, unroll=many)
    index = jnp.minimum(lax.axis_index("seq"), slices - 1)
    owner = lax.div(global_blocks[lax.div(index * size, 2 * HALF)], blocks)
    out_ref[:, 2 * HALF :, :] = jnp.broadcast_to(
        asked_ref[owner, MARKS:, :][None], (peers, size, DH)
    )

    def end(j, carry):
        copy(j, 0, 0, k_ref).wait()
        copy(j, 0, 1, v_ref).wait()
        return carry

    lax.fori_loop(0, peers, end, 0, unroll=many)


def split_kernel(count, keep_ref, got_ref, out_ref, *send_refs):
    share = out_ref.shape[2]
    _, column = places()
    own = pl.ds(pl.multiple_of(column * share, share), share)
    total = keep_ref[:, :, own, :].astype(jnp.float32) + got_ref[:, :, own, :].astype(jnp.float32)
    out_ref[...] = total.astype(out_ref.dtype)
    for m in range(1, count):
        there = pl.ds(pl.multiple_of((column ^ m) * share, share), share)
        send_refs[m - 1][...] = (
            keep_ref[:, :, there, :].astype(jnp.float32) + got_ref[:, :, there, :].astype(jnp.float32)
        ).astype(jnp.bfloat16)


def terms_kernel(keep_ref, *refs):
    *got_refs, terms_ref, low_ref, high_ref = refs
    peers, _, share, _ = terms_ref.shape
    odd = lax.rem(lax.axis_index("seq"), 2) == 1

    def total(slot, n=1):
        x = keep_ref[slot : slot + n].astype(jnp.float32)
        for ref in got_refs:
            x = x + ref[slot : slot + n].astype(jnp.float32)
        return x.astype(jnp.bfloat16)

    terms_ref[:, :2] = total(0, peers)
    glob = total(peers, G).reshape(1, 2 * G, share, DH)
    terms_ref[:, 2:] = jnp.broadcast_to(glob, (peers, 2 * G, share, DH))
    previous = total(peers + G)[0]
    following = total(peers + G + 1)[0]
    low_ref[...] = jnp.where(odd, previous, following)
    high_ref[...] = jnp.where(odd, following, previous)


def settle_kernel(requested, global_blocks, back_ref, low_ref, high_ref, *refs):
    *got_refs, out_ref, acc = refs
    blocks = out_ref.shape[0]
    peers, _, share, _ = back_ref.shape
    seq_index = lax.axis_index("seq")
    acc[...] = sum(ref[...].astype(jnp.float32) for ref in got_refs)
    at_low, at_high = edge_places(blocks)
    acc[jnp.clip(at_low - 1, 0, blocks - 1)] += low_ref[...].astype(jnp.float32)
    acc[jnp.clip(at_high - 1, 0, blocks - 1)] += high_ref[...].astype(jnp.float32)

    def one(j, carry):
        wanted = requested[j]

        @pl.when(wanted >= 0)
        def _():
            acc[wanted] += back_ref[j, :2].astype(jnp.float32)

        return carry

    lax.fori_loop(0, peers, one, 0)
    for j in range(G):

        @pl.when(lax.div(global_blocks[j], blocks) == seq_index)
        def _():
            rows = back_ref[:, 2 + 2 * j : 4 + 2 * j].astype(jnp.float32)
            acc[lax.rem(global_blocks[j], blocks)] += jnp.sum(rows, axis=0)

    out_ref[...] = acc[...].astype(jnp.bfloat16)


def join_kernel(count, *refs):
    *got_refs, dk_ref, dv_ref, dk, dv = refs
    blocks, _, share, _ = got_refs[0].shape
    core, column = places()
    for m in range(count):
        for c in range(2):
            at = (core ^ c) * HALF + (column ^ m) * share
            rows = pl.ds(pl.multiple_of(at, share), share)
            ref = got_refs[2 * m + c]
            dk[:, rows, :] = ref[:, 0]
            dv[:, rows, :] = ref[:, 1]
    dk_ref[...] = dk[...].reshape(dk_ref.shape)
    dv_ref[...] = dv[...].reshape(dv_ref.shape)


def edge_places(blocks):
    odd = lax.rem(lax.axis_index("seq"), 2)
    return (1 - odd) * (blocks + 1), odd * (blocks + 1)


def fill_window(k_ref, v_ref, low_ref, high_ref, k_all, v_all):
    rows = k_ref.shape[0]
    low, high = (pl.ds(pl.multiple_of(i * BLOCK, BLOCK), BLOCK) for i in edge_places(rows // BLOCK))
    for to, own, which in ((k_all, k_ref, 0), (v_all, v_ref, 1)):
        to[low, :] = low_ref[which]
        to[high, :] = high_ref[which]
        to[BLOCK : BLOCK + rows] = own[...]


def near_kernel(q_ref, g_ref, k_ref, v_ref, low_ref, high_ref, st_ref, k_all, v_all):
    step = pl.program_id(0)
    blocks = k_ref.shape[0] // BLOCK
    seq_index = lax.axis_index("seq")
    per = st_ref.shape[0]

    @pl.when(step == 0)
    def _():
        fill_window(k_ref, v_ref, low_ref, high_ref, k_all, v_all)

    for u in range(per):
        b = step * per + u
        q = stack_heads(q_ref, u)
        g = stack_heads(g_ref, u)
        no_left = jnp.logical_and(seq_index == 0, b == 0)
        no_right = jnp.logical_and(seq_index == lax.axis_size("seq") - 1, b == blocks - 1)
        biases = (jnp.where(no_left, MASKED, 0.0), None, jnp.where(no_right, MASKED, 0.0))
        for w in range(WINDOW):
            rows = pl.ds(pl.multiple_of((b + w) * BLOCK, BLOCK), BLOCK)
            top, _, _, l, d = panel(k_all[rows, :], v_all[rows, :], q, g)
            if biases[w] is not None:
                top = top + biases[w]
            st_ref[u, w : w + 1] = top
            st_ref[u, WINDOW + w : WINDOW + w + 1] = jnp.sum(l, axis=0, keepdims=True)
            st_ref[u, 2 * WINDOW + w : 2 * WINDOW + w + 1] = jnp.sum(d, axis=0, keepdims=True)


def far_kernel(
    random_blocks, q_ref, g_ref, mine_ref, other_ref, st_ref, low_ref, high_ref,
    ds_ref, sums_ref, *refs,
):
    *share_refs, k_all, v_all, acc, e_all, dp_all, ds_all, fd_ref, out_sems, sums_sem = refs
    blocks = q_ref.shape[0] // BLOCK
    peers = mine_ref.shape[0]
    core, column = places()
    own, opp = pl.ds(core * HALF, HALF), pl.ds((1 - core) * HALF, HALF)
    slices, size = glob_slices(peers)

    def at(b):
        return pl.ds(pl.multiple_of(b * BLOCK, BLOCK), BLOCK)

    def put(b):
        return pltpu.make_async_copy(ds_all.at[b], ds_ref.at[b], out_sems.at[b])

    for to, which in ((k_all, 0), (v_all, 1)):
        rows = slice(which * HALF, (which + 1) * HALF)
        to[:peers, own, :] = mine_ref[:, rows, :]
        to[:peers, opp, :] = other_ref[:, rows, :]
    for i in range(slices):
        unit, offset = divmod(i * size, HALF)
        to = (k_all, v_all)[unit % 2]
        slot = peers + unit // 2
        to[slot, pl.ds(pl.multiple_of(core * HALF + offset, MARKS), size), :] = mine_ref[i, 2 * HALF :, :]
        to[slot, pl.ds(pl.multiple_of((1 - core) * HALF + offset, MARKS), size), :] = other_ref[i, 2 * HALF :, :]
    acc[...] = jnp.zeros_like(acc)

    def heads(ref, b):
        rows = ref[at(b), :]
        return jnp.concatenate(
            [rows[:, h * DH : (h + 1) * DH] for h in range(rows.shape[1] // DH)], axis=0
        )

    def slots_of(b):
        return [lax.div(random_blocks[r, b], blocks) for r in range(R)] + [peers + j for j in range(G)]

    def work(new, new_slot, old, old_slot, stats):
        if new is not None:
            q1, g1, slots1 = heads(q_ref, new), heads(g_ref, new), slots_of(new)
        if old is not None:
            q2, g2, slots2 = heads(q_ref, old), heads(g_ref, old), slots_of(old)
        tops, ls, dd = [], [], []

        def dots(i):
            return mm(k_all[slots1[i]], q1, NT), mm(v_all[slots1[i]], g1, NT)

        if new is not None:
            ready = dots(0)
        for i in range(FAR):
            rows = slice(i * BLOCK, (i + 1) * BLOCK)
            if new is not None:
                s, dp = ready
                if i + 1 < FAR:
                    ready = dots(i + 1)
            if old is not None:
                p = e_all[old_slot, rows] * stats[i]
                ds = (p * (dp_all[old_slot, rows] - stats[FAR])).astype(jnp.bfloat16)
                ds_all[old, rows] = ds
            if new is not None:
                top = jnp.max(s, axis=0, keepdims=True) * SCALE
                e = jnp.exp2(s * SCALE - top)
                e_all[new_slot, rows] = e
                dp_all[new_slot, rows] = dp
                tops.append(top)
                ls.append(fold(e))
                dd.append(fold(e * dp))
            if old is not None:
                acc[slots2[i], 0] += mm(ds, q2, NN)
                acc[slots2[i], 1] += mm(p.astype(jnp.bfloat16), g2, NN)
        if old is not None:
            put(old).start()
        if new is None:
            return None
        near = [[st_ref[new, i * WINDOW + w : i * WINDOW + w + 1] for w in range(WINDOW)] for i in range(3)]
        top = functools.reduce(jnp.maximum, near[0] + tops)
        near_weight = [jnp.exp2(t - top) for t in near[0]]
        weight = [jnp.exp2(t - top) for t in tops]
        l = jnp.sum(sum(w * x for w, x in zip(weight, ls)), axis=0, keepdims=True)
        d = jnp.sum(sum(w * x for w, x in zip(weight, dd)), axis=0, keepdims=True)
        l = l + sum(w * x for w, x in zip(near_weight, near[1]))
        d = d + sum(w * x for w, x in zip(near_weight, near[2]))
        inv = 1.0 / l
        delta = d * inv
        for w in range(WINDOW):
            fd_ref[new, w : w + 1] = near[0][w]
            fd_ref[new, WINDOW + w : WINDOW + w + 1] = near_weight[w] * inv
        fd_ref[new, 2 * WINDOW : 2 * WINDOW + 1] = delta
        return tuple(w * inv for w in weight) + (delta,)

    turn = math.gcd(blocks, 4)

    def several(t, stats, last=False):
        for j in range(turn - last):
            b = t * turn + j
            stats = work(b + 1, (j + 1) % 2, b, j % 2, stats)
        return stats

    stats = work(0, 0, None, None, None)
    stats = lax.fori_loop(0, blocks // turn - 1, several, stats)
    stats = several(blocks // turn - 1, stats, True)
    sums = pltpu.make_async_copy(fd_ref, sums_ref.at[pl.ds(0, blocks)], sums_sem)
    sums.start()
    work(None, None, blocks - 1, 1, stats)

    for slot, w, b, swap in ((peers + G, 0, 0, 1), (peers + G + 1, WINDOW - 1, blocks - 1, 0)):
        odd = lax.rem(lax.axis_index("seq"), 2) == swap
        q, g = heads(q_ref, b), heads(g_ref, b)
        s = mm(jnp.where(odd, low_ref[0], high_ref[0]), q, NT)
        dp = mm(jnp.where(odd, low_ref[1], high_ref[1]), g, NT)
        p = jnp.exp2(s * SCALE - jnp.max(s, axis=0, keepdims=True) * SCALE)
        p = p * fd_ref[b, WINDOW + w : WINDOW + w + 1]
        ds = (p * (dp - fd_ref[b, 2 * WINDOW : 2 * WINDOW + 1])).astype(jnp.bfloat16)
        acc[slot, 0] = mm(ds, q, NN)
        acc[slot, 1] = mm(p.astype(jnp.bfloat16), g, NN)

    share = share_refs[0].shape[2]
    for m, ref in enumerate(share_refs):
        start = (core ^ (m & 1)) * HALF + (column ^ (m >> 1)) * share
        rows = pl.ds(pl.multiple_of(start, share), share)
        for which, f in ((0, FACTOR), (1, 1.0)):
            ref[:, which] = (acc[:, which, rows, :] * f).astype(ref.dtype)
    sums.wait()
    for b in range(blocks):
        put(b).wait()


def close_kernel(
    q_ref, g_ref, k_ref, v_ref, low_ref, high_ref, fd_ref, ds_ref, keep_ref, send_ref, k_all, v_all, acc
):
    step = pl.program_id(0)
    per = fd_ref.shape[0]
    core, _ = places()
    own, opp = pl.ds(core * HALF, HALF), pl.ds((1 - core) * HALF, HALF)

    @pl.when(step == 0)
    def _():
        fill_window(k_ref, v_ref, low_ref, high_ref, k_all, v_all)
        acc[...] = jnp.zeros_like(acc)

    for u in range(per):
        b = step * per + u
        q = stack_heads(q_ref, u)
        g = stack_heads(g_ref, u)
        delta = fd_ref[u, 2 * WINDOW : 2 * WINDOW + 1]
        ds, pb = [], []
        for w in range(WINDOW):
            rows = pl.ds(pl.multiple_of((b + w) * BLOCK, BLOCK), BLOCK)
            s = mm(k_all[rows, :], q, NT)
            dp = mm(v_all[rows, :], g, NT)
            top = fd_ref[u, w : w + 1]
            top = jnp.where(top < MASKED / 2, 0.0, top)
            p = jnp.exp2(s * SCALE - top) * fd_ref[u, WINDOW + w : WINDOW + w + 1]
            ds.append((p * (dp - delta)).astype(jnp.bfloat16))
            pb.append(p.astype(jnp.bfloat16))
        ds = jnp.concatenate(ds, axis=0)
        pb = jnp.concatenate(pb, axis=0)
        ds_ref[u] = ds
        shape = (WINDOW, BLOCK, DH)
        acc[pl.ds(b, WINDOW), 0] += mm(ds, q, NN).reshape(shape)
        acc[pl.ds(b, WINDOW), 1] += mm(pb, g, NN).reshape(shape)

    @pl.when(step == pl.num_programs(0) - 1)
    def _():
        for which, f in ((0, FACTOR), (1, 1.0)):
            keep_ref[:, which] = (acc[1:-1, which, own, :] * f).astype(keep_ref.dtype)
            send_ref[:, which] = (acc[1:-1, which, opp, :] * f).astype(jnp.bfloat16)


def queries_kernel(
    first, random_blocks, k_ref, low_ref, high_ref, mine_ref, other_ref, dsw_ref, dsf_ref, *refs
):
    *_, dq_ref, k_all, kt_all = refs
    blocks = k_ref.shape[0] // BLOCK
    peers = mine_ref.shape[0]
    per = dsw_ref.shape[0]
    core, _ = places()
    step = pl.program_id(0)
    first_random = blocks + 2
    first_global = first_random + peers
    slices, size = glob_slices(peers)

    @pl.when(step == 0)
    def _():
        at_low, at_high = edge_places(blocks)
        k_all[at_low] = low_ref[0]
        k_all[at_high] = high_ref[0]
        k_all[1 : blocks + 1] = k_ref[...].reshape(blocks, BLOCK, DH)
        for ref, c in ((mine_ref, core), (other_ref, 1 - core)):
            k_all[first_random:first_global, pl.ds(c * HALF, HALF), :] = ref[:, :HALF, :]
            for i in range(slices):
                unit, offset = divmod(i * size, HALF)
                if unit % 2 == 0:
                    rows = pl.ds(pl.multiple_of(c * HALF + offset, MARKS), size)
                    k_all[first_global + unit // 2, rows, :] = ref[i, 2 * HALF :, :]

        def turn(j, carry):
            kt_all[j] = k_all[j].T
            return carry

        lax.fori_loop(0, first_global + G, turn, 0, unroll=4)

    for u in range(per):
        b = first + step * per + u
        panels = [b + w for w in range(WINDOW)]
        panels += [first_random + lax.div(random_blocks[r, b], blocks) for r in range(R)]
        panels += [first_global + j for j in range(G)]
        turned = [kt_all[i] for i in panels]
        dqt = mm(jnp.concatenate(turned[:WINDOW], axis=1), dsw_ref[u], NN)
        dqt = (dqt + mm(jnp.concatenate(turned[WINDOW:], axis=1), dsf_ref[u], NN)) * FACTOR
        for h in range(dq_ref.shape[1] // DH):
            dq_ref[u * BLOCK : (u + 1) * BLOCK, h * DH : (h + 1) * DH] = (
                dqt[:, h * BLOCK : (h + 1) * BLOCK].T.astype(jnp.bfloat16)
            )


def whole(a):
    return pl.BlockSpec(a.shape, lambda i, *_: (0,) * len(a.shape))


def per_block(per, *rest):
    return pl.BlockSpec((per,) + rest, lambda i, *_: (i,) + (0,) * len(rest))


def partners(size, stride):
    return [(i, i ^ stride) for i in range(size)]


def body(query_vectors, key_vectors, value_vectors, output_grad, random_blocks, global_blocks):
    seq_count = lax.axis_size("seq")
    head_count = lax.axis_size("head")
    rows_dev, columns = query_vectors.shape
    blocks = rows_dev // BLOCK
    per = math.gcd(blocks, 4)
    steps = blocks // per
    lanes = columns // DH * BLOCK
    bf16 = jnp.bfloat16
    f32 = jnp.float32
    sds = jax.ShapeDtypeStruct
    core_pairs = partners(head_count, 1)
    limit = (16 + seq_count // 2) * MIB
    params = pltpu.CompilerParams(dimension_semantics=("arbitrary",), vmem_limit_bytes=limit)
    unit = 2 * blocks * lanes * BLOCK * DH

    vmem = pl.BlockSpec(memory_space=pltpu.VMEM)
    smem = pl.BlockSpec(memory_space=pltpu.SMEM)
    hbm = pl.BlockSpec(memory_space=pltpu.HBM)
    small = pltpu.CompilerParams(vmem_limit_bytes=limit)
    large = pltpu.CompilerParams(vmem_limit_bytes=60 * MIB)
    share = BLOCK // head_count
    columns_count = head_count // 2

    edge = (2, BLOCK, DH)
    _, size = glob_slices(seq_count)
    asking, to_low, to_high = pl.pallas_call(
        ask_kernel,
        out_shape=(
            sds((seq_count, MARKS + size, DH), bf16),
            sds(edge, bf16),
            sds(edge, bf16),
        ),
        in_specs=[smem, vmem, hbm, hbm],
        out_specs=(vmem, vmem, vmem),
        scratch_shapes=[
            pltpu.VMEM((2 * G * HALF, DH), bf16),
            pltpu.SemaphoreType.DMA((2 * G + 4,)),
        ],
        compiler_params=large,
        name="ask",
    )(global_blocks, random_blocks.T, key_vectors, value_vectors)
    asked = lax.all_to_all(asking, "seq", split_axis=0, concat_axis=0, tiled=True)

    low_pairs = [(i, i ^ 1) for i in range(seq_count)]
    high_pairs = [(i, i + 1 if i % 2 else i - 1) for i in range(1, seq_count - 1)]
    low = lax.ppermute(to_low, "seq", low_pairs)
    high = lax.ppermute(to_high, "seq", high_pairs)
    asked, low, high = lax.optimization_barrier((asked, low, high))

    served, requested = pl.pallas_call(
        serve_kernel,
        out_shape=(sds((seq_count, 2 * HALF + size, DH), bf16), sds((seq_count,), jnp.int32)),
        in_specs=[smem, vmem, hbm, hbm],
        out_specs=(vmem, smem),
        scratch_shapes=[pltpu.SemaphoreType.DMA((seq_count, 2))],
        compiler_params=large,
        name="serve",
    )(global_blocks, asked, key_vectors, value_vectors)
    mine = lax.all_to_all(served, "seq", split_axis=0, concat_axis=0, tiled=True)

    rows_spec = pl.BlockSpec((per * BLOCK, columns), lambda i, *_: (i, 0))
    st_spec = per_block(per, 2 * FOLD, lanes)
    fd_spec = per_block(per, FOLD, lanes)
    nearby = (key_vectors, value_vectors, low, high)
    window_scratch = [pltpu.VMEM(((blocks + 2) * BLOCK, DH), bf16)] * 2
    st = pl.pallas_call(
        near_kernel,
        out_shape=sds((blocks, 2 * FOLD, lanes), f32),
        grid=(steps,),
        in_specs=[rows_spec, rows_spec] + [whole(a) for a in nearby],
        out_specs=st_spec,
        scratch_shapes=window_scratch,
        compiler_params=params,
        cost_estimate=pl.CostEstimate(
            flops=2 * WINDOW * unit, bytes_accessed=4 * MIB, transcendentals=blocks * lanes * WINDOW * BLOCK
        ),
        name="near",
    )(query_vectors, output_grad, *nearby)
    mine, st = lax.optimization_barrier((mine, st))
    queries_in, grads_in, mine = lax.optimization_barrier((query_vectors, output_grad, mine))
    here = lax.axis_index("seq") < seq_count
    queries_in = jnp.where(here, queries_in, 0).astype(bf16)
    grads_in = jnp.where(here, grads_in, 0).astype(bf16)
    other = lax.ppermute(mine, "head", core_pairs)

    slots = seq_count + G + 2
    piece = (slots, 2, share, DH)
    dsf, fd, *pieces = pl.pallas_call(
        far_kernel,
        out_shape=(
            sds((blocks * SPARE, FAR * BLOCK, lanes), bf16),
            sds((blocks * SPARE * 20, FOLD, lanes), f32),
        )
        + (sds(piece, bf16),) * head_count,
        in_specs=[smem] + [vmem] * 7,
        out_specs=(hbm, hbm) + (vmem,) * head_count,
        scratch_shapes=[pltpu.VMEM((seq_count + G, BLOCK, DH), bf16)] * 2
        + [pltpu.VMEM((slots, 2, BLOCK, DH), f32)]
        + [pltpu.VMEM((2, FAR * BLOCK, lanes), f32)] * 2
        + [
            pltpu.VMEM((blocks, FAR * BLOCK, lanes), bf16),
            pltpu.VMEM((blocks, FOLD, lanes), f32),
            pltpu.SemaphoreType.DMA((blocks,)),
            pltpu.SemaphoreType.DMA(()),
        ],
        compiler_params=pltpu.CompilerParams(vmem_limit_bytes=max(limit, 42 * MIB)),
        cost_estimate=pl.CostEstimate(
            flops=5 * FAR * unit, bytes_accessed=8 * MIB, transcendentals=blocks * lanes * FAR * BLOCK
        ),
        name="far",
    )(random_blocks.T, queries_in, grads_in, mine, other, st, low, high)

    piece_w = (blocks, 2, HALF, DH)
    near_spec = per_block(per, WINDOW * BLOCK, lanes)
    far_spec = per_block(per, FAR * BLOCK, lanes)
    dsw, keep_w, send_w = pl.pallas_call(
        close_kernel,
        out_shape=(sds((blocks, WINDOW * BLOCK, lanes), bf16), sds(piece_w, bf16), sds(piece_w, bf16)),
        grid=(steps,),
        in_specs=[rows_spec, rows_spec] + [whole(a) for a in nearby] + [fd_spec],
        out_specs=(near_spec, whole(sds(piece_w, bf16)), whole(sds(piece_w, bf16))),
        scratch_shapes=window_scratch + [pltpu.VMEM((blocks + 2, 2, BLOCK, DH), f32)],
        compiler_params=large,
        cost_estimate=pl.CostEstimate(flops=4 * WINDOW * unit, bytes_accessed=8 * MIB, transcendentals=0),
        name="close",
    )(query_vectors, output_grad, *nearby, fd)

    others = [m << 1 for m in range(1, columns_count)]

    def reduced(kept, sent, name, dtype):
        got = lax.ppermute(sent, "head", core_pairs)
        part = (kept.shape[0], 2, share, DH)
        home, *away = pl.pallas_call(
            functools.partial(split_kernel, columns_count),
            out_shape=(sds(part, dtype),) + (sds(part, bf16),) * len(others),
            in_specs=[vmem, vmem],
            out_specs=(vmem,) * (1 + len(others)),
            compiler_params=small,
            name=name,
        )(kept, got)
        return [home] + [
            lax.ppermute(a, "head", partners(head_count, m)) for a, m in zip(away, others)
        ]

    parts = pieces[:1] + [
        lax.ppermute(pieces[m], "head", partners(head_count, m)) for m in range(1, head_count)
    ]
    parts[-1], send_w = lax.optimization_barrier((parts[-1], send_w))
    terms, to_low, to_high = pl.pallas_call(
        terms_kernel,
        out_shape=(
            sds((seq_count, 2 + 2 * G, share, DH), bf16),
            sds((2, share, DH), bf16),
            sds((2, share, DH), bf16),
        ),
        in_specs=[vmem] * len(parts),
        out_specs=(vmem,) * 3,
        compiler_params=small,
        name="terms",
    )(*parts)
    parts_w = reduced(keep_w, send_w, "split_close", bf16)
    dsw, to_low = lax.optimization_barrier((dsw, to_low))

    def queries(half, dsw, done):
        shift = half * (steps // 2)
        part = lambda *rest: pl.BlockSpec((per,) + rest, lambda i, *_: (i + shift,) + (0,) * len(rest))
        return pl.pallas_call(
            functools.partial(queries_kernel, shift * per),
            out_shape=sds(query_vectors.shape, bf16),
            grid_spec=pltpu.PrefetchScalarGridSpec(
                num_scalar_prefetch=1,
                grid=(steps // 2,),
                in_specs=[whole(a) for a in (key_vectors, low, high, mine, other)]
                + [part(WINDOW * BLOCK, lanes), part(FAR * BLOCK, lanes)]
                + [hbm] * len(done),
                out_specs=pl.BlockSpec((per * BLOCK, columns), lambda i, *_: (i + shift, 0)),
                scratch_shapes=[pltpu.VMEM((blocks + 2 + seq_count + G, BLOCK, DH), bf16)] * 2,
            ),
            input_output_aliases={8: 0} if done else {},
            compiler_params=large,
            cost_estimate=pl.CostEstimate(
                flops=LISTED * unit // 2, bytes_accessed=4 * MIB, transcendentals=0
            ),
            name="queries",
        )(random_blocks.T, key_vectors, low, high, mine, other, dsw, dsf, *done)

    query_grad = queries(0, dsw, ())
    back = lax.all_to_all(terms, "seq", split_axis=0, concat_axis=0, tiled=True)
    from_low = lax.ppermute(to_low, "seq", low_pairs)
    from_high = lax.ppermute(to_high, "seq", high_pairs)
    back, query_grad = lax.optimization_barrier((back, query_grad))
    held = pl.pallas_call(
        settle_kernel,
        out_shape=sds((blocks, 2, share, DH), bf16),
        in_specs=[smem, smem] + [vmem] * (3 + len(parts_w)),
        out_specs=vmem,
        scratch_shapes=[pltpu.VMEM((blocks, 2, share, DH), f32)],
        compiler_params=small,
        name="settle",
    )(requested, global_blocks, back, from_low, from_high, *parts_w)

    dsw, query_grad, held = lax.optimization_barrier((dsw, query_grad, held))
    query_grad = queries(1, dsw, (query_grad,))
    rows = [held] + [lax.ppermute(held, "head", partners(head_count, m)) for m in others]
    rows[-1], query_grad = lax.optimization_barrier((rows[-1], query_grad))
    pieces = []
    for a in rows:
        pieces += [a, lax.ppermute(a, "head", core_pairs)]
    key_grad, value_grad = pl.pallas_call(
        functools.partial(join_kernel, columns_count),
        out_shape=(sds(key_vectors.shape, bf16),) * 2,
        in_specs=[vmem] * len(pieces),
        out_specs=(vmem, vmem),
        scratch_shapes=[pltpu.VMEM((blocks, BLOCK, DH), bf16)] * 2,
        compiler_params=small,
        name="join",
    )(*pieces)
    return query_grad, key_grad, value_grad


def solution(mesh):
    return jax.shard_map(
        body,
        mesh=mesh,
        in_specs=(
            P("seq", "head"),
            P("seq", None),
            P("seq", None),
            P("seq", "head"),
            P("seq", None),
            P(),
        ),
        out_specs=(P("seq", "head"), P("seq", None), P("seq", None)),
        check_vma=False,
    )
```
